256 devices in a mesh: gx: 16 (over x_hi, y, core), gy: 8 (over z), comp: 2 (over x_lo).
Axes of the slice: x: 4 (x_hi: 2, x_lo: 2; x = x_hi * 2 + x_lo), y: 4, z: 8, core: 2. Of those that a mesh axis runs over, the one named last changes fastest.
Arguments:
- tracer: float32 [16, 640, 4096], P(None, 'gy', ('gx', 'comp')), may hold values from -6 to 6
- ocean_u: float32 [16, 640, 4096], P(None, 'gy', ('gx', 'comp')), may hold values from -6 to 6
- ocean_v: float32 [16, 640, 4096], P(None, 'gy', ('gx', 'comp')), may hold values from -6 to 6
- ocean_mask: int32 [640, 4096], P('gy', ('gx', 'comp')), may hold values 0 or 1
- diffusivity: float32 [16], replicated, may hold values from 0.02 to 0.2
- viscosity: float32 [16], replicated, may hold values from 0.02 to 0.2
- remap: float32 [16, 16], replicated, may hold values from -1.5 to 1.5
- fold_partner: int32 [4096], P(('gx', 'comp')), may hold values from 0 to 4095, as said below
- ice_u: float32 [640, 4096], P(('gy', 'comp'), 'gx'), may hold values from -3 to 3
- ice_v: float32 [640, 4096], P(('gy', 'comp'), 'gx'), may hold values from -3 to 3
- ice_mass: float32 [640, 4096], P(('gy', 'comp'), 'gx'), may hold values from 0.5 to 4
- ice_strength: float32 [640, 4096], P(('gy', 'comp'), 'gx'), may hold values from 0.2 to 2
- ice_mask: int32 [640, 4096], P(('gy', 'comp'), 'gx'), may hold values 0 or 1
Outputs:
- new_tracer: float32 [16, 640, 4096], P(None, 'gy', ('gx', 'comp'))
- new_ocean_u: float32 [16, 640, 4096], P(None, 'gy', ('gx', 'comp'))
- new_ocean_v: float32 [16, 640, 4096], P(None, 'gy', ('gx', 'comp'))
- new_ice_u: float32 [640, 4096], P(('gy', 'comp'), 'gx')
- new_ice_v: float32 [640, 4096], P(('gy', 'comp'), 'gx')
The draws below stay inside these ranges and needn't reach their ends.
Inputs may be any that keep to these rules, and one draw needn't show every extreme that they name: `fold_partner`: columns of zonal block k (blocks of 128 columns in order) pair with columns of block 31 - k; the partner of a column's partner is the column itself.
All inputs are finite; a program needn't handle non-finite values. No bound on the sum of `ocean_mask` or of `ice_mask` on one device may be relied on, other than what follows from the above.
Results may differ from the reference program's by a relative error of at most 0.000088.
Values sent between devices are 32-bit elements; how exact they have to be, the bound alone decides.
A program may use at most 64 MiB of HBM per device.

```python
import math
import jax
import jax.numpy as jnp
from jax import lax

LEV = 16
CX = 128
ITERS = 4
NX = 4096
NY = 640


def draw_fold_partner(key, part):
    key = jax.random.fold_in(key, 7)
    blocks = NX // CX
    half_count = blocks // 2
    block_keys = jax.random.split(key, half_count)
    shuffles = jax.vmap(lambda one_key: jax.random.permutation(one_key, CX))(block_keys)
    inverses = jnp.argsort(shuffles, axis=1, stable=True)
    lower = (blocks - 1 - jnp.arange(half_count))[:, None] * CX + shuffles
    upper = (jnp.arange(half_count)[:, None] * CX + inverses)[::-1]
    return jnp.concatenate([lower, upper], axis=0).reshape(-1).astype(jnp.int32)


def with_ends(values, rng, smallest, largest):
    index_at = [jax.random.randint(jax.random.fold_in(rng, axis), (), 0, length) for axis, length in enumerate(values.shape)]
    longest = values.shape.index(max(values.shape))
    next_to = index_at[:longest] + [(index_at[longest] + 1) % values.shape[longest]] + index_at[longest + 1:]
    return values.at[tuple(index_at)].set(smallest).at[tuple(next_to)].set(largest)


def block_scale(stream_key, dims, cuts, smallest, top_value):
    def one(dim, parts):
        steps = jax.random.uniform(jax.random.fold_in(jax.random.fold_in(stream_key, 6), dim), (parts,), jnp.float32, smallest / len(cuts), top_value / len(cuts))
        return jnp.repeat(jnp.exp(steps), dims[dim] // parts).reshape((-1,) + (1,) * (len(dims) - dim - 1))

    factor_of = one(*cuts[0])
    for cut in cuts[1:]:
        factor_of = factor_of * one(*cut)
    return factor_of


def gaussian(rng, dims, deviation, limit, pieces=(), dtype=jnp.bfloat16):
    loudness = block_scale(rng, dims, pieces, -0.22, 0.18) if pieces else 1.0
    drawn = jax.random.normal(rng, dims, jnp.float32) * deviation * loudness
    return jnp.minimum(jnp.maximum(drawn, -limit), limit).astype(dtype)


def setup_inputs(seed: int = 0) -> dict:
    keys = jax.random.split(jax.random.key(seed), 14)
    tracer = gaussian(keys[0], (LEV, NY, NX), 1.0, 6.0, ((1, 8), (2, 32)), jnp.float32)
    ocean_u = gaussian(keys[1], (LEV, NY, NX), 1.0, 6.0, ((1, 8), (2, 32)), jnp.float32)
    ocean_v = gaussian(keys[2], (LEV, NY, NX), 1.0, 6.0, ((1, 8), (2, 32)), jnp.float32)
    ocean_mask = with_ends((jax.random.randint(keys[3], (NY, NX), 0, 5) < 4).astype(jnp.int32), jax.random.fold_in(keys[3], 1), 0, 1)
    diffusivity = jnp.clip(jnp.exp(jax.random.uniform(keys[4], (LEV,), jnp.float32, math.log(0.02), math.log(0.2))), 0.02, 0.2)
    viscosity = jnp.clip(jnp.exp(jax.random.uniform(keys[5], (LEV,), jnp.float32, math.log(0.02), math.log(0.2))), 0.02, 0.2)
    remap = gaussian(keys[6], (LEV, LEV), LEV ** -0.5, 1.5, (), jnp.float32)
    fold_partner = draw_fold_partner(jax.random.fold_in(keys[13], 71), 0)
    ice_u = gaussian(keys[8], (NY, NX), 0.5, 3.0, ((0, 16), (1, 16)), jnp.float32)
    ice_v = gaussian(keys[9], (NY, NX), 0.5, 3.0, ((0, 16), (1, 16)), jnp.float32)
    ice_mass = jnp.clip(jnp.exp(math.log(4.0) - 2.0794415 * jax.random.uniform(keys[10], (NY, NX), jnp.float32) ** block_scale(keys[10], (NY, NX), ((0, 16), (1, 16)), -0.2, 0.2)), 0.5, 4.0)
    ice_strength = jnp.clip(jnp.exp(math.log(2.0) - 2.3025851 * jax.random.uniform(keys[11], (NY, NX), jnp.float32) ** block_scale(keys[11], (NY, NX), ((0, 16), (1, 16)), -0.2, 0.2)), 0.2, 2.0)
    ice_mask = with_ends((jax.random.randint(keys[12], (NY, NX), 0, 2) < 1).astype(jnp.int32), jax.random.fold_in(keys[12], 1), 0, 1)
    return dict(tracer=tracer, ocean_u=ocean_u, ocean_v=ocean_v, ocean_mask=ocean_mask, diffusivity=diffusivity, viscosity=viscosity, remap=remap, fold_partner=fold_partner, ice_u=ice_u, ice_v=ice_v, ice_mass=ice_mass, ice_strength=ice_strength, ice_mask=ice_mask)


RELAX = 0.5
STEP_SIZE = 0.3
COUPLE = 0.5

def neighbours(field, top_row):
    to_east = jnp.roll(field, -1, axis=-1)
    to_west = jnp.roll(field, 1, axis=-1)
    to_north = jnp.concatenate([field[..., 1:, :], top_row[..., None, :]], axis=-2)
    to_south = jnp.concatenate([jnp.zeros_like(field[..., :1, :]), field[..., :-1, :]], axis=-2)
    return (to_east, to_west, to_north, to_south)

def fold_row(field, fold_partner, fold_sign):
    return fold_sign * jnp.take(field[..., -1, :], fold_partner, axis=-1)

def diffuse(field, sea_mask, mask_sides, coefficient, fold_sign, fold_partner):
    to_east, to_west, to_north, to_south = neighbours(field, fold_row(field, fold_partner, fold_sign))
    mask_east, mask_west, mask_north, mask_south = mask_sides
    laplacian = mask_east * (to_east - field) + mask_west * (to_west - field)
    laplacian = laplacian + mask_north * (to_north - field) + mask_south * (to_south - field)
    return field + coefficient[:, None, None] * sea_mask * laplacian

def regrid(remap, field):
    return jnp.einsum('kl,lyx->kyx', remap, field, precision=lax.Precision.HIGHEST)

def reference(tracer, ocean_u, ocean_v, ocean_mask, diffusivity, viscosity, remap, fold_partner, ice_u, ice_v, ice_mass, ice_strength, ice_mask):
    sea_mask = ocean_mask.astype(jnp.float32)
    mask_sides = neighbours(sea_mask, fold_row(sea_mask, fold_partner, 1.0))
    new_tracer = regrid(remap, diffuse(tracer, sea_mask, mask_sides, diffusivity, 1.0, fold_partner))
    zonal_flow = regrid(remap, diffuse(ocean_u, sea_mask, mask_sides, viscosity, -1.0, fold_partner))
    merid_flow = regrid(remap, diffuse(ocean_v, sea_mask, mask_sides, viscosity, -1.0, fold_partner))
    surface_u = zonal_flow[0]
    surface_v = merid_flow[0]
    present = ice_mask.astype(jnp.float32)
    vel_u = ice_u
    vel_v = ice_v
    stress_a = jnp.zeros_like(ice_u)
    stress_b = jnp.zeros_like(ice_u)
    for cycle in range(ITERS):
        u_east, u_west, u_north, u_south = neighbours(vel_u, fold_row(vel_u, fold_partner, -1.0))
        v_east, v_west, v_north, v_south = neighbours(vel_v, fold_row(vel_v, fold_partner, -1.0))
        divergence = 0.5 * (u_east - u_west) + 0.5 * (v_north - v_south)
        shearing = 0.5 * (u_north - u_south) + 0.5 * (v_east - v_west)
        deformation = jnp.sqrt(divergence * divergence + (shearing * 0.5) ** 2 + 0.01)
        viscous = ice_strength / deformation
        stress_a = (stress_a + RELAX * (viscous * divergence - ice_strength)) / (1.0 + RELAX)
        stress_b = (stress_b + RELAX * viscous * shearing) / (1.0 + RELAX)
        a_east, a_west, a_north, a_south = neighbours(stress_a, fold_row(stress_a, fold_partner, 1.0))
        b_east, b_west, b_north, b_south = neighbours(stress_b, fold_row(stress_b, fold_partner, 1.0))
        force_u = 0.5 * (a_east - a_west) + 0.5 * (b_north - b_south)
        force_v = 0.5 * (b_east - b_west) + 0.5 * (a_north - a_south)
        vel_u = present * (vel_u + STEP_SIZE * (force_u / ice_mass + surface_u)) / (1.0 + STEP_SIZE)
        vel_v = present * (vel_v + STEP_SIZE * (force_v / ice_mass + surface_v)) / (1.0 + STEP_SIZE)
    tau_u = present * (vel_u - surface_u)
    tau_v = present * (vel_v - surface_v)
    zonal_flow = zonal_flow.at[0].add(COUPLE * sea_mask * tau_u)
    merid_flow = merid_flow.at[0].add(COUPLE * sea_mask * tau_v)
    return (new_tracer, zonal_flow, merid_flow, vel_u, vel_v)
```

```python
import jax
import jax.numpy as jnp
from jax import lax
from jax.experimental import pallas as pl
from jax.experimental.pallas import tpu as pltpu
from jax.sharding import PartitionSpec as P

ITERS = 4
RELAX = 0.5
STEP_SIZE = 0.3
COUPLE = 0.5
MESH = pl.DeviceIdType.MESH

LEV = 16
ROWS = 80
HALF = 40
COLS = 128
NF = 10
NS = NF + 1
REACH = 2
SIDE = 2 * REACH + 1
BLOCKS = 2 * SIDE
TOP = 16
SPAN = 96
OWN_REACH = {2: 0, 3: 1}
MIRROR_REACH = {1: 0, 2: 1, 3: 2}
OWN_ROWS = (8, 2, 1)
MIRROR_ROWS = (4, 3, 2)
PLANES = 3 * LEV + 1


def kernel(
    blocks,
    gys,
    tracer,
    ocean_u,
    ocean_v,
    ocean_mask,
    diffusivity_in,
    viscosity_in,
    remap_in,
    fold_in,
    ice_u,
    ice_v,
    ice_mass,
    ice_strength,
    ice_mask,
    new_tracer,
    new_ocean_u,
    new_ocean_v,
    new_ice_u,
    new_ice_v,
    F,
    DH,
    DL,
    KK,
    O,
    X,
    AB,
    S,
    SAB,
    SS,
    S2,
    SS2,
    PE,
    PW,
    EB,
    WB,
    CP,
    RE,
    RW,
    GE,
    MK,
    OM,
    IM,
    IDX,
    diffusivity,
    viscosity,
    remap,
    remap_wide,
    fold_partner,
    in_sem,
    ice_sem,
    ice_send,
    ice_recv,
    edge_send,
    edge_recv,
    rim_send,
    rim_recv,
    strip_send,
    strip_recv,
    again_send,
    again_recv,
    out_sem,
    vel_send,
    vel_recv,
):
    gx, gy, comp = lax.axis_index("gx"), lax.axis_index("gy"), lax.axis_index("comp")
    me = gx * 2 + comp
    has_north = gy < gys - 1
    has_south = gy > 0
    is_top = gy == gys - 1

    def at(block, row):
        return {"gx": block // 2, "gy": row, "comp": lax.rem(block, 2)}

    def wrap(block):
        return lax.rem(block + 2 * blocks, blocks)

    east, west, mirror = wrap(me + 1), wrap(me - 1), blocks - 1 - me
    partner = at(gx * 2 + 1 - comp, gy)

    strips = [(SIDE + REACH, mirror, False, MIRROR_ROWS[0])]
    for d in (1, -1, 2, -2):
        strips.append((SIDE + REACH + d, wrap(mirror + d), d % 2 == 1, MIRROR_ROWS[abs(d)]))
        strips.append((REACH + d, wrap(me - d), False, OWN_ROWS[abs(d)]))

    barrier = pltpu.get_barrier_semaphore()

    def greet(target):
        pl.semaphore_signal(barrier, inc=1, device_id=target, device_id_type=MESH)

    greet(at(east, gy))
    greet(at(west, gy))

    @pl.when(has_north)
    def _():
        for block in (me, east, west):
            greet(at(block, gy + 1))

    @pl.when(has_south)
    def _():
        for block in (me, east, west):
            greet(at(block, gy - 1))

    @pl.when(is_top)
    def _():
        for _, block, own, _ in strips:
            if own:

                @pl.when(block != me)
                def _(block=block):
                    greet(at(block, gy))
            else:
                greet(at(block, gy))

    def load(src, dst, sem):
        copy = pltpu.make_async_copy(src, dst, sem)
        copy.start()
        return copy

    load_u = load(ocean_u, F.at[LEV : 2 * LEV, 8 : 8 + ROWS, :], in_sem.at[0])
    load_v = load(ocean_v, F.at[2 * LEV : 3 * LEV, 8 : 8 + ROWS, :], in_sem.at[1])
    load_t = load(tracer, F.at[0:LEV, 8 : 8 + ROWS, :], in_sem.at[3])
    small = [
        load(ocean_mask, OM, in_sem.at[2]),
        load(remap_in, remap, in_sem.at[4]),
        load(diffusivity_in, diffusivity, in_sem.at[5]),
        load(viscosity_in, viscosity, in_sem.at[6]),
        load(fold_in, fold_partner, in_sem.at[7]),
        load(remap_in, remap_wide, in_sem.at[8]),
    ]
    ice_in = (ice_u, ice_v, ice_mass, ice_strength, ice_mask)

    def ice_place(i, half):
        rows = pl.ds(pl.multiple_of(TOP + HALF * half, 8), HALF)
        if i == 4:
            return IM.at[pl.ds(pl.multiple_of(HALF * half, 8), HALF), :]
        return X.at[i, rows, 0:COLS]

    mine = pl.ds(pl.multiple_of(COLS * comp, COLS), COLS)
    other = pl.ds(pl.multiple_of(COLS * (1 - comp), COLS), COLS)
    ice_local = [load(ice_in[i].at[:, mine], ice_place(i, comp), ice_sem.at[i]) for i in range(5)]

    first8, last8 = slice(TOP, TOP + 8), slice(TOP + ROWS - 8, TOP + ROWS)
    south8, north8 = slice(TOP - 8, TOP), slice(TOP + ROWS, TOP + ROWS + 8)

    @pl.when(jnp.logical_not(has_south))
    def _():
        X[:, south8, 0:COLS] = jnp.zeros((NF, 8, COLS), jnp.float32)
        EB[0:8, :] = jnp.zeros((8, COLS), jnp.float32)
        WB[0:8, :] = jnp.zeros((8, COLS), jnp.float32)
        F[:, 0:8, :] = jnp.zeros((PLANES, 8, COLS), jnp.float32)

    @pl.when(is_top)
    def _():
        X[:, north8, 0:COLS] = jnp.zeros((NF, 8, COLS), jnp.float32)
        EB[88:96, :] = jnp.zeros((8, COLS), jnp.float32)
        WB[88:96, :] = jnp.zeros((8, COLS), jnp.float32)

    outer = jnp.zeros((NF, 8, 2 * COLS), jnp.float32)
    X[:, 0:8, :] = outer
    X[:, 104:112, :] = outer
    AB[:, 0:8, :] = outer[0:2]
    AB[:, 104:112, :] = outer[0:2]

    count = 2 + 3 * has_north.astype(jnp.int32) + 3 * has_south.astype(jnp.int32)
    strip_count = 0
    for _, block, own, _ in strips:
        strip_count = strip_count + ((block != me).astype(jnp.int32) if own else 1)
    count = count + is_top.astype(jnp.int32) * strip_count
    pl.semaphore_wait(barrier, count)

    def send(src, dst, send_sem, recv_sem, target):
        copy = pltpu.make_async_remote_copy(
            src_ref=src,
            dst_ref=dst,
            send_sem=send_sem,
            recv_sem=recv_sem,
            device_id=target,
            device_id_type=MESH,
        )
        return copy

    ice_away = []
    for i in range(5):
        copy = send(
            ice_in[i].at[:, other], ice_place(i, comp), ice_send.at[i], ice_recv.at[i], partner
        )
        copy.start()
        ice_away.append(copy)

    lane = lax.broadcasted_iota(jnp.int32, (1, COLS), 1)
    row8 = lax.broadcasted_iota(jnp.int32, (8, 1), 0)
    tile_rows = slice(TOP, TOP + ROWS)

    for copy in small:
        copy.wait()
    sea = OM[...].astype(jnp.float32)
    X[9, tile_rows, 0:COLS] = sea
    F[3 * LEV, 8 : 8 + ROWS, :] = sea
    for i, copy in ((0, load_u), (1, load_v)):
        copy.wait()
        base = jnp.zeros((ROWS, COLS), jnp.float32)
        spread = jnp.zeros((ROWS, COLS), jnp.float32)
        for l in range(LEV):
            weighted = remap[0, l] * F[LEV * (i + 1) + l, 8 : 8 + ROWS, :]
            base = base + weighted
            spread = spread + viscosity[l] * weighted
        X[5 + i, tile_rows, 0:COLS] = base
        X[7 + i, tile_rows, 0:COLS] = spread

    load_t.wait()
    row_n = send(F.at[:, 87:88, :], F.at[:, 7:8, :], edge_send.at[2], edge_recv.at[2], at(me, gy + 1))
    row_s = send(F.at[:, 8:9, :], F.at[:, 88:89, :], edge_send.at[3], edge_recv.at[3], at(me, gy - 1))
    row_f = send(F.at[:, 87:88, :], F.at[:, 88:89, :], edge_send.at[4], edge_recv.at[4], at(mirror, gy))

    @pl.when(has_north)
    def _():
        row_n.start()

    @pl.when(has_south)
    def _():
        row_s.start()

    @pl.when(is_top)
    def _():
        row_f.start()

    def pack(f, packed):
        return jnp.where((lane >> 1) == f, pltpu.roll(F[f, 8 : 8 + ROWS, :], 2 * f + 1, 1), packed)

    CP[...] = lax.fori_loop(0, PLANES, pack, jnp.zeros((ROWS, COLS), jnp.float32), unroll=7)
    col_to_e = send(CP, RW, edge_send.at[0], edge_recv.at[0], at(east, gy))
    col_to_w = send(CP, RE, edge_send.at[1], edge_recv.at[1], at(west, gy))
    col_to_e.start()
    col_to_w.start()

    lane2 = lax.broadcasted_iota(jnp.int32, (LEV, LEV * LEV), 1)
    weights = jnp.zeros((LEV, LEV * LEV), jnp.float32)
    for l in range(LEV):
        weights = jnp.where((lane2 >> 4) == l, remap_wide[:, l : l + 1], weights)
    high = weights.astype(jnp.bfloat16).astype(jnp.float32)
    low = weights - high
    diagonal = (lane2 & 15) == lax.broadcasted_iota(jnp.int32, (LEV, LEV * LEV), 0)
    for k in range(LEV):
        rows = slice(LEV * k, LEV * (k + 1))
        high_k = jnp.where(diagonal, high[k : k + 1], 0.0).astype(jnp.bfloat16)
        KK[rows, 0:256] = high_k
        KK[rows, 256:512] = jnp.where(diagonal, low[k : k + 1], 0.0).astype(jnp.bfloat16)
        KK[rows, 512:768] = high_k

    for i in range(5):
        ice_local[i].wait()
        ice_away[i].wait_recv()
    X[4, tile_rows, 0:COLS] = IM[...].astype(jnp.float32)

    pack_e = jnp.zeros((ROWS, COLS), jnp.float32)
    pack_w = jnp.zeros((ROWS, COLS), jnp.float32)
    for f in range(NF):
        value = X[f, tile_rows, 0:COLS]
        keep = (lane >= 8 * f) & (lane < 8 * f + 8)
        pack_e = jnp.where(keep, pltpu.roll(value, 8 * f + 8, 1), pack_e)
        pack_w = jnp.where(keep, pltpu.roll(value, 8 * f, 1) if f else value, pack_w)
    PE[...] = pack_e
    PW[...] = pack_w
    to_e = send(PE, WB.at[8 : 8 + ROWS], rim_send.at[0], rim_recv.at[0], at(east, gy))
    to_w = send(PW, EB.at[8 : 8 + ROWS], rim_send.at[1], rim_recv.at[1], at(west, gy))
    to_n = [
        send(X.at[:, last8, 0:COLS], X.at[:, south8, 0:COLS], rim_send.at[2], rim_recv.at[2], at(me, gy + 1)),
        send(PE.at[ROWS - 8 : ROWS], WB.at[0:8], rim_send.at[3], rim_recv.at[3], at(east, gy + 1)),
        send(PW.at[ROWS - 8 : ROWS], EB.at[0:8], rim_send.at[4], rim_recv.at[4], at(west, gy + 1)),
    ]
    to_s = [
        send(X.at[:, first8, 0:COLS], X.at[:, north8, 0:COLS], rim_send.at[5], rim_recv.at[5], at(me, gy - 1)),
        send(PE.at[0:8], WB.at[88:96], rim_send.at[6], rim_recv.at[6], at(east, gy - 1)),
        send(PW.at[0:8], EB.at[88:96], rim_send.at[7], rim_recv.at[7], at(west, gy - 1)),
    ]

    def strip_ends(src, dst, slot, rows):
        kept = slice(8 - rows, 8)
        return src.at[:, kept, :], dst.at[:, kept, COLS * slot : COLS * (slot + 1)]

    def strip_copy(again, slot, block, rows):
        src, dst = strip_ends(SS2, S2, slot, rows) if again else strip_ends(SS, S, slot, rows)
        sent, received = (again_send, again_recv) if again else (strip_send, strip_recv)
        return send(src, dst, sent.at[slot], received.at[slot], at(block, gy))

    def strips_start(again):
        for slot, block, own, rows in strips:
            if own:

                @pl.when(block != me)
                def _(slot=slot, block=block, rows=rows):
                    strip_copy(again, slot, block, rows).start()

                @pl.when(block == me)
                def _(slot=slot, rows=rows):
                    src, dst = strip_ends(SS2, S2, slot, rows) if again else strip_ends(SS, S, slot, rows)
                    pltpu.make_async_copy(src, dst, (again_recv if again else strip_recv).at[slot]).start()
            else:
                strip_copy(again, slot, block, rows).start()

    def strips_arrive(again):
        for slot, block, own, rows in strips:
            strip_copy(again, slot, block, rows).wait_recv()

    def strips_sent(again):
        for slot, block, own, rows in strips:
            if own:

                @pl.when(block != me)
                def _(slot=slot, block=block, rows=rows):
                    strip_copy(again, slot, block, rows).wait_send()
            else:
                strip_copy(again, slot, block, rows).wait_send()

    middle = slice(COLS * REACH, COLS * (REACH + 1))

    @pl.when(is_top)
    def _():
        SS[0:NF] = X[0:NF, last8, 0:COLS]
        inside = fold_partner[...] - COLS * mirror
        SS[NF] = jnp.broadcast_to(inside.astype(jnp.float32), (8, COLS))
        strips_start(False)

    to_e.start()
    to_w.start()

    @pl.when(has_north)
    def _():
        for copy in to_n:
            copy.start()

    @pl.when(has_south)
    def _():
        for copy in to_s:
            copy.start()

    col_to_e.wait()
    col_to_w.wait()

    @pl.when(has_north)
    def _():
        row_n.wait_send()
        row_s.wait_recv()

    @pl.when(has_south)
    def _():
        row_s.wait_send()
        row_n.wait_recv()


    @pl.when(is_top)
    def _():
        row_f.wait()
        inside = jnp.broadcast_to(fold_partner[...] - COLS * mirror, (8, COLS))

        def fold_edge(f, carry):
            taken = jnp.take_along_axis(F[f, 88:96, :], inside, axis=1, mode="promise_in_bounds")
            F[f, 88:96, :] = jnp.where((f < LEV) | (f == 3 * LEV), taken, -taken)
            return carry

        lax.fori_loop(0, PLANES, fold_edge, 0, unroll=7)

    GE[...] = jnp.where((lane & 1) == 0, pltpu.roll(RE[...], COLS - 1, 1), pltpu.roll(RW[...], 1, 1))

    def plane_sides(f):
        value = F[f, 8 : 8 + ROWS, :]
        edges = pltpu.roll(GE[...], COLS - 1 - 2 * f, 1)
        to_east = jnp.where(lane == COLS - 1, edges, pltpu.roll(value, COLS - 1, 1))
        to_west = jnp.where(lane == 0, edges, pltpu.roll(value, 1, 1))
        return value, to_east, to_west, F[f, 9 : 9 + ROWS, :], F[f, 7 : 7 + ROWS, :]

    seas = plane_sides(3 * LEV)
    degree = jnp.zeros((ROWS, COLS), jnp.float32)
    for i in range(4):
        weight = seas[0] * seas[i + 1]
        MK[i] = weight
        degree = degree + weight
    MK[4] = degree

    def diffuse(g):
        coefficient = diffusivity if g == 0 else viscosity

        def one(l, carry):
            f = g * LEV + l
            value, to_east, to_west, to_north, to_south = plane_sides(f)
            total = MK[0] * to_east + MK[1] * to_west + MK[2] * to_north + MK[3] * to_south
            new = value + coefficient[l] * (total - MK[4] * value)
            high = new.astype(jnp.bfloat16)
            DH[f] = high
            DL[f] = (new - high.astype(jnp.float32)).astype(jnp.bfloat16)
            return carry

        lax.fori_loop(0, LEV, one, 0, unroll=4)

    def regrid(g):
        planes = slice(g * LEV, (g + 1) * LEV)
        pieces = range(0, ROWS, LEV)
        high = jnp.concatenate([DH[planes, r : r + LEV, :].reshape(LEV * LEV, COLS) for r in pieces], axis=1)
        low = jnp.concatenate([DL[planes, r : r + LEV, :].reshape(LEV * LEV, COLS) for r in pieces], axis=1)
        new = jnp.dot(KK[...], jnp.concatenate([high, high, low], axis=0), preferred_element_type=jnp.float32)
        for i, r in enumerate(pieces):
            O[planes, r : r + LEV, :] = new[:, COLS * i : COLS * (i + 1)].reshape(LEV, LEV, COLS)

    outs = (new_tracer, new_ocean_u, new_ocean_v)

    def store(g):
        copy = pltpu.make_async_copy(O.at[g * LEV : (g + 1) * LEV], outs[g], out_sem.at[g])
        copy.start()
        return copy

    diffuse(0)
    diffuse(1)
    diffuse(2)

    to_e.wait()
    to_w.wait()

    @pl.when(has_north)
    def _():
        for copy in to_n:
            copy.wait_send()
        for copy in to_s:
            copy.wait_recv()

    @pl.when(has_south)
    def _():
        for copy in to_s:
            copy.wait_send()
        for copy in to_n:
            copy.wait_recv()

    for f in range(NF):
        from_e = pltpu.roll(EB[...], COLS - 8 * f, 1) if f else EB[...]
        from_w = pltpu.roll(WB[...], COLS - 8 - 8 * f, 1)
        X[f, 8 : 8 + SPAN, COLS : 2 * COLS] = jnp.where(
            lane < 8, from_e, jnp.where(lane >= COLS - 8, from_w, 0.0)
        )

    def inside_of(i):
        return IDX[:, COLS * i : COLS * (i + 1)]

    def fold_block(ref, f, i, sign):
        j = BLOCKS - 1 - i
        value = ref[f, :, COLS * j : COLS * (j + 1)]
        taken = jnp.take_along_axis(value, inside_of(i), axis=1, mode="promise_in_bounds")
        return taken if sign > 0 else -taken

    def close_top(ref, f, strip_ref, sf, sign):
        own = fold_block(strip_ref, sf, REACH, sign)
        to_the_e = fold_block(strip_ref, sf, REACH + 1, sign)
        to_the_w = fold_block(strip_ref, sf, REACH - 1, sign)
        ref[f, 96:97, 0:COLS] = own[7:8]
        ref[f, 96:97, COLS : 2 * COLS] = jnp.where(lane < COLS // 2, to_the_e, to_the_w)[7:8]

    @pl.when(is_top)
    def _():
        S[:, :, middle] = SS[...]
        strips_arrive(False)
        IDX[...] = jnp.broadcast_to(S[NF, 7:8, :], IDX.shape).astype(jnp.int32)
        for f, sign in ((7, -1), (8, -1), (9, 1)):
            close_top(X, f, S, f, sign)

    def window(first, reach):
        middle = first + REACH
        low, high = middle - reach, middle + reach + 1
        wide_low, wide_high = max(low - 1, first), min(high + 1, first + SIDE)
        return low, high, wide_low, wide_high

    def strip_sides(ref, f, win, sign):
        low, high, wide_low, wide_high = win
        wide = ref[f, :, COLS * wide_low : COLS * wide_high]
        length = COLS * (wide_high - wide_low)
        cut = slice(COLS * (low - wide_low), COLS * (high - wide_low))
        value = wide[:, cut]
        to_east = pltpu.roll(wide, length - 1, 1)[:, cut]
        to_west = pltpu.roll(wide, 1, 1)[:, cut]
        folded = jnp.concatenate([fold_block(ref, f, i, sign) for i in range(low, high)], axis=1)
        to_north = jnp.where(row8 == 7, folded, pltpu.roll(value, 7, 0))
        to_south = pltpu.roll(value, 1, 0)
        return value, to_east, to_west, to_north, to_south

    def windows(left):
        found = []
        if left in OWN_REACH:
            found.append(window(0, OWN_REACH[left]))
        if left in MIRROR_REACH:
            found.append(window(SIDE, MIRROR_REACH[left]))
        return found

    def lap_of(seas, values):
        total = seas[1] * (values[1] - values[0])
        for i in range(2, 5):
            total = total + seas[i] * (values[i] - values[0])
        return total * seas[0]

    SHARE = STEP_SIZE / (1.0 + STEP_SIZE)
    KEEP = 1.0 / (1.0 + STEP_SIZE)

    def ready(ref, rows, cols, surfaces):
        present = ref[4, rows, cols]
        ref[5, rows, cols] = SHARE * present * surfaces[0]
        ref[6, rows, cols] = SHARE * present * surfaces[1]
        mass = ref[2, rows, cols]
        ref[2, rows, cols] = 0.5 * SHARE * present / jnp.where(mass > 0.0, mass, 1.0)
        ref[4, rows, cols] = KEEP * present

    def strips_ready():
        for win in windows(2):
            cols = slice(COLS * win[0], COLS * win[1])
            seas = strip_sides(S, 9, win, 1)
            surfaces = [
                S[5 + i, :, cols] + lap_of(seas, strip_sides(S, 7 + i, win, -1)) for i in range(2)
            ]
            ready(S, slice(0, 8), cols, surfaces)
        S[3] = S[3] * (RELAX / (1.0 + RELAX))

    def main_sides(ref, f, start, size):
        value = ref[f, start : start + size, :]
        return (
            value,
            pltpu.roll(value, 2 * COLS - 1, 1),
            pltpu.roll(value, 1, 1),
            ref[f, start + 1 : start + size + 1, :],
            ref[f, start - 1 : start + size - 1, :],
        )

    CHUNK = 24
    chunks = range(8, 8 + SPAN, CHUNK)

    def tile_ready():
        for start in chunks:
            rows = slice(start, start + CHUNK)
            seas = main_sides(X, 9, start, CHUNK)
            surfaces = [X[5 + i, rows, :] + lap_of(seas, main_sides(X, 7 + i, start, CHUNK)) for i in range(2)]
            ready(X, rows, slice(0, 2 * COLS), surfaces)
            X[3, rows, :] = X[3, rows, :] * (RELAX / (1.0 + RELAX))

    def stress(u, v, third, old):
        twice_d = (u[1] - u[2]) + (v[3] - v[4])
        twice_h = (u[3] - u[4]) + (v[1] - v[2])
        viscous = third * lax.rsqrt(twice_d * twice_d + 0.25 * (twice_h * twice_h) + 0.04)
        a = viscous * twice_d - third
        b = viscous * twice_h
        if old is not None:
            a = a + old[0] * (1.0 / (1.0 + RELAX))
            b = b + old[1] * (1.0 / (1.0 + RELAX))
        return a, b

    def push(ref, vel, rows, cols, a, b):
        keep, mobility = ref[4, rows, cols], ref[2, rows, cols]
        new_u = keep * vel[0, rows, cols] + mobility * ((a[1] - a[2]) + (b[3] - b[4])) + ref[5, rows, cols]
        new_v = keep * vel[1, rows, cols] + mobility * ((b[1] - b[2]) + (a[3] - a[4])) + ref[6, rows, cols]
        vel[0, rows, cols] = new_u
        vel[1, rows, cols] = new_v

    every = slice(0, 8)

    def tile_stress(first):
        for start in chunks:
            rows = slice(start, start + CHUNK)
            u, v = main_sides(X, 0, start, CHUNK), main_sides(X, 1, start, CHUNK)
            old = None if first else (AB[0, rows, :], AB[1, rows, :])
            AB[0, rows, :], AB[1, rows, :] = stress(u, v, X[3, rows, :], old)

    def tile_push():
        for start in chunks:
            rows = slice(start, start + CHUNK)
            push(X, X, rows, slice(0, 2 * COLS), main_sides(AB, 0, start, CHUNK), main_sides(AB, 1, start, CHUNK))

    def tile_cycle(cycle, carry):
        tile_stress(False)
        tile_push()
        return carry

    def top_cycles(cycles):
        vel, sig, i_a, i_b = (S, SAB, 0, 1) if cycles[0] == 0 else (S2, S2, 2, 3)
        for cycle in cycles:
            left = 3 if cycle == cycles[0] else 1
            close_top(X, 0, vel, 0, -1)
            close_top(X, 1, vel, 1, -1)
            for win in windows(left):
                cols = slice(COLS * win[0], COLS * win[1])
                u, v = strip_sides(vel, 0, win, -1), strip_sides(vel, 1, win, -1)
                old = (sig[i_a, :, cols], sig[i_b, :, cols]) if cycle else None
                sig[i_a, :, cols], sig[i_b, :, cols] = stress(u, v, S[3, :, cols], old)
            tile_stress(cycle == 0)
            close_top(AB, 0, sig, i_a, 1)
            close_top(AB, 1, sig, i_b, 1)
            for win in windows(left - 1):
                cols = slice(COLS * win[0], COLS * win[1])
                push(S, vel, every, cols, strip_sides(sig, i_a, win, 1), strip_sides(sig, i_b, win, 1))
            tile_push()

    @pl.when(is_top)
    def _():
        strips_ready()
        tile_ready()
        top_cycles((0, 1))
        SS2[0:2] = X[0:2, last8, 0:COLS]
        SS2[2:4] = AB[:, last8, 0:COLS]
        S2[:, :, middle] = SS2[...]
        strips_start(True)

    @pl.when(jnp.logical_not(is_top))
    def _():
        tile_ready()
        AB[:, 8 : 8 + SPAN, :] = jnp.zeros((2, SPAN, 2 * COLS), jnp.float32)
        lax.fori_loop(0, 2, tile_cycle, 0)

    regrid(0)
    stores = [store(0)]
    regrid(1)

    @pl.when(is_top)
    def _():
        strips_arrive(True)
        to_the_e = S2[0:2, 7:8, COLS * (REACH + 1) : COLS * (REACH + 2)]
        to_the_w = S2[0:2, 7:8, COLS * (REACH - 1) : COLS * REACH]
        X[0:2, TOP + ROWS - 1 : TOP + ROWS, COLS : 2 * COLS] = jnp.where(lane < COLS // 2, to_the_e, to_the_w)
        top_cycles((2, 3))

    @pl.when(jnp.logical_not(is_top))
    def _():
        lax.fori_loop(0, 2, tile_cycle, 0)

    away = pl.ds(pl.multiple_of(TOP + HALF * (1 - comp), 8), HALF)
    here = pl.ds(pl.multiple_of(TOP + HALF * comp, 8), HALF)
    ice_out = (new_ice_u, new_ice_v)
    vel_away, vel_here = [], []
    for i in range(2):
        copy = send(X.at[i, away, 0:COLS], ice_out[i].at[:, mine], vel_send.at[i], vel_recv.at[i], partner)
        copy.start()
        vel_away.append(copy)
        copy = pltpu.make_async_copy(X.at[i, here, 0:COLS], ice_out[i].at[:, mine], out_sem.at[3 + i])
        copy.start()
        vel_here.append(copy)

    for i in range(2):
        g = i + 1
        if g == 2:
            regrid(g)
        tau = X[i, tile_rows, 0:COLS] - X[5 + i, tile_rows, 0:COLS] * (1.0 / SHARE)
        O[g * LEV] = O[g * LEV] + COUPLE * (X[9, tile_rows, 0:COLS] * tau)
        stores.append(store(g))

    @pl.when(is_top)
    def _():
        strips_sent(False)
        strips_sent(True)

    for copy in ice_away:
        copy.wait_send()
    for copy in vel_away:
        copy.wait()
    for copy in vel_here + stores:
        copy.wait()


def deliver(*refs):
    count = len(refs) // 2
    sems = refs[-1]
    copies = [pltpu.make_async_copy(refs[i], refs[count + i], sems.at[i]) for i in range(count)]
    for copy in copies:
        copy.start()
    for copy in copies:
        copy.wait()


def solution(mesh):
    blocks = mesh.shape["gx"] * 2
    gys = mesh.shape["gy"]
    ocean = P(None, "gy", ("gx", "comp"))
    flat = P("gy", ("gx", "comp"))
    ice = P(("gy", "comp"), "gx")
    in_specs = (ocean, ocean, ocean, flat, P(), P(), P(), P(("gx", "comp")), ice, ice, ice, ice, ice)
    out_specs = (ocean, ocean, ocean, ice, ice)

    def body(tracer, ocean_u, ocean_v, ocean_mask, diffusivity, viscosity, remap, fold_partner, *ice_fields):
        f32 = jnp.float32
        anywhere = pl.BlockSpec(memory_space=pl.ANY)
        main_memory = pl.BlockSpec(memory_space=pltpu.HBM)
        vmem = pltpu.VMEM
        dma = pltpu.SemaphoreType.DMA
        ocean_shape = jax.ShapeDtypeStruct(tracer.shape, f32)
        ice_shape = jax.ShapeDtypeStruct(ice_fields[0].shape, f32)

        def step(*args):
            kernel(blocks, gys, *args)

        shapes = (ocean_shape, ocean_shape, ocean_shape, ice_shape, ice_shape)
        results = pl.pallas_call(
            step,
            out_shape=shapes,
            in_specs=[main_memory] * 13,
            out_specs=(anywhere,) * 5,
            scratch_shapes=[
                vmem((PLANES, 96, COLS), f32),
                vmem((3 * LEV, ROWS, COLS), jnp.bfloat16),
                vmem((3 * LEV, ROWS, COLS), jnp.bfloat16),
                vmem((LEV * LEV, 3 * LEV * LEV), jnp.bfloat16),
                vmem((3 * LEV, ROWS, COLS), f32),
                vmem((NF, 112, 2 * COLS), f32),
                vmem((2, 112, 2 * COLS), f32),
                vmem((NS, 8, BLOCKS * COLS), f32),
                vmem((2, 8, BLOCKS * COLS), f32),
                vmem((NS, 8, COLS), f32),
                vmem((4, 8, BLOCKS * COLS), f32),
                vmem((4, 8, COLS), f32),
                vmem((ROWS, COLS), f32),
                vmem((ROWS, COLS), f32),
                vmem((SPAN, COLS), f32),
                vmem((SPAN, COLS), f32),
                vmem((ROWS, COLS), f32),
                vmem((ROWS, COLS), f32),
                vmem((ROWS, COLS), f32),
                vmem((ROWS, COLS), f32),
                vmem((5, ROWS, COLS), f32),
                vmem((ROWS, COLS), jnp.int32),
                vmem((ROWS, COLS), jnp.int32),
                vmem((8, BLOCKS * COLS), jnp.int32),
                pltpu.SMEM((LEV,), f32),
                pltpu.SMEM((LEV,), f32),
                pltpu.SMEM((LEV, LEV), f32),
                vmem((LEV, LEV), f32),
                vmem((1, COLS), jnp.int32),
                dma((9,)),
                dma((5,)),
                dma((5,)),
                dma((5,)),
                dma((5,)),
                dma((5,)),
                dma((8,)),
                dma((8,)),
                dma((BLOCKS,)),
                dma((BLOCKS,)),
                dma((BLOCKS,)),
                dma((BLOCKS,)),
                dma((5,)),
                dma((2,)),
                dma((2,)),
            ],
            compiler_params=pltpu.CompilerParams(
                collective_id=0, has_side_effects=True, vmem_limit_bytes=32 * 1024 * 1024
            ),
        )(
            *[
                pltpu.with_memory_space_constraint(value, pltpu.HBM)
                for value in (
                    tracer,
                    ocean_u,
                    ocean_v,
                    ocean_mask,
                    diffusivity,
                    viscosity,
                    remap,
                    fold_partner.reshape(1, COLS),
                    *ice_fields,
                )
            ]
        )
        return pl.pallas_call(
            deliver,
            out_shape=shapes,
            in_specs=[anywhere] * 5,
            out_specs=(main_memory,) * 5,
            scratch_shapes=[dma((5,))],
            compiler_params=pltpu.CompilerParams(vmem_limit_bytes=1024 * 1024),
        )(*results)

    return jax.shard_map(body, mesh=mesh, in_specs=in_specs, out_specs=out_specs, check_vma=False)
```

```python
import jax
import jax.numpy as jnp
from jax import lax
from jax.experimental import pallas as pl
from jax.experimental.pallas import tpu as pltpu
from jax.sharding import PartitionSpec as P

ITERS = 4
RELAX = 0.5
STEP_SIZE = 0.3
COUPLE = 0.5
MESH = pl.DeviceIdType.MESH

LEV = 16
ROWS = 80
HALF = 40
COLS = 128
NF = 10
NS = NF + 1
REACH = 2
SIDE = 2 * REACH + 1
BLOCKS = 2 * SIDE
TOP = 16
SPAN = 96
OWN_REACH = {2: 0, 3: 1}
MIRROR_REACH = {1: 0, 2: 1, 3: 2}
OWN_ROWS = (8, 2, 1)
MIRROR_ROWS = (4, 3, 2)
PLANES = 3 * LEV + 1


def kernel(
    blocks,
    gys,
    tracer,
    ocean_u,
    ocean_v,
    ocean_mask,
    diffusivity_in,
    viscosity_in,
    remap_in,
    fold_in,
    ice_u,
    ice_v,
    ice_mass,
    ice_strength,
    ice_mask,
    new_tracer,
    new_ocean_u,
    new_ocean_v,
    new_ice_u,
    new_ice_v,
    F,
    DH,
    DL,
    KK,
    O,
    X,
    AB,
    XT,
    ABT,
    S,
    SAB,
    SS,
    S2,
    SS2,
    PE,
    PW,
    EB,
    WB,
    CP,
    RE,
    RW,
    GE,
    MK,
    OM,
    IM,
    IDX,
    diffusivity,
    viscosity,
    remap,
    remap_wide,
    fold_partner,
    in_sem,
    ice_sem,
    ice_send,
    ice_recv,
    edge_send,
    edge_recv,
    rim_send,
    rim_recv,
    strip_send,
    strip_recv,
    again_send,
    again_recv,
    out_sem,
    vel_send,
    vel_recv,
):
    gx, gy, comp = lax.axis_index("gx"), lax.axis_index("gy"), lax.axis_index("comp")
    me = gx * 2 + comp
    has_north = gy < gys - 1
    has_south = gy > 0
    is_top = gy == gys - 1

    def at(block, row):
        return {"gx": block // 2, "gy": row, "comp": lax.rem(block, 2)}

    def wrap(block):
        return lax.rem(block + 2 * blocks, blocks)

    east, west, mirror = wrap(me + 1), wrap(me - 1), blocks - 1 - me
    partner = at(gx * 2 + 1 - comp, gy)

    strips = [(SIDE + REACH, mirror, False, MIRROR_ROWS[0])]
    for d in (1, -1, 2, -2):
        strips.append((SIDE + REACH + d, wrap(mirror + d), d % 2 == 1, MIRROR_ROWS[abs(d)]))
        strips.append((REACH + d, wrap(me - d), False, OWN_ROWS[abs(d)]))

    barrier = pltpu.get_barrier_semaphore()

    def greet(target):
        pl.semaphore_signal(barrier, inc=1, device_id=target, device_id_type=MESH)

    greet(at(east, gy))
    greet(at(west, gy))

    @pl.when(has_north)
    def _():
        for block in (me, east, west):
            greet(at(block, gy + 1))

    @pl.when(has_south)
    def _():
        for block in (me, east, west):
            greet(at(block, gy - 1))

    @pl.when(is_top)
    def _():
        for _, block, own, _ in strips:
            if own:

                @pl.when(block != me)
                def _(block=block):
                    greet(at(block, gy))
            else:
                greet(at(block, gy))

    def load(src, dst, sem):
        copy = pltpu.make_async_copy(src, dst, sem)
        copy.start()
        return copy

    load_u = load(ocean_u, F.at[LEV : 2 * LEV, 8 : 8 + ROWS, :], in_sem.at[0])
    load_v = load(ocean_v, F.at[2 * LEV : 3 * LEV, 8 : 8 + ROWS, :], in_sem.at[1])
    load_t = load(tracer, F.at[0:LEV, 8 : 8 + ROWS, :], in_sem.at[3])
    small = [
        load(ocean_mask, OM, in_sem.at[2]),
        load(remap_in, remap, in_sem.at[4]),
        load(diffusivity_in, diffusivity, in_sem.at[5]),
        load(viscosity_in, viscosity, in_sem.at[6]),
        load(fold_in, fold_partner, in_sem.at[7]),
        load(remap_in, remap_wide, in_sem.at[8]),
    ]
    ice_in = (ice_u, ice_v, ice_mass, ice_strength, ice_mask)

    def ice_place(i, half):
        rows = pl.ds(pl.multiple_of(TOP + HALF * half, 8), HALF)
        if i == 4:
            return IM.at[pl.ds(pl.multiple_of(HALF * half, 8), HALF), :]
        return X.at[i, rows, 0:COLS]

    mine = pl.ds(pl.multiple_of(COLS * comp, COLS), COLS)
    other = pl.ds(pl.multiple_of(COLS * (1 - comp), COLS), COLS)
    ice_local = [load(ice_in[i].at[:, mine], ice_place(i, comp), ice_sem.at[i]) for i in range(5)]

    first8, last8 = slice(TOP, TOP + 8), slice(TOP + ROWS - 8, TOP + ROWS)
    south8, north8 = slice(TOP - 8, TOP), slice(TOP + ROWS, TOP + ROWS + 8)

    @pl.when(jnp.logical_not(has_south))
    def _():
        X[:, south8, 0:COLS] = jnp.zeros((NF, 8, COLS), jnp.float32)
        EB[0:8, :] = jnp.zeros((8, COLS), jnp.float32)
        WB[0:8, :] = jnp.zeros((8, COLS), jnp.float32)
        F[:, 0:8, :] = jnp.zeros((PLANES, 8, COLS), jnp.float32)

    @pl.when(is_top)
    def _():
        X[:, north8, 0:COLS] = jnp.zeros((NF, 8, COLS), jnp.float32)
        EB[88:96, :] = jnp.zeros((8, COLS), jnp.float32)
        WB[88:96, :] = jnp.zeros((8, COLS), jnp.float32)

    outer = jnp.zeros((NF, 8, 2 * COLS), jnp.float32)
    X[:, 0:8, :] = outer
    X[:, 104:112, :] = outer
    AB[...] = jnp.zeros((2, 112, 2 * COLS), jnp.float32)

    count = 2 + 3 * has_north.astype(jnp.int32) + 3 * has_south.astype(jnp.int32)
    strip_count = 0
    for _, block, own, _ in strips:
        strip_count = strip_count + ((block != me).astype(jnp.int32) if own else 1)
    count = count + is_top.astype(jnp.int32) * strip_count
    pl.semaphore_wait(barrier, count)

    def send(src, dst, send_sem, recv_sem, target):
        copy = pltpu.make_async_remote_copy(
            src_ref=src,
            dst_ref=dst,
            send_sem=send_sem,
            recv_sem=recv_sem,
            device_id=target,
            device_id_type=MESH,
        )
        return copy

    ice_away = []
    for i in range(5):
        copy = send(
            ice_in[i].at[:, other], ice_place(i, comp), ice_send.at[i], ice_recv.at[i], partner
        )
        copy.start()
        ice_away.append(copy)

    lane = lax.broadcasted_iota(jnp.int32, (1, COLS), 1)
    row8 = lax.broadcasted_iota(jnp.int32, (8, 1), 0)
    tile_rows = slice(TOP, TOP + ROWS)

    for copy in small:
        copy.wait()
    sea = OM[...].astype(jnp.float32)
    X[9, tile_rows, 0:COLS] = sea
    F[3 * LEV, 8 : 8 + ROWS, :] = sea
    for i, copy in ((0, load_u), (1, load_v)):
        copy.wait()
        base = jnp.zeros((ROWS, COLS), jnp.float32)
        spread = jnp.zeros((ROWS, COLS), jnp.float32)
        for l in range(LEV):
            weighted = remap[0, l] * F[LEV * (i + 1) + l, 8 : 8 + ROWS, :]
            base = base + weighted
            spread = spread + viscosity[l] * weighted
        X[5 + i, tile_rows, 0:COLS] = base
        X[7 + i, tile_rows, 0:COLS] = spread

    load_t.wait()
    row_n = send(F.at[:, 87:88, :], F.at[:, 7:8, :], edge_send.at[2], edge_recv.at[2], at(me, gy + 1))
    row_s = send(F.at[:, 8:9, :], F.at[:, 88:89, :], edge_send.at[3], edge_recv.at[3], at(me, gy - 1))
    row_f = send(F.at[:, 87:88, :], F.at[:, 88:89, :], edge_send.at[4], edge_recv.at[4], at(mirror, gy))

    @pl.when(has_north)
    def _():
        row_n.start()

    @pl.when(has_south)
    def _():
        row_s.start()

    @pl.when(is_top)
    def _():
        row_f.start()

    def pack(f, packed):
        return jnp.where((lane >> 1) == f, pltpu.roll(F[f, 8 : 8 + ROWS, :], 2 * f + 1, 1), packed)

    CP[...] = lax.fori_loop(0, PLANES, pack, jnp.zeros((ROWS, COLS), jnp.float32), unroll=7)
    col_to_e = send(CP, RW, edge_send.at[0], edge_recv.at[0], at(east, gy))
    col_to_w = send(CP, RE, edge_send.at[1], edge_recv.at[1], at(west, gy))
    col_to_e.start()
    col_to_w.start()

    lane2 = lax.broadcasted_iota(jnp.int32, (LEV, LEV * LEV), 1)
    weights = jnp.zeros((LEV, LEV * LEV), jnp.float32)
    for l in range(LEV):
        weights = jnp.where((lane2 >> 4) == l, remap_wide[:, l : l + 1], weights)
    high = weights.astype(jnp.bfloat16).astype(jnp.float32)
    low = weights - high
    diagonal = (lane2 & 15) == lax.broadcasted_iota(jnp.int32, (LEV, LEV * LEV), 0)
    for k in range(LEV):
        rows = slice(LEV * k, LEV * (k + 1))
        high_k = jnp.where(diagonal, high[k : k + 1], 0.0).astype(jnp.bfloat16)
        KK[rows, 0:256] = high_k
        KK[rows, 256:512] = jnp.where(diagonal, low[k : k + 1], 0.0).astype(jnp.bfloat16)
        KK[rows, 512:768] = high_k

    for i in range(5):
        ice_local[i].wait()
        ice_away[i].wait_recv()
    X[4, tile_rows, 0:COLS] = IM[...].astype(jnp.float32)

    pack_e = jnp.zeros((ROWS, COLS), jnp.float32)
    pack_w = jnp.zeros((ROWS, COLS), jnp.float32)
    for f in range(NF):
        value = X[f, tile_rows, 0:COLS]
        keep = (lane >= 8 * f) & (lane < 8 * f + 8)
        pack_e = jnp.where(keep, pltpu.roll(value, 8 * f + 8, 1), pack_e)
        pack_w = jnp.where(keep, pltpu.roll(value, 8 * f, 1) if f else value, pack_w)
    PE[...] = pack_e
    PW[...] = pack_w
    to_e = send(PE, WB.at[8 : 8 + ROWS], rim_send.at[0], rim_recv.at[0], at(east, gy))
    to_w = send(PW, EB.at[8 : 8 + ROWS], rim_send.at[1], rim_recv.at[1], at(west, gy))
    to_n = [
        send(X.at[:, last8, 0:COLS], X.at[:, south8, 0:COLS], rim_send.at[2], rim_recv.at[2], at(me, gy + 1)),
        send(PE.at[ROWS - 8 : ROWS], WB.at[0:8], rim_send.at[3], rim_recv.at[3], at(east, gy + 1)),
        send(PW.at[ROWS - 8 : ROWS], EB.at[0:8], rim_send.at[4], rim_recv.at[4], at(west, gy + 1)),
    ]
    to_s = [
        send(X.at[:, first8, 0:COLS], X.at[:, north8, 0:COLS], rim_send.at[5], rim_recv.at[5], at(me, gy - 1)),
        send(PE.at[0:8], WB.at[88:96], rim_send.at[6], rim_recv.at[6], at(east, gy - 1)),
        send(PW.at[0:8], EB.at[88:96], rim_send.at[7], rim_recv.at[7], at(west, gy - 1)),
    ]

    def strip_ends(src, dst, slot, rows):
        kept = slice(8 - rows, 8)
        return src.at[:, kept, :], dst.at[:, kept, COLS * slot : COLS * (slot + 1)]

    def strip_copy(again, slot, block, rows):
        src, dst = strip_ends(SS2, S2, slot, rows) if again else strip_ends(SS, S, slot, rows)
        sent, received = (again_send, again_recv) if again else (strip_send, strip_recv)
        return send(src, dst, sent.at[slot], received.at[slot], at(block, gy))

    def strips_start(again):
        for slot, block, own, rows in strips:
            if own:

                @pl.when(block != me)
                def _(slot=slot, block=block, rows=rows):
                    strip_copy(again, slot, block, rows).start()

                @pl.when(block == me)
                def _(slot=slot, rows=rows):
                    src, dst = strip_ends(SS2, S2, slot, rows) if again else strip_ends(SS, S, slot, rows)
                    pltpu.make_async_copy(src, dst, (again_recv if again else strip_recv).at[slot]).start()
            else:
                strip_copy(again, slot, block, rows).start()

    def strips_arrive(again):
        for slot, block, own, rows in strips:
            strip_copy(again, slot, block, rows).wait_recv()

    def strips_sent(again):
        for slot, block, own, rows in strips:
            if own:

                @pl.when(block != me)
                def _(slot=slot, block=block, rows=rows):
                    strip_copy(again, slot, block, rows).wait_send()
            else:
                strip_copy(again, slot, block, rows).wait_send()

    middle = slice(COLS * REACH, COLS * (REACH + 1))

    to_e.start()
    to_w.start()

    @pl.when(has_north)
    def _():
        for copy in to_n:
            copy.start()

    @pl.when(has_south)
    def _():
        for copy in to_s:
            copy.start()

    @pl.when(is_top)
    def _():
        SS[0:NF] = X[0:NF, last8, 0:COLS]
        inside = fold_partner[...] - COLS * mirror
        SS[NF] = jnp.broadcast_to(inside.astype(jnp.float32), (8, COLS))
        S[:, :, middle] = SS[...]
        strips_start(False)

    to_e.wait()
    to_w.wait()

    @pl.when(has_north)
    def _():
        for copy in to_n:
            copy.wait_send()
        for copy in to_s:
            copy.wait_recv()

    @pl.when(has_south)
    def _():
        for copy in to_s:
            copy.wait_send()
        for copy in to_n:
            copy.wait_recv()

    for f in range(NF):
        from_e = pltpu.roll(EB[...], COLS - 8 * f, 1) if f else EB[...]
        from_w = pltpu.roll(WB[...], COLS - 8 - 8 * f, 1)
        X[f, 8 : 8 + SPAN, COLS : 2 * COLS] = jnp.where(
            lane < 8, from_e, jnp.where(lane >= COLS - 8, from_w, 0.0)
        )

    def inside_of(i):
        return IDX[:, COLS * i : COLS * (i + 1)]

    def fold_block(ref, f, i, sign):
        j = BLOCKS - 1 - i
        value = ref[f, :, COLS * j : COLS * (j + 1)]
        taken = jnp.take_along_axis(value, inside_of(i), axis=1, mode="promise_in_bounds")
        return taken if sign > 0 else -taken

    def close_top(ref, f, strip_ref, sf, sign):
        own = fold_block(strip_ref, sf, REACH, sign)
        to_the_e = fold_block(strip_ref, sf, REACH + 1, sign)
        to_the_w = fold_block(strip_ref, sf, REACH - 1, sign)
        ref[f, 24:25, 0:COLS] = own[7:8]
        ref[f, 24:25, COLS : 2 * COLS] = jnp.where(lane < COLS // 2, to_the_e, to_the_w)[7:8]

    def window(first, reach):
        middle = first + REACH
        low, high = middle - reach, middle + reach + 1
        wide_low, wide_high = max(low - 1, first), min(high + 1, first + SIDE)
        return low, high, wide_low, wide_high

    def strip_sides(ref, f, win, sign):
        low, high, wide_low, wide_high = win
        wide = ref[f, :, COLS * wide_low : COLS * wide_high]
        length = COLS * (wide_high - wide_low)
        cut = slice(COLS * (low - wide_low), COLS * (high - wide_low))
        value = wide[:, cut]
        to_east = pltpu.roll(wide, length - 1, 1)[:, cut]
        to_west = pltpu.roll(wide, 1, 1)[:, cut]
        folded = jnp.concatenate([fold_block(ref, f, i, sign) for i in range(low, high)], axis=1)
        to_north = jnp.where(row8 == 7, folded, pltpu.roll(value, 7, 0))
        to_south = pltpu.roll(value, 1, 0)
        return value, to_east, to_west, to_north, to_south

    def windows(left):
        found = []
        if left in OWN_REACH:
            found.append(window(0, OWN_REACH[left]))
        if left in MIRROR_REACH:
            found.append(window(SIDE, MIRROR_REACH[left]))
        return found

    def lap_of(seas, values):
        total = seas[1] * (values[1] - values[0])
        for i in range(2, 5):
            total = total + seas[i] * (values[i] - values[0])
        return total * seas[0]

    SHARE = STEP_SIZE / (1.0 + STEP_SIZE)
    KEEP = 1.0 / (1.0 + STEP_SIZE)

    def ready(ref, rows, cols, surfaces):
        present = ref[4, rows, cols]
        ref[5, rows, cols] = SHARE * present * surfaces[0]
        ref[6, rows, cols] = SHARE * present * surfaces[1]
        mass = ref[2, rows, cols]
        ref[2, rows, cols] = 0.5 * SHARE * present / jnp.where(mass > 0.0, mass, 1.0)
        ref[4, rows, cols] = KEEP * present

    def strips_ready():
        for win in windows(2):
            cols = slice(COLS * win[0], COLS * win[1])
            seas = strip_sides(S, 9, win, 1)
            surfaces = [
                S[5 + i, :, cols] + lap_of(seas, strip_sides(S, 7 + i, win, -1)) for i in range(2)
            ]
            ready(S, slice(0, 8), cols, surfaces)
        S[3] = S[3] * (RELAX / (1.0 + RELAX))

    def main_sides(ref, f, start, size):
        value = ref[f, start : start + size, :]
        return (
            value,
            pltpu.roll(value, 2 * COLS - 1, 1),
            pltpu.roll(value, 1, 1),
            ref[f, start + 1 : start + size + 1, :],
            ref[f, start - 1 : start + size - 1, :],
        )

    CHUNK = 24
    chunks = range(8, 8 + SPAN, CHUNK)

    def chunk_ready(ref, start):
        rows = slice(start, start + CHUNK)
        seas = main_sides(ref, 9, start, CHUNK)
        surfaces = [ref[5 + i, rows, :] + lap_of(seas, main_sides(ref, 7 + i, start, CHUNK)) for i in range(2)]
        ready(ref, rows, slice(0, 2 * COLS), surfaces)
        ref[3, rows, :] = ref[3, rows, :] * (RELAX / (1.0 + RELAX))

    def stress(u, v, third, old):
        twice_d = (u[1] - u[2]) + (v[3] - v[4])
        twice_h = (u[3] - u[4]) + (v[1] - v[2])
        viscous = third * lax.rsqrt(twice_d * twice_d + 0.25 * (twice_h * twice_h) + 0.04)
        a = viscous * twice_d - third
        b = viscous * twice_h
        if old is not None:
            a = a + old[0] * (1.0 / (1.0 + RELAX))
            b = b + old[1] * (1.0 / (1.0 + RELAX))
        return a, b

    def push(ref, vel, rows, cols, a, b):
        keep, mobility = ref[4, rows, cols], ref[2, rows, cols]
        new_u = keep * vel[0, rows, cols] + mobility * ((a[1] - a[2]) + (b[3] - b[4])) + ref[5, rows, cols]
        new_v = keep * vel[1, rows, cols] + mobility * ((b[1] - b[2]) + (a[3] - a[4])) + ref[6, rows, cols]
        vel[0, rows, cols] = new_u
        vel[1, rows, cols] = new_v

    every = slice(0, 8)

    def chunk_stress(vel, sig, start, first=False):
        rows = slice(start, start + CHUNK)
        u, v = main_sides(vel, 0, start, CHUNK), main_sides(vel, 1, start, CHUNK)
        old = None if first else (sig[0, rows, :], sig[1, rows, :])
        sig[0, rows, :], sig[1, rows, :] = stress(u, v, vel[3, rows, :], old)

    def chunk_push(vel, sig, start):
        a, b = main_sides(sig, 0, start, CHUNK), main_sides(sig, 1, start, CHUNK)
        push(vel, vel, slice(start, start + CHUNK), slice(0, 2 * COLS), a, b)

    def tile_cycle(cycle, carry):
        for start in chunks:
            chunk_stress(X, AB, start)
        for start in chunks:
            chunk_push(X, AB, start)
        return carry

    low_piece, high_piece, low_tile, high_tile = slice(8, 16), slice(16, 24), slice(80, 88), slice(88, 96)

    def top_cycles(cycles):
        vel, sig, i_a, i_b = (S, SAB, 0, 1) if cycles[0] == 0 else (S2, S2, 2, 3)
        for cycle in cycles:
            left = 3 if cycle == cycles[0] else 1
            close_top(XT, 0, vel, 0, -1)
            close_top(XT, 1, vel, 1, -1)
            for win in windows(left):
                cols = slice(COLS * win[0], COLS * win[1])
                u, v = strip_sides(vel, 0, win, -1), strip_sides(vel, 1, win, -1)
                old = (sig[i_a, :, cols], sig[i_b, :, cols]) if cycle else None
                sig[i_a, :, cols], sig[i_b, :, cols] = stress(u, v, S[3, :, cols], old)
            chunk_stress(XT, ABT, 8, cycle == 0)
            close_top(ABT, 0, sig, i_a, 1)
            close_top(ABT, 1, sig, i_b, 1)
            for win in windows(left - 1):
                cols = slice(COLS * win[0], COLS * win[1])
                push(S, vel, every, cols, strip_sides(sig, i_a, win, 1), strip_sides(sig, i_b, win, 1))
            chunk_push(XT, ABT, 8)

    @pl.when(is_top)
    def _():
        XT[...] = X[:, 72:112, :]
        ABT[...] = jnp.zeros((2, 40, 2 * COLS), jnp.float32)

    for start in chunks:
        chunk_ready(X, start)
    lax.fori_loop(0, 2, tile_cycle, 0)

    @pl.when(is_top)
    def _():
        strips_arrive(False)
        IDX[...] = jnp.broadcast_to(S[NF, 7:8, :], IDX.shape).astype(jnp.int32)
        for f, sign in ((7, -1), (8, -1), (9, 1)):
            close_top(XT, f, S, f, sign)
        strips_ready()
        chunk_ready(XT, 8)
        top_cycles((0, 1))
        SS2[0:2] = XT[0:2, high_piece, 0:COLS]
        SS2[2:4] = ABT[:, high_piece, 0:COLS]
        strips_start(True)
        S2[:, :, middle] = SS2[...]
        X[0:2, high_tile, :] = XT[0:2, high_piece, :]
        X[5:7, high_tile, :] = XT[5:7, high_piece, :]
        AB[:, high_tile, :] = ABT[:, high_piece, :]
        XT[0:2, low_piece, :] = X[0:2, low_tile, :]
        ABT[:, low_piece, :] = AB[:, low_tile, :]

    lax.fori_loop(0, 2, tile_cycle, 0)

    away = pl.ds(pl.multiple_of(TOP + HALF * (1 - comp), 8), HALF)
    here = pl.ds(pl.multiple_of(TOP + HALF * comp, 8), HALF)
    ice_out = (new_ice_u, new_ice_v)
    vel_away = [
        send(X.at[i, away, 0:COLS], ice_out[i].at[:, mine], vel_send.at[i], vel_recv.at[i], partner) for i in range(2)
    ]
    vel_here = [
        pltpu.make_async_copy(X.at[i, here, 0:COLS], ice_out[i].at[:, mine], out_sem.at[3 + i]) for i in range(2)
    ]

    @pl.when(jnp.logical_not(is_top))
    def _():
        for copy in vel_away + vel_here:
            copy.start()

    col_to_e.wait()
    col_to_w.wait()

    @pl.when(has_north)
    def _():
        row_n.wait_send()
        row_s.wait_recv()

    @pl.when(has_south)
    def _():
        row_s.wait_send()
        row_n.wait_recv()


    @pl.when(is_top)
    def _():
        row_f.wait()
        inside = jnp.broadcast_to(fold_partner[...] - COLS * mirror, (8, COLS))

        def fold_edge(f, carry):
            taken = jnp.take_along_axis(F[f, 88:96, :], inside, axis=1, mode="promise_in_bounds")
            F[f, 88:96, :] = jnp.where((f < LEV) | (f == 3 * LEV), taken, -taken)
            return carry

        lax.fori_loop(0, PLANES, fold_edge, 0, unroll=7)

    GE[...] = jnp.where((lane & 1) == 0, pltpu.roll(RE[...], COLS - 1, 1), pltpu.roll(RW[...], 1, 1))

    def plane_sides(f):
        value = F[f, 8 : 8 + ROWS, :]
        edges = pltpu.roll(GE[...], COLS - 1 - 2 * f, 1)
        to_east = jnp.where(lane == COLS - 1, edges, pltpu.roll(value, COLS - 1, 1))
        to_west = jnp.where(lane == 0, edges, pltpu.roll(value, 1, 1))
        return value, to_east, to_west, F[f, 9 : 9 + ROWS, :], F[f, 7 : 7 + ROWS, :]

    seas = plane_sides(3 * LEV)
    degree = jnp.zeros((ROWS, COLS), jnp.float32)
    for i in range(4):
        weight = seas[0] * seas[i + 1]
        MK[i] = weight
        degree = degree + weight
    MK[4] = degree

    def diffuse(g):
        coefficient = diffusivity if g == 0 else viscosity

        def one(l, carry):
            f = g * LEV + l
            value, to_east, to_west, to_north, to_south = plane_sides(f)
            total = MK[0] * to_east + MK[1] * to_west + MK[2] * to_north + MK[3] * to_south
            new = value + coefficient[l] * (total - MK[4] * value)
            high = new.astype(jnp.bfloat16)
            DH[f] = high
            DL[f] = (new - high.astype(jnp.float32)).astype(jnp.bfloat16)
            return carry

        lax.fori_loop(0, LEV, one, 0, unroll=4)

    def regrid(g):
        planes = slice(g * LEV, (g + 1) * LEV)
        pieces = range(0, ROWS, LEV)
        high = jnp.concatenate([DH[planes, r : r + LEV, :].reshape(LEV * LEV, COLS) for r in pieces], axis=1)
        low = jnp.concatenate([DL[planes, r : r + LEV, :].reshape(LEV * LEV, COLS) for r in pieces], axis=1)
        new = jnp.dot(KK[...], jnp.concatenate([high, high, low], axis=0), preferred_element_type=jnp.float32)
        for i, r in enumerate(pieces):
            O[planes, r : r + LEV, :] = new[:, COLS * i : COLS * (i + 1)].reshape(LEV, LEV, COLS)

    outs = (new_tracer, new_ocean_u, new_ocean_v)

    def store(g):
        copy = pltpu.make_async_copy(O.at[g * LEV : (g + 1) * LEV], outs[g], out_sem.at[g])
        copy.start()
        return copy

    diffuse(0)
    diffuse(1)

    @pl.when(is_top)
    def _():
        strips_arrive(True)
        to_the_e = S2[0:2, 7:8, COLS * (REACH + 1) : COLS * (REACH + 2)]
        to_the_w = S2[0:2, 7:8, COLS * (REACH - 1) : COLS * REACH]
        XT[0:2, 23:24, COLS : 2 * COLS] = jnp.where(lane < COLS // 2, to_the_e, to_the_w)
        top_cycles((2, 3))
        X[0:2, high_tile, :] = XT[0:2, high_piece, :]
        for copy in vel_away + vel_here:
            copy.start()

    diffuse(2)
    regrid(0)
    stores = [store(0)]

    for i in range(2):
        g = i + 1
        regrid(g)
        tau = X[i, tile_rows, 0:COLS] - X[5 + i, tile_rows, 0:COLS] * (1.0 / SHARE)
        O[g * LEV] = O[g * LEV] + COUPLE * (X[9, tile_rows, 0:COLS] * tau)
        stores.append(store(g))

    @pl.when(is_top)
    def _():
        strips_sent(False)
        strips_sent(True)

    for copy in ice_away:
        copy.wait_send()
    for copy in vel_away:
        copy.wait()
    for copy in vel_here + stores:
        copy.wait()


def deliver(*refs):
    count = len(refs) // 2
    sems = refs[-1]
    copies = [pltpu.make_async_copy(refs[i], refs[count + i], sems.at[i]) for i in range(count)]
    for copy in copies:
        copy.start()
    for copy in copies:
        copy.wait()


def solution(mesh):
    blocks = mesh.shape["gx"] * 2
    gys = mesh.shape["gy"]
    ocean = P(None, "gy", ("gx", "comp"))
    flat = P("gy", ("gx", "comp"))
    ice = P(("gy", "comp"), "gx")
    in_specs = (ocean, ocean, ocean, flat, P(), P(), P(), P(("gx", "comp")), ice, ice, ice, ice, ice)
    out_specs = (ocean, ocean, ocean, ice, ice)

    def body(tracer, ocean_u, ocean_v, ocean_mask, diffusivity, viscosity, remap, fold_partner, *ice_fields):
        f32 = jnp.float32
        anywhere = pl.BlockSpec(memory_space=pl.ANY)
        main_memory = pl.BlockSpec(memory_space=pltpu.HBM)
        vmem = pltpu.VMEM
        dma = pltpu.SemaphoreType.DMA
        ocean_shape = jax.ShapeDtypeStruct(tracer.shape, f32)
        ice_shape = jax.ShapeDtypeStruct(ice_fields[0].shape, f32)

        def step(*args):
            kernel(blocks, gys, *args)

        shapes = (ocean_shape, ocean_shape, ocean_shape, ice_shape, ice_shape)
        results = pl.pallas_call(
            step,
            out_shape=shapes,
            in_specs=[main_memory] * 13,
            out_specs=(anywhere,) * 5,
            scratch_shapes=[
                vmem((PLANES, 96, COLS), f32),
                vmem((3 * LEV, ROWS, COLS), jnp.bfloat16),
                vmem((3 * LEV, ROWS, COLS), jnp.bfloat16),
                vmem((LEV * LEV, 3 * LEV * LEV), jnp.bfloat16),
                vmem((3 * LEV, ROWS, COLS), f32),
                vmem((NF, 112, 2 * COLS), f32),
                vmem((2, 112, 2 * COLS), f32),
                vmem((NF, 40, 2 * COLS), f32),
                vmem((2, 40, 2 * COLS), f32),
                vmem((NS, 8, BLOCKS * COLS), f32),
                vmem((2, 8, BLOCKS * COLS), f32),
                vmem((NS, 8, COLS), f32),
                vmem((4, 8, BLOCKS * COLS), f32),
                vmem((4, 8, COLS), f32),
                vmem((ROWS, COLS), f32),
                vmem((ROWS, COLS), f32),
                vmem((SPAN, COLS), f32),
                vmem((SPAN, COLS), f32),
                vmem((ROWS, COLS), f32),
                vmem((ROWS, COLS), f32),
                vmem((ROWS, COLS), f32),
                vmem((ROWS, COLS), f32),
                vmem((5, ROWS, COLS), f32),
                vmem((ROWS, COLS), jnp.int32),
                vmem((ROWS, COLS), jnp.int32),
                vmem((8, BLOCKS * COLS), jnp.int32),
                pltpu.SMEM((LEV,), f32),
                pltpu.SMEM((LEV,), f32),
                pltpu.SMEM((LEV, LEV), f32),
                vmem((LEV, LEV), f32),
                vmem((1, COLS), jnp.int32),
                dma((9,)),
                dma((5,)),
                dma((5,)),
                dma((5,)),
                dma((5,)),
                dma((5,)),
                dma((8,)),
                dma((8,)),
                dma((BLOCKS,)),
                dma((BLOCKS,)),
                dma((BLOCKS,)),
                dma((BLOCKS,)),
                dma((5,)),
                dma((2,)),
                dma((2,)),
            ],
            compiler_params=pltpu.CompilerParams(
                collective_id=0, has_side_effects=True, vmem_limit_bytes=32 * 1024 * 1024
            ),
        )(
            *[
                pltpu.with_memory_space_constraint(value, pltpu.HBM)
                for value in (
                    tracer,
                    ocean_u,
                    ocean_v,
                    ocean_mask,
                    diffusivity,
                    viscosity,
                    remap,
                    fold_partner.reshape(1, COLS),
                    *ice_fields,
                )
            ]
        )
        return pl.pallas_call(
            deliver,
            out_shape=shapes,
            in_specs=[anywhere] * 5,
            out_specs=(main_memory,) * 5,
            scratch_shapes=[dma((5,))],
            compiler_params=pltpu.CompilerParams(vmem_limit_bytes=1024 * 1024),
        )(*results)

    return jax.shard_map(body, mesh=mesh, in_specs=in_specs, out_specs=out_specs, check_vma=False)
```

```python
import jax
import jax.numpy as jnp
from jax import lax
from jax.experimental import pallas as pl
from jax.experimental.pallas import tpu as pltpu
from jax.sharding import PartitionSpec as P

ITERS = 4
RELAX = 0.5
STEP_SIZE = 0.3
COUPLE = 0.5
MESH = pl.DeviceIdType.MESH

LEV = 16
ROWS = 80
HALF = 40
COLS = 128
NF = 7
NS = NF + 1
REACH = 2
SIDE = 2 * REACH + 1
BLOCKS = 2 * SIDE
TOP = 16
SPAN = 96
OWN_REACH = {2: 0, 3: 1}
MIRROR_REACH = {1: 0, 2: 1, 3: 2}
OWN_ROWS = (8, 2, 1)
MIRROR_ROWS = (4, 3, 2)
SEA = 3 * LEV
PLANES = SEA + 3


def kernel(
    blocks,
    gys,
    tracer,
    ocean_u,
    ocean_v,
    ocean_mask,
    diffusivity_in,
    viscosity_in,
    remap_in,
    fold_in,
    ice_u,
    ice_v,
    ice_mass,
    ice_strength,
    ice_mask,
    new_tracer,
    new_ocean_u,
    new_ocean_v,
    new_ice_u,
    new_ice_v,
    F,
    DH,
    DL,
    KK,
    O,
    X,
    AB,
    XT,
    ABT,
    S,
    SAB,
    SS,
    S2,
    SS2,
    PE,
    PW,
    EB,
    WB,
    EBS,
    WBS,
    EBN,
    WBN,
    CE,
    CW,
    RE,
    RW,
    GE,
    MK,
    OM,
    IM,
    IDX,
    diffusivity,
    viscosity,
    remap,
    remap_wide,
    fold_partner,
    in_sem,
    ice_sem,
    ice_send,
    ice_recv,
    edge_send,
    edge_recv,
    rim_send,
    rim_recv,
    strip_send,
    strip_recv,
    again_send,
    again_recv,
    out_sem,
    vel_send,
    vel_recv,
):
    gx, gy, comp = lax.axis_index("gx"), lax.axis_index("gy"), lax.axis_index("comp")
    me = gx * 2 + comp
    has_north = gy < gys - 1
    has_south = gy > 0
    is_top = gy == gys - 1

    def at(block, row):
        return {"gx": block // 2, "gy": row, "comp": lax.rem(block, 2)}

    def wrap(block):
        return lax.rem(block + 2 * blocks, blocks)

    east, west, mirror = wrap(me + 1), wrap(me - 1), blocks - 1 - me
    partner = at(gx * 2 + 1 - comp, gy)

    strips = [(SIDE + REACH, mirror, False, MIRROR_ROWS[0])]
    for d in (1, -1, 2, -2):
        strips.append((SIDE + REACH + d, wrap(mirror + d), d % 2 == 1, MIRROR_ROWS[abs(d)]))
        strips.append((REACH + d, wrap(me - d), False, OWN_ROWS[abs(d)]))

    barrier = pltpu.get_barrier_semaphore()

    def greet(target):
        pl.semaphore_signal(barrier, inc=1, device_id=target, device_id_type=MESH)

    greet(at(east, gy))
    greet(at(west, gy))

    @pl.when(has_north)
    def _():
        for block in (me, east, west):
            greet(at(block, gy + 1))

    @pl.when(has_south)
    def _():
        for block in (me, east, west):
            greet(at(block, gy - 1))

    @pl.when(is_top)
    def _():
        for _, block, own, _ in strips:
            if own:

                @pl.when(block != me)
                def _(block=block):
                    greet(at(block, gy))
            else:
                greet(at(block, gy))

    def load(src, dst, sem):
        copy = pltpu.make_async_copy(src, dst, sem)
        copy.start()
        return copy

    load_u = load(ocean_u, F.at[LEV : 2 * LEV, 8 : 8 + ROWS, :], in_sem.at[0])
    load_v = load(ocean_v, F.at[2 * LEV : 3 * LEV, 8 : 8 + ROWS, :], in_sem.at[1])
    load_t = load(tracer, F.at[0:LEV, 8 : 8 + ROWS, :], in_sem.at[3])
    small = [
        load(ocean_mask, OM, in_sem.at[2]),
        load(remap_in, remap, in_sem.at[4]),
        load(diffusivity_in, diffusivity, in_sem.at[5]),
        load(viscosity_in, viscosity, in_sem.at[6]),
        load(fold_in, fold_partner, in_sem.at[7]),
        load(remap_in, remap_wide, in_sem.at[8]),
    ]
    ice_in = (ice_u, ice_v, ice_mass, ice_strength, ice_mask)

    def ice_place(i, half):
        rows = pl.ds(pl.multiple_of(TOP + HALF * half, 8), HALF)
        if i == 4:
            return IM.at[pl.ds(pl.multiple_of(HALF * half, 8), HALF), :]
        return X.at[i, rows, 0:COLS]

    mine = pl.ds(pl.multiple_of(COLS * comp, COLS), COLS)
    other = pl.ds(pl.multiple_of(COLS * (1 - comp), COLS), COLS)
    ice_local = [load(ice_in[i].at[:, mine], ice_place(i, comp), ice_sem.at[i]) for i in range(5)]

    first8, last8 = slice(TOP, TOP + 8), slice(TOP + ROWS - 8, TOP + ROWS)
    south8, north8 = slice(TOP - 8, TOP), slice(TOP + ROWS, TOP + ROWS + 8)

    @pl.when(jnp.logical_not(has_south))
    def _():
        X[:, south8, 0:COLS] = jnp.zeros((NF, 8, COLS), jnp.float32)
        EBS[...] = jnp.zeros((8, COLS), jnp.float32)
        WBS[...] = jnp.zeros((8, COLS), jnp.float32)
        F[:, 0:8, :] = jnp.zeros((PLANES, 8, COLS), jnp.float32)

    @pl.when(is_top)
    def _():
        X[:, north8, 0:COLS] = jnp.zeros((NF, 8, COLS), jnp.float32)
        EBN[...] = jnp.zeros((8, COLS), jnp.float32)
        WBN[...] = jnp.zeros((8, COLS), jnp.float32)

    outer = jnp.zeros((NF, 8, 2 * COLS), jnp.float32)
    X[:, 0:8, :] = outer
    X[:, 104:112, :] = outer
    AB[...] = jnp.zeros((2, 112, 2 * COLS), jnp.float32)

    count = 2 + 3 * has_north.astype(jnp.int32) + 3 * has_south.astype(jnp.int32)
    strip_count = 0
    for _, block, own, _ in strips:
        strip_count = strip_count + ((block != me).astype(jnp.int32) if own else 1)
    count = count + is_top.astype(jnp.int32) * strip_count
    pl.semaphore_wait(barrier, count)

    def send(src, dst, send_sem, recv_sem, target):
        copy = pltpu.make_async_remote_copy(
            src_ref=src,
            dst_ref=dst,
            send_sem=send_sem,
            recv_sem=recv_sem,
            device_id=target,
            device_id_type=MESH,
        )
        return copy

    ice_away = []
    for i in range(5):
        copy = send(
            ice_in[i].at[:, other], ice_place(i, comp), ice_send.at[i], ice_recv.at[i], partner
        )
        copy.start()
        ice_away.append(copy)

    lane = lax.broadcasted_iota(jnp.int32, (1, COLS), 1)
    row8 = lax.broadcasted_iota(jnp.int32, (8, 1), 0)
    tile_rows = slice(TOP, TOP + ROWS)

    for copy in small:
        copy.wait()
    sea = OM[...].astype(jnp.float32)
    F[SEA, 8 : 8 + ROWS, :] = sea
    for i, copy in ((0, load_u), (1, load_v)):
        copy.wait()

        def level(l, sums, i=i):
            weighted = remap[0, l] * F[LEV * (i + 1) + l, 8 : 8 + ROWS, :]
            return sums[0] + weighted, sums[1] + viscosity[l] * weighted

        zero = jnp.zeros((ROWS, COLS), jnp.float32)
        base, spread = lax.fori_loop(0, LEV, level, (zero, zero), unroll=4)
        X[5 + i, tile_rows, 0:COLS] = base
        F[SEA + 1 + i, 8 : 8 + ROWS, :] = spread

    load_t.wait()
    row_n = send(F.at[:, 87:88, :], F.at[:, 7:8, :], edge_send.at[2], edge_recv.at[2], at(me, gy + 1))
    row_s = send(F.at[:, 8:9, :], F.at[:, 88:89, :], edge_send.at[3], edge_recv.at[3], at(me, gy - 1))
    row_f = send(F.at[:, 87:88, :], F.at[:, 88:89, :], edge_send.at[4], edge_recv.at[4], at(mirror, gy))

    @pl.when(has_north)
    def _():
        row_n.start()

    @pl.when(has_south)
    def _():
        row_s.start()

    @pl.when(is_top)
    def _():
        row_f.start()

    def pack(f, packed):
        return jnp.where((lane >> 1) == f, pltpu.roll(F[f, 8 : 8 + ROWS, :], 2 * f + 1, 1), packed)

    packed = lax.fori_loop(0, PLANES, pack, jnp.zeros((ROWS, COLS), jnp.float32), unroll=3)
    even = (lane & 1) == 0
    CE[...] = jnp.where(even, packed[0:HALF], pltpu.roll(packed[HALF:ROWS], 1, 1))
    CW[...] = jnp.where(even, pltpu.roll(packed[HALF:ROWS], COLS - 1, 1), packed[0:HALF])
    col_to_e = send(CE, RW, edge_send.at[0], edge_recv.at[0], at(east, gy))
    col_to_w = send(CW, RE, edge_send.at[1], edge_recv.at[1], at(west, gy))
    col_to_e.start()
    col_to_w.start()

    lane2 = lax.broadcasted_iota(jnp.int32, (LEV, LEV * LEV), 1)
    weights = jnp.zeros((LEV, LEV * LEV), jnp.float32)
    for l in range(LEV):
        weights = jnp.where((lane2 >> 4) == l, remap_wide[:, l : l + 1], weights)
    high = weights.astype(jnp.bfloat16).astype(jnp.float32)
    low = weights - high
    diagonal = (lane2 & 15) == lax.broadcasted_iota(jnp.int32, (LEV, LEV * LEV), 0)
    for k in range(LEV):
        rows = slice(LEV * k, LEV * (k + 1))
        high_k = jnp.where(diagonal, high[k : k + 1], 0.0).astype(jnp.bfloat16)
        KK[rows, 0:256] = high_k
        KK[rows, 256:512] = jnp.where(diagonal, low[k : k + 1], 0.0).astype(jnp.bfloat16)
        KK[rows, 512:768] = high_k

    col_to_e.wait()
    col_to_w.wait()

    @pl.when(has_north)
    def _():
        row_n.wait_send()
        row_s.wait_recv()

    @pl.when(has_south)
    def _():
        row_s.wait_send()
        row_n.wait_recv()


    @pl.when(is_top)
    def _():
        row_f.wait()
        inside = jnp.broadcast_to(fold_partner[...] - COLS * mirror, (8, COLS))

        for f in range(SEA, PLANES):
            taken = jnp.take_along_axis(F[f, 88:96, :], inside, axis=1, mode="promise_in_bounds")
            F[f, 88:96, :] = taken if f == SEA else -taken

    GE[0:HALF] = jnp.where(even, pltpu.roll(RE[...], COLS - 1, 1), pltpu.roll(RW[...], 1, 1))
    GE[HALF:ROWS] = jnp.where(even, RE[...], RW[...])

    def plane_sides(f):
        value = F[f, 8 : 8 + ROWS, :]
        edges = pltpu.roll(GE[...], COLS - 1 - 2 * f, 1)
        to_east = jnp.where(lane == COLS - 1, edges, pltpu.roll(value, COLS - 1, 1))
        to_west = jnp.where(lane == 0, edges, pltpu.roll(value, 1, 1))
        return value, to_east, to_west, F[f, 9 : 9 + ROWS, :], F[f, 7 : 7 + ROWS, :]

    seas = plane_sides(SEA)
    degree = jnp.zeros((ROWS, COLS), jnp.float32)
    for i in range(4):
        weight = seas[0] * seas[i + 1]
        MK[i] = weight
        degree = degree + weight
    MK[4] = degree

    def lap(f):
        value, to_east, to_west, to_north, to_south = plane_sides(f)
        total = MK[0] * to_east + MK[1] * to_west + MK[2] * to_north + MK[3] * to_south
        return value, total - MK[4] * value

    for i in range(2):
        X[5 + i, tile_rows, 0:COLS] = X[5 + i, tile_rows, 0:COLS] + lap(SEA + 1 + i)[1]

    for i in range(5):
        ice_local[i].wait()
        ice_away[i].wait_recv()
    X[4, tile_rows, 0:COLS] = IM[...].astype(jnp.float32)


    def rim_pack(f, packed):
        south_half, north_half = X[f, TOP : TOP + HALF, 0:COLS], X[f, TOP + HALF : TOP + ROWS, 0:COLS]
        group = lane >> 3
        new = []
        for edge, old in ((8, packed[0]), (0, packed[1])):
            kept = jnp.where(group == f, pltpu.roll(south_half, 8 * f + edge, 1), old)
            new.append(jnp.where(group == f + 8, pltpu.roll(north_half, 64 + 8 * f + edge, 1), kept))
        return tuple(new)

    zero = jnp.zeros((HALF, COLS), jnp.float32)
    pack_e, pack_w = lax.fori_loop(0, NF, rim_pack, (zero, zero), unroll=7)
    PE[...] = pack_e
    PW[...] = pack_w
    to_e = send(PE, WB, rim_send.at[0], rim_recv.at[0], at(east, gy))
    to_w = send(PW, EB, rim_send.at[1], rim_recv.at[1], at(west, gy))
    to_n = [
        send(X.at[:, last8, 0:COLS], X.at[:, south8, 0:COLS], rim_send.at[2], rim_recv.at[2], at(me, gy + 1)),
        send(PE.at[HALF - 8 : HALF], WBS, rim_send.at[3], rim_recv.at[3], at(east, gy + 1)),
        send(PW.at[HALF - 8 : HALF], EBS, rim_send.at[4], rim_recv.at[4], at(west, gy + 1)),
    ]
    to_s = [
        send(X.at[:, first8, 0:COLS], X.at[:, north8, 0:COLS], rim_send.at[5], rim_recv.at[5], at(me, gy - 1)),
        send(PE.at[0:8], WBN, rim_send.at[6], rim_recv.at[6], at(east, gy - 1)),
        send(PW.at[0:8], EBN, rim_send.at[7], rim_recv.at[7], at(west, gy - 1)),
    ]

    def strip_ends(src, dst, slot, rows):
        kept = slice(8 - rows, 8)
        return src.at[:, kept, :], dst.at[:, kept, COLS * slot : COLS * (slot + 1)]

    def strip_copy(again, slot, block, rows):
        src, dst = strip_ends(SS2, S2, slot, rows) if again else strip_ends(SS, S, slot, rows)
        sent, received = (again_send, again_recv) if again else (strip_send, strip_recv)
        return send(src, dst, sent.at[slot], received.at[slot], at(block, gy))

    def strips_start(again):
        for slot, block, own, rows in strips:
            if own:

                @pl.when(block != me)
                def _(slot=slot, block=block, rows=rows):
                    strip_copy(again, slot, block, rows).start()

                @pl.when(block == me)
                def _(slot=slot, rows=rows):
                    src, dst = strip_ends(SS2, S2, slot, rows) if again else strip_ends(SS, S, slot, rows)
                    pltpu.make_async_copy(src, dst, (again_recv if again else strip_recv).at[slot]).start()
            else:
                strip_copy(again, slot, block, rows).start()

    def strips_arrive(again):
        for slot, block, own, rows in strips:
            strip_copy(again, slot, block, rows).wait_recv()

    def strips_sent(again):
        for slot, block, own, rows in strips:
            if own:

                @pl.when(block != me)
                def _(slot=slot, block=block, rows=rows):
                    strip_copy(again, slot, block, rows).wait_send()
            else:
                strip_copy(again, slot, block, rows).wait_send()

    middle = slice(COLS * REACH, COLS * (REACH + 1))

    to_e.start()
    to_w.start()

    @pl.when(has_north)
    def _():
        for copy in to_n:
            copy.start()

    @pl.when(has_south)
    def _():
        for copy in to_s:
            copy.start()

    @pl.when(is_top)
    def _():
        SS[0:NF] = X[0:NF, last8, 0:COLS]
        inside = fold_partner[...] - COLS * mirror
        SS[NF] = jnp.broadcast_to(inside.astype(jnp.float32), (8, COLS))
        S[:, :, middle] = SS[...]
        strips_start(False)

    def diffuse(f, carry):
        coefficient = jnp.where(f < LEV, diffusivity[f & (LEV - 1)], viscosity[f & (LEV - 1)])
        value, spread = lap(f)
        new = value + coefficient * spread
        high = new.astype(jnp.bfloat16)
        DH[f] = high
        DL[f] = (new - high.astype(jnp.float32)).astype(jnp.bfloat16)
        return carry

    @pl.when(is_top)
    def _():
        inside = jnp.broadcast_to(fold_partner[...] - COLS * mirror, (8, COLS))

        def fold_edge(f, carry):
            taken = jnp.take_along_axis(F[f, 88:96, :], inside, axis=1, mode="promise_in_bounds")
            F[f, 88:96, :] = jnp.where(f < LEV, taken, -taken)
            return carry

        lax.fori_loop(0, 3 * LEV, fold_edge, 0, unroll=8)

    lax.fori_loop(0, 3 * LEV, diffuse, 0, unroll=4)

    to_e.wait()
    to_w.wait()

    @pl.when(has_north)
    def _():
        for copy in to_n:
            copy.wait_send()
        for copy in to_s:
            copy.wait_recv()

    @pl.when(has_south)
    def _():
        for copy in to_s:
            copy.wait_send()
        for copy in to_n:
            copy.wait_recv()

    def rim_unpack(f, carry):
        def put(rows, e, w, half):
            from_e = pltpu.roll(e, lax.rem(COLS + half - 8 * f, COLS), 1)
            from_w = pltpu.roll(w, lax.rem(2 * COLS - 8 + half - 8 * f, COLS), 1)
            X[f, rows, COLS : 2 * COLS] = jnp.where(
                lane < 8, from_e, jnp.where(lane >= COLS - 8, from_w, 0.0)
            )

        put(slice(TOP, TOP + HALF), EB[...], WB[...], 0)
        put(slice(TOP + HALF, TOP + ROWS), EB[...], WB[...], 64)
        put(slice(TOP - 8, TOP), EBS[...], WBS[...], 64)
        put(slice(TOP + ROWS, TOP + ROWS + 8), EBN[...], WBN[...], 0)
        return carry

    lax.fori_loop(0, NF, rim_unpack, 0, unroll=7)

    def inside_of(i):
        return IDX[:, COLS * i : COLS * (i + 1)]

    def fold_block(ref, f, i, sign):
        j = BLOCKS - 1 - i
        value = ref[f, :, COLS * j : COLS * (j + 1)]
        taken = jnp.take_along_axis(value, inside_of(i), axis=1, mode="promise_in_bounds")
        return taken if sign > 0 else -taken

    def close_top(ref, f, strip_ref, sf, sign):
        own = fold_block(strip_ref, sf, REACH, sign)
        to_the_e = fold_block(strip_ref, sf, REACH + 1, sign)
        to_the_w = fold_block(strip_ref, sf, REACH - 1, sign)
        ref[f, 24:25, 0:COLS] = own[7:8]
        ref[f, 24:25, COLS : 2 * COLS] = jnp.where(lane < COLS // 2, to_the_e, to_the_w)[7:8]

    def window(first, reach):
        middle = first + REACH
        low, high = middle - reach, middle + reach + 1
        wide_low, wide_high = max(low - 1, first), min(high + 1, first + SIDE)
        return low, high, wide_low, wide_high

    def strip_sides(ref, f, win, sign):
        low, high, wide_low, wide_high = win
        wide = ref[f, :, COLS * wide_low : COLS * wide_high]
        length = COLS * (wide_high - wide_low)
        cut = slice(COLS * (low - wide_low), COLS * (high - wide_low))
        value = wide[:, cut]
        to_east = pltpu.roll(wide, length - 1, 1)[:, cut]
        to_west = pltpu.roll(wide, 1, 1)[:, cut]
        folded = jnp.concatenate([fold_block(ref, f, i, sign) for i in range(low, high)], axis=1)
        to_north = jnp.where(row8 == 7, folded, pltpu.roll(value, 7, 0))
        to_south = pltpu.roll(value, 1, 0)
        return value, to_east, to_west, to_north, to_south

    def windows(left):
        found = []
        if left in OWN_REACH:
            found.append(window(0, OWN_REACH[left]))
        if left in MIRROR_REACH:
            found.append(window(SIDE, MIRROR_REACH[left]))
        return found

    SHARE = STEP_SIZE / (1.0 + STEP_SIZE)
    KEEP = 1.0 / (1.0 + STEP_SIZE)

    def ready(ref, rows, cols):
        present = ref[4, rows, cols]
        ref[5, rows, cols] = SHARE * present * ref[5, rows, cols]
        ref[6, rows, cols] = SHARE * present * ref[6, rows, cols]
        mass = ref[2, rows, cols]
        ref[2, rows, cols] = 0.5 * SHARE * present / jnp.where(mass > 0.0, mass, 1.0)
        ref[4, rows, cols] = KEEP * present
        ref[3, rows, cols] = ref[3, rows, cols] * (RELAX / (1.0 + RELAX))

    def main_sides(ref, f, start, size):
        value = ref[f, start : start + size, :]
        return (
            value,
            pltpu.roll(value, 2 * COLS - 1, 1),
            pltpu.roll(value, 1, 1),
            ref[f, start + 1 : start + size + 1, :],
            ref[f, start - 1 : start + size - 1, :],
        )

    CHUNK = 24
    chunks = range(8, 8 + SPAN, CHUNK)

    def stress(u, v, third, old):
        twice_d = (u[1] - u[2]) + (v[3] - v[4])
        twice_h = (u[3] - u[4]) + (v[1] - v[2])
        viscous = third * lax.rsqrt(twice_d * twice_d + 0.25 * (twice_h * twice_h) + 0.04)
        a = viscous * twice_d - third
        b = viscous * twice_h
        if old is not None:
            a = a + old[0] * (1.0 / (1.0 + RELAX))
            b = b + old[1] * (1.0 / (1.0 + RELAX))
        return a, b

    def push(ref, vel, rows, cols, a, b):
        keep, mobility = ref[4, rows, cols], ref[2, rows, cols]
        new_u = keep * vel[0, rows, cols] + mobility * ((a[1] - a[2]) + (b[3] - b[4])) + ref[5, rows, cols]
        new_v = keep * vel[1, rows, cols] + mobility * ((b[1] - b[2]) + (a[3] - a[4])) + ref[6, rows, cols]
        vel[0, rows, cols] = new_u
        vel[1, rows, cols] = new_v

    every = slice(0, 8)

    def chunk_stress(vel, sig, start, first=False):
        rows = slice(start, start + CHUNK)
        u, v = main_sides(vel, 0, start, CHUNK), main_sides(vel, 1, start, CHUNK)
        old = None if first else (sig[0, rows, :], sig[1, rows, :])
        sig[0, rows, :], sig[1, rows, :] = stress(u, v, vel[3, rows, :], old)

    def chunk_push(vel, sig, start):
        a, b = main_sides(sig, 0, start, CHUNK), main_sides(sig, 1, start, CHUNK)
        push(vel, vel, slice(start, start + CHUNK), slice(0, 2 * COLS), a, b)

    def tile_cycle(cycle, carry):
        for start in chunks:
            chunk_stress(X, AB, start)
        for start in chunks:
            chunk_push(X, AB, start)
        return carry

    low_piece, high_piece, low_tile, high_tile = slice(8, 16), slice(16, 24), slice(80, 88), slice(88, 96)

    def top_cycles(cycles):
        vel, sig, i_a, i_b = (S, SAB, 0, 1) if cycles[0] == 0 else (S2, S2, 2, 3)
        for cycle in cycles:
            left = 3 if cycle == cycles[0] else 1
            close_top(XT, 0, vel, 0, -1)
            close_top(XT, 1, vel, 1, -1)
            for win in windows(left):
                cols = slice(COLS * win[0], COLS * win[1])
                u, v = strip_sides(vel, 0, win, -1), strip_sides(vel, 1, win, -1)
                old = (sig[i_a, :, cols], sig[i_b, :, cols]) if cycle else None
                sig[i_a, :, cols], sig[i_b, :, cols] = stress(u, v, S[3, :, cols], old)
            chunk_stress(XT, ABT, 8, cycle == 0)
            close_top(ABT, 0, sig, i_a, 1)
            close_top(ABT, 1, sig, i_b, 1)
            for win in windows(left - 1):
                cols = slice(COLS * win[0], COLS * win[1])
                push(S, vel, every, cols, strip_sides(sig, i_a, win, 1), strip_sides(sig, i_b, win, 1))
            chunk_push(XT, ABT, 8)

    for start in chunks:
        ready(X, slice(start, start + CHUNK), slice(0, 2 * COLS))

    @pl.when(is_top)
    def _():
        XT[...] = X[:, 72:112, :]
        ABT[...] = jnp.zeros((2, 40, 2 * COLS), jnp.float32)

    lax.fori_loop(0, 2, tile_cycle, 0)

    @pl.when(is_top)
    def _():
        strips_arrive(False)
        IDX[...] = jnp.broadcast_to(S[NF, 7:8, :], IDX.shape).astype(jnp.int32)
        ready(S, every, slice(0, BLOCKS * COLS))
        top_cycles((0, 1))
        SS2[0:2] = XT[0:2, high_piece, 0:COLS]
        SS2[2:4] = ABT[:, high_piece, 0:COLS]
        strips_start(True)
        S2[:, :, middle] = SS2[...]
        X[0:2, high_tile, :] = XT[0:2, high_piece, :]
        AB[:, high_tile, :] = ABT[:, high_piece, :]
        XT[0:2, low_piece, :] = X[0:2, low_tile, :]
        ABT[:, low_piece, :] = AB[:, low_tile, :]

    lax.fori_loop(0, 2, tile_cycle, 0)

    away = pl.ds(pl.multiple_of(TOP + HALF * (1 - comp), 8), HALF)
    here = pl.ds(pl.multiple_of(TOP + HALF * comp, 8), HALF)
    ice_out = (new_ice_u, new_ice_v)
    vel_away = [
        send(X.at[i, away, 0:COLS], ice_out[i].at[:, mine], vel_send.at[i], vel_recv.at[i], partner) for i in range(2)
    ]
    vel_here = [
        pltpu.make_async_copy(X.at[i, here, 0:COLS], ice_out[i].at[:, mine], out_sem.at[3 + i]) for i in range(2)
    ]

    @pl.when(jnp.logical_not(is_top))
    def _():
        for copy in vel_away + vel_here:
            copy.start()

    def regrid(g):
        planes = pl.ds(g * LEV, LEV)
        pieces = range(0, ROWS, LEV)
        high = jnp.concatenate([DH[planes, r : r + LEV, :].reshape(LEV * LEV, COLS) for r in pieces], axis=1)
        low = jnp.concatenate([DL[planes, r : r + LEV, :].reshape(LEV * LEV, COLS) for r in pieces], axis=1)
        new = jnp.dot(KK[...], jnp.concatenate([high, high, low], axis=0), preferred_element_type=jnp.float32)
        for i, r in enumerate(pieces):
            O[planes, r : r + LEV, :] = new[:, COLS * i : COLS * (i + 1)].reshape(LEV, LEV, COLS)

    @pl.when(is_top)
    def _():
        def early(g, carry):
            regrid(g)
            return carry

        lax.fori_loop(0, 2, early, 0)
        strips_arrive(True)
        to_the_e = S2[0:2, 7:8, COLS * (REACH + 1) : COLS * (REACH + 2)]
        to_the_w = S2[0:2, 7:8, COLS * (REACH - 1) : COLS * REACH]
        XT[0:2, 23:24, COLS : 2 * COLS] = jnp.where(lane < COLS // 2, to_the_e, to_the_w)
        top_cycles((2, 3))
        X[0:2, high_tile, :] = XT[0:2, high_piece, :]
        for copy in vel_away + vel_here:
            copy.start()

    outs = (new_tracer, new_ocean_u, new_ocean_v)

    stores = [
        pltpu.make_async_copy(O.at[g * LEV : (g + 1) * LEV], outs[g], out_sem.at[g]) for g in range(3)
    ]

    def finish(g, carry):
        @pl.when(jnp.logical_not(is_top) | (g == 2))
        def _():
            regrid(g)

        for i in range(3):

            @pl.when(g == i)
            def _(i=i):
                if i:
                    tau = X[i - 1, tile_rows, 0:COLS] - X[4 + i, tile_rows, 0:COLS] * (1.0 / SHARE)
                    O[i * LEV] = O[i * LEV] + COUPLE * (F[SEA, 8 : 8 + ROWS, :] * tau)
                stores[i].start()

        return carry

    lax.fori_loop(0, 3, finish, 0)

    @pl.when(is_top)
    def _():
        strips_sent(False)
        strips_sent(True)

    for copy in ice_away:
        copy.wait_send()
    for copy in vel_away:
        copy.wait()
    for copy in vel_here + stores:
        copy.wait()


def deliver(*refs):
    count = len(refs) // 2
    sems = refs[-1]
    copies = [pltpu.make_async_copy(refs[i], refs[count + i], sems.at[i]) for i in range(count)]
    for copy in copies:
        copy.start()
    for copy in copies:
        copy.wait()


def solution(mesh):
    blocks = mesh.shape["gx"] * 2
    gys = mesh.shape["gy"]
    ocean = P(None, "gy", ("gx", "comp"))
    flat = P("gy", ("gx", "comp"))
    ice = P(("gy", "comp"), "gx")
    in_specs = (ocean, ocean, ocean, flat, P(), P(), P(), P(("gx", "comp")), ice, ice, ice, ice, ice)
    out_specs = (ocean, ocean, ocean, ice, ice)

    def body(tracer, ocean_u, ocean_v, ocean_mask, diffusivity, viscosity, remap, fold_partner, *ice_fields):
        f32 = jnp.float32
        anywhere = pl.BlockSpec(memory_space=pl.ANY)
        main_memory = pl.BlockSpec(memory_space=pltpu.HBM)
        vmem = pltpu.VMEM
        dma = pltpu.SemaphoreType.DMA
        ocean_shape = jax.ShapeDtypeStruct(tracer.shape, f32)
        ice_shape = jax.ShapeDtypeStruct(ice_fields[0].shape, f32)

        def step(*args):
            kernel(blocks, gys, *args)

        shapes = (ocean_shape, ocean_shape, ocean_shape, ice_shape, ice_shape)
        results = pl.pallas_call(
            step,
            out_shape=shapes,
            in_specs=[main_memory] * 13,
            out_specs=(anywhere,) * 5,
            scratch_shapes=[
                vmem((PLANES, 96, COLS), f32),
                vmem((3 * LEV, ROWS, COLS), jnp.bfloat16),
                vmem((3 * LEV, ROWS, COLS), jnp.bfloat16),
                vmem((LEV * LEV, 3 * LEV * LEV), jnp.bfloat16),
                vmem((3 * LEV, ROWS, COLS), f32),
                vmem((NF, 112, 2 * COLS), f32),
                vmem((2, 112, 2 * COLS), f32),
                vmem((NF, 40, 2 * COLS), f32),
                vmem((2, 40, 2 * COLS), f32),
                vmem((NS, 8, BLOCKS * COLS), f32),
                vmem((2, 8, BLOCKS * COLS), f32),
                vmem((NS, 8, COLS), f32),
                vmem((4, 8, BLOCKS * COLS), f32),
                vmem((4, 8, COLS), f32),
                vmem((HALF, COLS), f32),
                vmem((HALF, COLS), f32),
                vmem((HALF, COLS), f32),
                vmem((HALF, COLS), f32),
                vmem((8, COLS), f32),
                vmem((8, COLS), f32),
                vmem((8, COLS), f32),
                vmem((8, COLS), f32),
                vmem((HALF, COLS), f32),
                vmem((HALF, COLS), f32),
                vmem((HALF, COLS), f32),
                vmem((HALF, COLS), f32),
                vmem((ROWS, COLS), f32),
                vmem((5, ROWS, COLS), f32),
                vmem((ROWS, COLS), jnp.int32),
                vmem((ROWS, COLS), jnp.int32),
                vmem((8, BLOCKS * COLS), jnp.int32),
                pltpu.SMEM((LEV,), f32),
                pltpu.SMEM((LEV,), f32),
                pltpu.SMEM((LEV, LEV), f32),
                vmem((LEV, LEV), f32),
                vmem((1, COLS), jnp.int32),
                dma((9,)),
                dma((5,)),
                dma((5,)),
                dma((5,)),
                dma((5,)),
                dma((5,)),
                dma((8,)),
                dma((8,)),
                dma((BLOCKS,)),
                dma((BLOCKS,)),
                dma((BLOCKS,)),
                dma((BLOCKS,)),
                dma((5,)),
                dma((2,)),
                dma((2,)),
            ],
            compiler_params=pltpu.CompilerParams(
                collective_id=0, has_side_effects=True, vmem_limit_bytes=32 * 1024 * 1024
            ),
        )(
            *[
                pltpu.with_memory_space_constraint(value, pltpu.HBM)
                for value in (
                    tracer,
                    ocean_u,
                    ocean_v,
                    ocean_mask,
                    diffusivity,
                    viscosity,
                    remap,
                    fold_partner.reshape(1, COLS),
                    *ice_fields,
                )
            ]
        )
        return pl.pallas_call(
            deliver,
            out_shape=shapes,
            in_specs=[anywhere] * 5,
            out_specs=(main_memory,) * 5,
            scratch_shapes=[dma((5,))],
            compiler_params=pltpu.CompilerParams(vmem_limit_bytes=1024 * 1024),
        )(*results)

    return jax.shard_map(body, mesh=mesh, in_specs=in_specs, out_specs=out_specs, check_vma=False)
```

```python
import jax
import jax.numpy as jnp
from jax import lax
from jax.experimental import pallas as pl
from jax.experimental.pallas import tpu as pltpu
from jax.sharding import PartitionSpec as P

ITERS = 4
RELAX = 0.5
STEP_SIZE = 0.3
COUPLE = 0.5
MESH = pl.DeviceIdType.MESH

LEV = 16
ROWS = 80
HALF = 40
COLS = 128
NF = 7
NS = NF + 1
REACH = 2
SIDE = 2 * REACH + 1
BLOCKS = 2 * SIDE
TOP = 16
SPAN = 96
OWN_REACH = {2: 0, 3: 1}
MIRROR_REACH = {1: 0, 2: 1, 3: 2}
OWN_ROWS = (8, 2, 1)
MIRROR_ROWS = (4, 3, 2)
SEA = 3 * LEV
PLANES = SEA + 3


quarters = [slice(4 * i, 4 * i + 4) for i in range(LEV // 4)]


def kernel(
    blocks,
    gys,
    tracer,
    ocean_u,
    ocean_v,
    ocean_mask,
    diffusivity_in,
    viscosity_in,
    remap_in,
    fold_in,
    ice_u,
    ice_v,
    ice_mass,
    ice_strength,
    ice_mask,
    new_tracer,
    new_ocean_u,
    new_ocean_v,
    new_ice_u,
    new_ice_v,
    F,
    DH,
    DL,
    KK,
    O,
    X,
    AB,
    XT,
    ABT,
    S,
    SAB,
    SS,
    S2,
    SS2,
    PE,
    PW,
    EB,
    WB,
    EBS,
    WBS,
    EBN,
    WBN,
    TR,
    BR,
    NR,
    SR,
    CK,
    RKE,
    RKW,
    GK,
    TK,
    BK,
    NK,
    SK,
    CE,
    CW,
    RE,
    RW,
    GE,
    MK,
    OM,
    IM,
    IDX,
    diffusivity,
    viscosity,
    remap,
    remap_wide,
    fold_partner,
    in_sem,
    ice_sem,
    ice_send,
    ice_recv,
    edge_send,
    edge_recv,
    first_send,
    first_recv,
    rim_send,
    rim_recv,
    strip_send,
    strip_recv,
    again_send,
    again_recv,
    out_sem,
    vel_send,
    vel_recv,
):
    gx, gy, comp = lax.axis_index("gx"), lax.axis_index("gy"), lax.axis_index("comp")
    me = gx * 2 + comp
    has_north = gy < gys - 1
    has_south = gy > 0
    is_top = gy == gys - 1

    def at(block, row):
        return {"gx": block // 2, "gy": row, "comp": lax.rem(block, 2)}

    def wrap(block):
        return lax.rem(block + 2 * blocks, blocks)

    east, west, mirror = wrap(me + 1), wrap(me - 1), blocks - 1 - me
    partner = at(gx * 2 + 1 - comp, gy)

    strips = [(SIDE + REACH, mirror, False, MIRROR_ROWS[0])]
    for d in (1, -1, 2, -2):
        strips.append((SIDE + REACH + d, wrap(mirror + d), d % 2 == 1, MIRROR_ROWS[abs(d)]))
        strips.append((REACH + d, wrap(me - d), False, OWN_ROWS[abs(d)]))

    def load(src, dst, sem):
        copy = pltpu.make_async_copy(src, dst, sem)
        copy.start()
        return copy

    def load_planes(src, g, sem):
        for q in quarters:
            load(src.at[q], F.at[g * LEV + q.start : g * LEV + q.stop, 8 : 8 + ROWS, :], sem)
        return pltpu.make_async_copy(src, F.at[g * LEV : (g + 1) * LEV, 8 : 8 + ROWS, :], sem)

    load_u = load_planes(ocean_u, 1, in_sem.at[0])
    load_v = load_planes(ocean_v, 2, in_sem.at[1])
    small = [
        load(ocean_mask, OM, in_sem.at[2]),
        load(remap_in, remap, in_sem.at[4]),
        load(diffusivity_in, diffusivity, in_sem.at[5]),
        load(viscosity_in, viscosity, in_sem.at[6]),
        load(fold_in, fold_partner, in_sem.at[7]),
        load(remap_in, remap_wide, in_sem.at[8]),
    ]
    barrier = pltpu.get_barrier_semaphore()

    def greet(target):
        pl.semaphore_signal(barrier, inc=1, device_id=target, device_id_type=MESH)

    greet(at(east, gy))
    greet(at(west, gy))

    @pl.when(has_north)
    def _():
        for block in (me, east, west):
            greet(at(block, gy + 1))

    @pl.when(has_south)
    def _():
        for block in (me, east, west):
            greet(at(block, gy - 1))

    @pl.when(is_top)
    def _():
        for _, block, own, _ in strips:
            if own:

                @pl.when(block != me)
                def _(block=block):
                    greet(at(block, gy))
            else:
                greet(at(block, gy))

    ice_in = (ice_u, ice_v, ice_mass, ice_strength, ice_mask)

    def ice_place(i, half):
        rows = pl.ds(pl.multiple_of(TOP + HALF * half, 8), HALF)
        if i == 4:
            return IM.at[pl.ds(pl.multiple_of(HALF * half, 8), HALF), :]
        return X.at[i, rows, 0:COLS]

    mine = pl.ds(pl.multiple_of(COLS * comp, COLS), COLS)
    other = pl.ds(pl.multiple_of(COLS * (1 - comp), COLS), COLS)
    ice_local = [load(ice_in[i].at[:, mine], ice_place(i, comp), ice_sem.at[i]) for i in range(5)]

    first8, last8 = slice(TOP, TOP + 8), slice(TOP + ROWS - 8, TOP + ROWS)
    south8, north8 = slice(TOP - 8, TOP), slice(TOP + ROWS, TOP + ROWS + 8)

    @pl.when(jnp.logical_not(has_south))
    def _():
        X[:, south8, 0:COLS] = jnp.zeros((NF, 8, COLS), jnp.float32)
        EBS[...] = jnp.zeros((8, COLS), jnp.float32)
        WBS[...] = jnp.zeros((8, COLS), jnp.float32)
        SR[...] = jnp.zeros((3 * LEV, COLS), jnp.float32)
        SK[...] = jnp.zeros((8, COLS), jnp.float32)

    @pl.when(is_top)
    def _():
        X[:, north8, 0:COLS] = jnp.zeros((NF, 8, COLS), jnp.float32)
        EBN[...] = jnp.zeros((8, COLS), jnp.float32)
        WBN[...] = jnp.zeros((8, COLS), jnp.float32)

    outer = jnp.zeros((NF, 8, 2 * COLS), jnp.float32)
    X[:, 0:8, :] = outer
    X[:, 104:112, :] = outer
    AB[...] = jnp.zeros((2, 112, 2 * COLS), jnp.float32)

    count = 2 + 3 * has_north.astype(jnp.int32) + 3 * has_south.astype(jnp.int32)
    strip_count = 0
    for _, block, own, _ in strips:
        strip_count = strip_count + ((block != me).astype(jnp.int32) if own else 1)
    count = count + is_top.astype(jnp.int32) * strip_count
    pl.semaphore_wait(barrier, count)

    def send(src, dst, send_sem, recv_sem, target):
        copy = pltpu.make_async_remote_copy(
            src_ref=src,
            dst_ref=dst,
            send_sem=send_sem,
            recv_sem=recv_sem,
            device_id=target,
            device_id_type=MESH,
        )
        return copy

    ice_away = []
    for i in range(5):
        copy = send(
            ice_in[i].at[:, other], ice_place(i, comp), ice_send.at[i], ice_recv.at[i], partner
        )
        copy.start()
        ice_away.append(copy)

    load_t = load_planes(tracer, 0, in_sem.at[3])
    lane = lax.broadcasted_iota(jnp.int32, (1, COLS), 1)
    even = (lane & 1) == 0
    row8 = lax.broadcasted_iota(jnp.int32, (8, 1), 0)
    tile_rows = slice(TOP, TOP + ROWS)

    for copy in small:
        copy.wait()
    sea = OM[...].astype(jnp.float32)
    F[SEA, 8 : 8 + ROWS, :] = sea
    for i, copy in ((0, load_u), (1, load_v)):
        copy.wait()

        def level(l, sums, i=i):
            weighted = remap[0, l] * F[LEV * (i + 1) + l, 8 : 8 + ROWS, :]
            return sums[0] + weighted, sums[1] + viscosity[l] * weighted

        zero = jnp.zeros((ROWS, COLS), jnp.float32)
        base, spread = lax.fori_loop(0, LEV, level, (zero, zero), unroll=4)
        X[5 + i, tile_rows, 0:COLS] = base
        F[SEA + 1 + i, 8 : 8 + ROWS, :] = spread

    first = [(3 * t + p, SEA + p, slice(8 + 8 * t, 16 + 8 * t)) for t in range(ROWS // 8) for p in range(3)]
    packed = jnp.zeros((8, COLS), jnp.float32)
    for m, f, rows in first:
        packed = jnp.where((lane >> 1) == m, pltpu.roll(F[f, rows, :], 2 * m + 1, 1), packed)
    CK[...] = packed
    for p in range(3):
        TK[p : p + 1, :] = F[SEA + p, 87:88, :]
        BK[p : p + 1, :] = F[SEA + p, 8:9, :]
    first_e = send(CK, RKW, first_send.at[0], first_recv.at[0], at(east, gy))
    first_w = send(CK, RKE, first_send.at[1], first_recv.at[1], at(west, gy))
    first_n = send(TK, SK, first_send.at[2], first_recv.at[2], at(me, gy + 1))
    first_s = send(BK, NK, first_send.at[3], first_recv.at[3], at(me, gy - 1))
    first_f = send(TK, NK, first_send.at[4], first_recv.at[4], at(mirror, gy))
    first_e.start()
    first_w.start()

    @pl.when(has_north)
    def _():
        first_n.start()

    @pl.when(has_south)
    def _():
        first_s.start()

    @pl.when(is_top)
    def _():
        first_f.start()

    load_t.wait()
    for f in range(3 * LEV):
        TR[f : f + 1, :] = F[f, 87:88, :]
        BR[f : f + 1, :] = F[f, 8:9, :]
    row_n = send(TR, SR, edge_send.at[2], edge_recv.at[2], at(me, gy + 1))
    row_s = send(BR, NR, edge_send.at[3], edge_recv.at[3], at(me, gy - 1))
    row_f = send(TR, NR, edge_send.at[4], edge_recv.at[4], at(mirror, gy))

    @pl.when(has_north)
    def _():
        row_n.start()

    @pl.when(has_south)
    def _():
        row_s.start()

    @pl.when(is_top)
    def _():
        row_f.start()

    def pack(f, packed):
        return jnp.where((lane >> 1) == f, pltpu.roll(F[f, 8 : 8 + ROWS, :], 2 * f + 1, 1), packed)

    packed = lax.fori_loop(0, 3 * LEV, pack, jnp.zeros((ROWS, COLS), jnp.float32), unroll=3)
    CE[...] = jnp.where(even, packed[0:HALF], pltpu.roll(packed[HALF:ROWS], 1, 1))
    CW[...] = jnp.where(even, pltpu.roll(packed[HALF:ROWS], COLS - 1, 1), packed[0:HALF])
    col_to_e = send(CE, RW, edge_send.at[0], edge_recv.at[0], at(east, gy))
    col_to_w = send(CW, RE, edge_send.at[1], edge_recv.at[1], at(west, gy))
    col_to_e.start()
    col_to_w.start()

    lane2 = lax.broadcasted_iota(jnp.int32, (LEV, LEV * LEV), 1)
    weights = jnp.zeros((LEV, LEV * LEV), jnp.float32)
    for l in range(LEV):
        weights = jnp.where((lane2 >> 4) == l, remap_wide[:, l : l + 1], weights)
    high = weights.astype(jnp.bfloat16).astype(jnp.float32)
    low = weights - high
    diagonal = (lane2 & 15) == lax.broadcasted_iota(jnp.int32, (LEV, LEV * LEV), 0)
    for k in range(LEV):
        rows = slice(LEV * k, LEV * (k + 1))
        high_k = jnp.where(diagonal, high[k : k + 1], 0.0).astype(jnp.bfloat16)
        KK[rows, 0:256] = high_k
        KK[rows, 256:512] = jnp.where(diagonal, low[k : k + 1], 0.0).astype(jnp.bfloat16)
        KK[rows, 512:768] = high_k

    first_e.wait()
    first_w.wait()

    @pl.when(has_north)
    def _():
        first_n.wait_send()
        first_s.wait_recv()

    @pl.when(has_south)
    def _():
        first_s.wait_send()
        first_n.wait_recv()

    inside_here = fold_partner[...] - COLS * mirror

    @pl.when(is_top)
    def _():
        first_f.wait()
        inside = jnp.broadcast_to(inside_here, (8, COLS))
        taken = jnp.take_along_axis(NK[...], inside, axis=1, mode="promise_in_bounds")
        NK[...] = jnp.where(row8 == 0, taken, -taken)

    GK[...] = jnp.where(even, pltpu.roll(RKE[...], COLS - 1, 1), pltpu.roll(RKW[...], 1, 1))
    for p in range(3):
        F[SEA + p, 88:89, :] = NK[p : p + 1, :]
        F[SEA + p, 7:8, :] = SK[p : p + 1, :]

    def sides_of(f, edges):
        value = F[f, 8 : 8 + ROWS, :]
        to_east = jnp.where(lane == COLS - 1, edges, pltpu.roll(value, COLS - 1, 1))
        to_west = jnp.where(lane == 0, edges, pltpu.roll(value, 1, 1))
        return value, to_east, to_west, F[f, 9 : 9 + ROWS, :], F[f, 7 : 7 + ROWS, :]

    def first_edges(f):
        return jnp.concatenate([pltpu.roll(GK[...], COLS - 1 - 2 * m, 1) for m, g, _ in first if g == f], axis=0)

    def lap(f, edges):
        value, to_east, to_west, to_north, to_south = sides_of(f, edges)
        total = MK[0] * to_east + MK[1] * to_west + MK[2] * to_north + MK[3] * to_south
        return value, total - MK[4] * value

    seas = sides_of(SEA, first_edges(SEA))
    degree = jnp.zeros((ROWS, COLS), jnp.float32)
    for i in range(4):
        weight = seas[0] * seas[i + 1]
        MK[i] = weight
        degree = degree + weight
    MK[4] = degree
    for i in range(2):
        f = SEA + 1 + i
        X[5 + i, tile_rows, 0:COLS] = X[5 + i, tile_rows, 0:COLS] + lap(f, first_edges(f))[1]

    for i in range(5):
        ice_local[i].wait()
        ice_away[i].wait_recv()
    X[4, tile_rows, 0:COLS] = IM[...].astype(jnp.float32)


    def rim_pack(f, packed):
        south_half, north_half = X[f, TOP : TOP + HALF, 0:COLS], X[f, TOP + HALF : TOP + ROWS, 0:COLS]
        group = lane >> 3
        new = []
        for edge, old in ((8, packed[0]), (0, packed[1])):
            kept = jnp.where(group == f, pltpu.roll(south_half, 8 * f + edge, 1), old)
            new.append(jnp.where(group == f + 8, pltpu.roll(north_half, 64 + 8 * f + edge, 1), kept))
        return tuple(new)

    zero = jnp.zeros((HALF, COLS), jnp.float32)
    pack_e, pack_w = lax.fori_loop(0, NF, rim_pack, (zero, zero), unroll=7)
    PE[...] = pack_e
    PW[...] = pack_w
    to_e = send(PE, WB, rim_send.at[0], rim_recv.at[0], at(east, gy))
    to_w = send(PW, EB, rim_send.at[1], rim_recv.at[1], at(west, gy))
    to_n = [
        send(X.at[:, last8, 0:COLS], X.at[:, south8, 0:COLS], rim_send.at[2], rim_recv.at[2], at(me, gy + 1)),
        send(PE.at[HALF - 8 : HALF], WBS, rim_send.at[3], rim_recv.at[3], at(east, gy + 1)),
        send(PW.at[HALF - 8 : HALF], EBS, rim_send.at[4], rim_recv.at[4], at(west, gy + 1)),
    ]
    to_s = [
        send(X.at[:, first8, 0:COLS], X.at[:, north8, 0:COLS], rim_send.at[5], rim_recv.at[5], at(me, gy - 1)),
        send(PE.at[0:8], WBN, rim_send.at[6], rim_recv.at[6], at(east, gy - 1)),
        send(PW.at[0:8], EBN, rim_send.at[7], rim_recv.at[7], at(west, gy - 1)),
    ]

    def strip_ends(src, dst, slot, rows):
        kept = slice(8 - rows, 8)
        return src.at[:, kept, :], dst.at[:, kept, COLS * slot : COLS * (slot + 1)]

    def strip_copy(again, slot, block, rows):
        src, dst = strip_ends(SS2, S2, slot, rows) if again else strip_ends(SS, S, slot, rows)
        sent, received = (again_send, again_recv) if again else (strip_send, strip_recv)
        return send(src, dst, sent.at[slot], received.at[slot], at(block, gy))

    def strips_start(again):
        for slot, block, own, rows in strips:
            if own:

                @pl.when(block != me)
                def _(slot=slot, block=block, rows=rows):
                    strip_copy(again, slot, block, rows).start()

                @pl.when(block == me)
                def _(slot=slot, rows=rows):
                    src, dst = strip_ends(SS2, S2, slot, rows) if again else strip_ends(SS, S, slot, rows)
                    pltpu.make_async_copy(src, dst, (again_recv if again else strip_recv).at[slot]).start()
            else:
                strip_copy(again, slot, block, rows).start()

    def strips_arrive(again):
        for slot, block, own, rows in strips:
            strip_copy(again, slot, block, rows).wait_recv()

    def strips_sent(again):
        for slot, block, own, rows in strips:
            if own:

                @pl.when(block != me)
                def _(slot=slot, block=block, rows=rows):
                    strip_copy(again, slot, block, rows).wait_send()
            else:
                strip_copy(again, slot, block, rows).wait_send()

    middle = slice(COLS * REACH, COLS * (REACH + 1))

    to_e.start()
    to_w.start()

    @pl.when(has_north)
    def _():
        for copy in to_n:
            copy.start()

    @pl.when(has_south)
    def _():
        for copy in to_s:
            copy.start()

    @pl.when(is_top)
    def _():
        SS[0:NF] = X[0:NF, last8, 0:COLS]
        SS[NF] = jnp.broadcast_to(inside_here.astype(jnp.float32), (8, COLS))
        S[:, :, middle] = SS[...]
        strips_start(False)

    col_to_e.wait()
    col_to_w.wait()

    @pl.when(has_north)
    def _():
        row_n.wait_send()
        row_s.wait_recv()

    @pl.when(has_south)
    def _():
        row_s.wait_send()
        row_n.wait_recv()

    @pl.when(is_top)
    def _():
        row_f.wait()
        inside = jnp.broadcast_to(inside_here, (8, COLS))
        for r in range(0, 3 * LEV, 8):
            taken = jnp.take_along_axis(NR[r : r + 8, :], inside, axis=1, mode="promise_in_bounds")
            NR[r : r + 8, :] = taken if r < LEV else -taken

    for f in range(3 * LEV):
        F[f, 88:89, :] = NR[f : f + 1, :]
        F[f, 7:8, :] = SR[f : f + 1, :]
    GE[0:HALF] = jnp.where(even, pltpu.roll(RE[...], COLS - 1, 1), pltpu.roll(RW[...], 1, 1))
    GE[HALF:ROWS] = jnp.where(even, RE[...], RW[...])

    def diffuse(f, carry):
        coefficient = jnp.where(f < LEV, diffusivity[f & (LEV - 1)], viscosity[f & (LEV - 1)])
        value, spread = lap(f, pltpu.roll(GE[...], COLS - 1 - 2 * f, 1))
        new = value + coefficient * spread
        high = new.astype(jnp.bfloat16)
        DH[f] = high
        DL[f] = (new - high.astype(jnp.float32)).astype(jnp.bfloat16)
        return carry

    lax.fori_loop(0, 3 * LEV, diffuse, 0, unroll=4)

    to_e.wait()
    to_w.wait()

    @pl.when(has_north)
    def _():
        for copy in to_n:
            copy.wait_send()
        for copy in to_s:
            copy.wait_recv()

    @pl.when(has_south)
    def _():
        for copy in to_s:
            copy.wait_send()
        for copy in to_n:
            copy.wait_recv()

    def rim_unpack(f, carry):
        def put(rows, e, w, half):
            from_e = pltpu.roll(e, lax.rem(COLS + half - 8 * f, COLS), 1)
            from_w = pltpu.roll(w, lax.rem(2 * COLS - 8 + half - 8 * f, COLS), 1)
            X[f, rows, COLS : 2 * COLS] = jnp.where(
                lane < 8, from_e, jnp.where(lane >= COLS - 8, from_w, 0.0)
            )

        put(slice(TOP, TOP + HALF), EB[...], WB[...], 0)
        put(slice(TOP + HALF, TOP + ROWS), EB[...], WB[...], 64)
        put(slice(TOP - 8, TOP), EBS[...], WBS[...], 64)
        put(slice(TOP + ROWS, TOP + ROWS + 8), EBN[...], WBN[...], 0)
        return carry

    lax.fori_loop(0, NF, rim_unpack, 0, unroll=7)

    def inside_of(i):
        return IDX[:, COLS * i : COLS * (i + 1)]

    def fold_block(ref, f, i, sign):
        j = BLOCKS - 1 - i
        value = ref[f, :, COLS * j : COLS * (j + 1)]
        taken = jnp.take_along_axis(value, inside_of(i), axis=1, mode="promise_in_bounds")
        return taken if sign > 0 else -taken

    def close_top(ref, f, strip_ref, sf, sign):
        own = fold_block(strip_ref, sf, REACH, sign)
        to_the_e = fold_block(strip_ref, sf, REACH + 1, sign)
        to_the_w = fold_block(strip_ref, sf, REACH - 1, sign)
        ref[f, 24:25, 0:COLS] = own[7:8]
        ref[f, 24:25, COLS : 2 * COLS] = jnp.where(lane < COLS // 2, to_the_e, to_the_w)[7:8]

    def window(first, reach):
        middle = first + REACH
        low, high = middle - reach, middle + reach + 1
        wide_low, wide_high = max(low - 1, first), min(high + 1, first + SIDE)
        return low, high, wide_low, wide_high

    def strip_sides(ref, f, win, sign):
        low, high, wide_low, wide_high = win
        wide = ref[f, :, COLS * wide_low : COLS * wide_high]
        length = COLS * (wide_high - wide_low)
        cut = slice(COLS * (low - wide_low), COLS * (high - wide_low))
        value = wide[:, cut]
        to_east = pltpu.roll(wide, length - 1, 1)[:, cut]
        to_west = pltpu.roll(wide, 1, 1)[:, cut]
        folded = jnp.concatenate([fold_block(ref, f, i, sign) for i in range(low, high)], axis=1)
        to_north = jnp.where(row8 == 7, folded, pltpu.roll(value, 7, 0))
        to_south = pltpu.roll(value, 1, 0)
        return value, to_east, to_west, to_north, to_south

    def windows(left):
        found = []
        if left in OWN_REACH:
            found.append(window(0, OWN_REACH[left]))
        if left in MIRROR_REACH:
            found.append(window(SIDE, MIRROR_REACH[left]))
        return found

    SHARE = STEP_SIZE / (1.0 + STEP_SIZE)
    KEEP = 1.0 / (1.0 + STEP_SIZE)

    def ready(ref, rows, cols):
        present = ref[4, rows, cols]
        ref[5, rows, cols] = SHARE * present * ref[5, rows, cols]
        ref[6, rows, cols] = SHARE * present * ref[6, rows, cols]
        mass = ref[2, rows, cols]
        ref[2, rows, cols] = 0.5 * SHARE * present / jnp.where(mass > 0.0, mass, 1.0)
        ref[4, rows, cols] = KEEP * present
        ref[3, rows, cols] = ref[3, rows, cols] * (RELAX / (1.0 + RELAX))

    def main_sides(ref, f, start, size):
        value = ref[f, start : start + size, :]
        return (
            value,
            pltpu.roll(value, 2 * COLS - 1, 1),
            pltpu.roll(value, 1, 1),
            ref[f, start + 1 : start + size + 1, :],
            ref[f, start - 1 : start + size - 1, :],
        )

    CHUNK = 24
    chunks = range(8, 8 + SPAN, CHUNK)

    def stress(u, v, third, old):
        twice_d = (u[1] - u[2]) + (v[3] - v[4])
        twice_h = (u[3] - u[4]) + (v[1] - v[2])
        viscous = third * lax.rsqrt(twice_d * twice_d + 0.25 * (twice_h * twice_h) + 0.04)
        a = viscous * twice_d - third
        b = viscous * twice_h
        if old is not None:
            a = a + old[0] * (1.0 / (1.0 + RELAX))
            b = b + old[1] * (1.0 / (1.0 + RELAX))
        return a, b

    def push(ref, vel, rows, cols, a, b):
        keep, mobility = ref[4, rows, cols], ref[2, rows, cols]
        new_u = keep * vel[0, rows, cols] + mobility * ((a[1] - a[2]) + (b[3] - b[4])) + ref[5, rows, cols]
        new_v = keep * vel[1, rows, cols] + mobility * ((b[1] - b[2]) + (a[3] - a[4])) + ref[6, rows, cols]
        vel[0, rows, cols] = new_u
        vel[1, rows, cols] = new_v

    every = slice(0, 8)

    def chunk_stress(vel, sig, start, first=False):
        rows = slice(start, start + CHUNK)
        u, v = main_sides(vel, 0, start, CHUNK), main_sides(vel, 1, start, CHUNK)
        old = None if first else (sig[0, rows, :], sig[1, rows, :])
        sig[0, rows, :], sig[1, rows, :] = stress(u, v, vel[3, rows, :], old)

    def chunk_push(vel, sig, start):
        a, b = main_sides(sig, 0, start, CHUNK), main_sides(sig, 1, start, CHUNK)
        push(vel, vel, slice(start, start + CHUNK), slice(0, 2 * COLS), a, b)

    def tile_cycle(cycle, carry):
        for start in chunks:
            chunk_stress(X, AB, start)
        for start in chunks:
            chunk_push(X, AB, start)
        return carry

    low_piece, high_piece, low_tile, high_tile = slice(8, 16), slice(16, 24), slice(80, 88), slice(88, 96)

    def top_cycles():
        for left in (3, 1):
            close_top(XT, 0, S, 0, -1)
            close_top(XT, 1, S, 1, -1)
            for win in windows(left):
                cols = slice(COLS * win[0], COLS * win[1])
                u, v = strip_sides(S, 0, win, -1), strip_sides(S, 1, win, -1)
                old = (SAB[0, :, cols], SAB[1, :, cols])
                SAB[0, :, cols], SAB[1, :, cols] = stress(u, v, S[3, :, cols], old)
            chunk_stress(XT, ABT, 8)
            close_top(ABT, 0, SAB, 0, 1)
            close_top(ABT, 1, SAB, 1, 1)
            for win in windows(left - 1):
                cols = slice(COLS * win[0], COLS * win[1])
                push(S, S, every, cols, strip_sides(SAB, 0, win, 1), strip_sides(SAB, 1, win, 1))
            chunk_push(XT, ABT, 8)

    away = pl.ds(pl.multiple_of(TOP + HALF * (1 - comp), 8), HALF)
    here = pl.ds(pl.multiple_of(TOP + HALF * comp, 8), HALF)
    ice_out = (new_ice_u, new_ice_v)
    vel_away = [
        send(X.at[i, away, 0:COLS], ice_out[i].at[:, mine], vel_send.at[i], vel_recv.at[i], partner) for i in range(2)
    ]
    vel_here = [
        pltpu.make_async_copy(X.at[i, here, 0:COLS], ice_out[i].at[:, mine], out_sem.at[3 + i]) for i in range(2)
    ]

    for start in chunks:
        ready(X, slice(start, start + CHUNK), slice(0, 2 * COLS))

    @pl.when(is_top)
    def _():
        XT[...] = X[:, 72:112, :]
        ABT[...] = jnp.zeros((2, 40, 2 * COLS), jnp.float32)
        SAB[...] = jnp.zeros((2, 8, BLOCKS * COLS), jnp.float32)

    def two_cycles(phase, carry):
        lax.fori_loop(0, 2, tile_cycle, 0)

        @pl.when(is_top & (phase == 0))
        def _():
            strips_arrive(False)
            IDX[...] = jnp.broadcast_to(S[NF, 7:8, :], IDX.shape).astype(jnp.int32)
            ready(S, every, slice(0, BLOCKS * COLS))

        @pl.when(is_top & (phase == 1))
        def _():
            strips_arrive(True)
            to_the_e = S2[0:2, 7:8, COLS * (REACH + 1) : COLS * (REACH + 2)]
            to_the_w = S2[0:2, 7:8, COLS * (REACH - 1) : COLS * REACH]
            XT[0:2, 23:24, COLS : 2 * COLS] = jnp.where(lane < COLS // 2, to_the_e, to_the_w)
            S[0:2] = S2[0:2]
            SAB[...] = S2[2:4]

        @pl.when(is_top)
        def _():
            top_cycles()

        @pl.when(is_top & (phase == 0))
        def _():
            SS2[0:2] = XT[0:2, high_piece, 0:COLS]
            SS2[2:4] = ABT[:, high_piece, 0:COLS]
            strips_start(True)
            S2[:, :, middle] = SS2[...]
            X[0:2, high_tile, :] = XT[0:2, high_piece, :]
            AB[:, high_tile, :] = ABT[:, high_piece, :]
            XT[0:2, low_piece, :] = X[0:2, low_tile, :]
            ABT[:, low_piece, :] = AB[:, low_tile, :]

        return carry

    lax.fori_loop(0, 2, two_cycles, 0)

    @pl.when(is_top)
    def _():
        X[0:2, high_tile, :] = XT[0:2, high_piece, :]

    for copy in vel_away + vel_here:
        copy.start()

    def regrid(g):
        planes = pl.ds(g * LEV, LEV)
        pieces = range(0, ROWS, LEV)
        high = jnp.concatenate([DH[planes, r : r + LEV, :].reshape(LEV * LEV, COLS) for r in pieces], axis=1)
        low = jnp.concatenate([DL[planes, r : r + LEV, :].reshape(LEV * LEV, COLS) for r in pieces], axis=1)
        new = jnp.dot(KK[...], jnp.concatenate([high, high, low], axis=0), preferred_element_type=jnp.float32)
        for i, r in enumerate(pieces):
            O[planes, r : r + LEV, :] = new[:, COLS * i : COLS * (i + 1)].reshape(LEV, LEV, COLS)

    outs = (new_tracer, new_ocean_u, new_ocean_v)

    stores = [
        pltpu.make_async_copy(O.at[g * LEV : (g + 1) * LEV], outs[g], out_sem.at[g]) for g in range(3)
    ]

    def finish(g, carry):
        regrid(g)
        for i in range(3):

            @pl.when(g == i)
            def _(i=i):
                if i:
                    tau = X[i - 1, tile_rows, 0:COLS] - X[4 + i, tile_rows, 0:COLS] * (1.0 / SHARE)
                    O[i * LEV] = O[i * LEV] + COUPLE * (F[SEA, 8 : 8 + ROWS, :] * tau)
                for q in quarters:
                    pltpu.make_async_copy(
                        O.at[i * LEV + q.start : i * LEV + q.stop], outs[i].at[q], out_sem.at[i]
                    ).start()

        return carry

    lax.fori_loop(0, 3, finish, 0)

    @pl.when(is_top)
    def _():
        strips_sent(False)
        strips_sent(True)

    for copy in ice_away:
        copy.wait_send()
    for copy in vel_away:
        copy.wait()
    for copy in vel_here + stores:
        copy.wait()


def deliver(*refs):
    count = len(refs) // 2
    sems = refs[-1]
    copies = [pltpu.make_async_copy(refs[i], refs[count + i], sems.at[i]) for i in range(count)]
    for i in range(3):
        for q in quarters:
            pltpu.make_async_copy(refs[i].at[q], refs[count + i].at[q], sems.at[i]).start()
    for copy in copies[3:]:
        copy.start()
    for copy in copies:
        copy.wait()


def solution(mesh):
    blocks = mesh.shape["gx"] * 2
    gys = mesh.shape["gy"]
    ocean = P(None, "gy", ("gx", "comp"))
    flat = P("gy", ("gx", "comp"))
    ice = P(("gy", "comp"), "gx")
    in_specs = (ocean, ocean, ocean, flat, P(), P(), P(), P(("gx", "comp")), ice, ice, ice, ice, ice)
    out_specs = (ocean, ocean, ocean, ice, ice)

    def body(tracer, ocean_u, ocean_v, ocean_mask, diffusivity, viscosity, remap, fold_partner, *ice_fields):
        f32 = jnp.float32
        anywhere = pl.BlockSpec(memory_space=pl.ANY)
        main_memory = pl.BlockSpec(memory_space=pltpu.HBM)
        vmem = pltpu.VMEM
        dma = pltpu.SemaphoreType.DMA
        ocean_shape = jax.ShapeDtypeStruct(tracer.shape, f32)
        ice_shape = jax.ShapeDtypeStruct(ice_fields[0].shape, f32)

        def step(*args):
            kernel(blocks, gys, *args)

        shapes = (ocean_shape, ocean_shape, ocean_shape, ice_shape, ice_shape)
        results = pl.pallas_call(
            step,
            out_shape=shapes,
            in_specs=[main_memory] * 13,
            out_specs=(anywhere,) * 5,
            scratch_shapes=[
                vmem((PLANES, 96, COLS), f32),
                vmem((3 * LEV, ROWS, COLS), jnp.bfloat16),
                vmem((3 * LEV, ROWS, COLS), jnp.bfloat16),
                vmem((LEV * LEV, 3 * LEV * LEV), jnp.bfloat16),
                vmem((3 * LEV, ROWS, COLS), f32),
                vmem((NF, 112, 2 * COLS), f32),
                vmem((2, 112, 2 * COLS), f32),
                vmem((NF, 40, 2 * COLS), f32),
                vmem((2, 40, 2 * COLS), f32),
                vmem((NS, 8, BLOCKS * COLS), f32),
                vmem((2, 8, BLOCKS * COLS), f32),
                vmem((NS, 8, COLS), f32),
                vmem((4, 8, BLOCKS * COLS), f32),
                vmem((4, 8, COLS), f32),
                vmem((HALF, COLS), f32),
                vmem((HALF, COLS), f32),
                vmem((HALF, COLS), f32),
                vmem((HALF, COLS), f32),
                vmem((8, COLS), f32),
                vmem((8, COLS), f32),
                vmem((8, COLS), f32),
                vmem((8, COLS), f32),
                vmem((3 * LEV, COLS), f32),
                vmem((3 * LEV, COLS), f32),
                vmem((3 * LEV, COLS), f32),
                vmem((3 * LEV, COLS), f32),
                *[vmem((8, COLS), f32)] * 8,
                vmem((HALF, COLS), f32),
                vmem((HALF, COLS), f32),
                vmem((HALF, COLS), f32),
                vmem((HALF, COLS), f32),
                vmem((ROWS, COLS), f32),
                vmem((5, ROWS, COLS), f32),
                vmem((ROWS, COLS), jnp.int32),
                vmem((ROWS, COLS), jnp.int32),
                vmem((8, BLOCKS * COLS), jnp.int32),
                pltpu.SMEM((LEV,), f32),
                pltpu.SMEM((LEV,), f32),
                pltpu.SMEM((LEV, LEV), f32),
                vmem((LEV, LEV), f32),
                vmem((1, COLS), jnp.int32),
                dma((9,)),
                dma((5,)),
                dma((5,)),
                dma((5,)),
                dma((5,)),
                dma((5,)),
                dma((5,)),
                dma((5,)),
                dma((8,)),
                dma((8,)),
                dma((BLOCKS,)),
                dma((BLOCKS,)),
                dma((BLOCKS,)),
                dma((BLOCKS,)),
                dma((5,)),
                dma((2,)),
                dma((2,)),
            ],
            compiler_params=pltpu.CompilerParams(
                collective_id=0, has_side_effects=True, vmem_limit_bytes=32 * 1024 * 1024
            ),
        )(
            *[
                pltpu.with_memory_space_constraint(value, pltpu.HBM)
                for value in (
                    tracer,
                    ocean_u,
                    ocean_v,
                    ocean_mask,
                    diffusivity,
                    viscosity,
                    remap,
                    fold_partner.reshape(1, COLS),
                    *ice_fields,
                )
            ]
        )
        return pl.pallas_call(
            deliver,
            out_shape=shapes,
            in_specs=[anywhere] * 5,
            out_specs=(main_memory,) * 5,
            scratch_shapes=[dma((5,))],
            compiler_params=pltpu.CompilerParams(vmem_limit_bytes=1024 * 1024),
        )(*results)

    return jax.shard_map(body, mesh=mesh, in_specs=in_specs, out_specs=out_specs, check_vma=False)
```

```python
import jax
import jax.numpy as jnp
from jax import lax
from jax.experimental import pallas as pl
from jax.experimental.pallas import tpu as pltpu
from jax.sharding import PartitionSpec as P

ITERS = 4
RELAX = 0.5
STEP_SIZE = 0.3
COUPLE = 0.5
MESH = pl.DeviceIdType.MESH

LEV = 16
ROWS = 80
HALF = 40
COLS = 128
NF = 7
NS = NF + 1
REACH = 2
SIDE = 2 * REACH + 1
BLOCKS = 2 * SIDE
TOP = 16
SPAN = 96
OWN_REACH = {2: 0, 3: 1}
MIRROR_REACH = {1: 0, 2: 1, 3: 2}
OWN_ROWS = (8, 2, 1)
MIRROR_ROWS = (4, 3, 2)
SEA = 3 * LEV
PLANES = SEA + 3


def kernel(
    blocks,
    gys,
    tracer,
    ocean_u,
    ocean_v,
    ocean_mask,
    diffusivity_in,
    viscosity_in,
    remap_in,
    fold_in,
    ice_u,
    ice_v,
    ice_mass,
    ice_strength,
    ice_mask,
    new_tracer,
    new_ocean_u,
    new_ocean_v,
    new_ice,
    F,
    DH,
    DL,
    KK,
    O,
    X,
    AB,
    XT,
    ABT,
    S,
    SAB,
    SS,
    S2,
    SS2,
    PE,
    PW,
    EB,
    WB,
    EBS,
    WBS,
    EBN,
    WBN,
    TR,
    BR,
    NR,
    SR,
    CK,
    RKE,
    RKW,
    GK,
    TK,
    BK,
    NK,
    SK,
    CE,
    CW,
    RE,
    RW,
    GE,
    MK,
    OM,
    IM,
    IDX,
    diffusivity,
    viscosity,
    remap,
    remap_wide,
    fold_partner,
    in_sem,
    ice_sem,
    ice_send,
    ice_recv,
    edge_send,
    edge_recv,
    first_send,
    first_recv,
    rim_send,
    rim_recv,
    strip_send,
    strip_recv,
    again_send,
    again_recv,
    out_sem,
    vel_send,
    vel_recv,
):
    gx, gy, comp = lax.axis_index("gx"), lax.axis_index("gy"), lax.axis_index("comp")
    me = gx * 2 + comp
    has_north = gy < gys - 1
    has_south = gy > 0
    is_top = gy == gys - 1

    def at(block, row):
        return {"gx": block // 2, "gy": row, "comp": lax.rem(block, 2)}

    def wrap(block):
        return lax.rem(block + 2 * blocks, blocks)

    east, west, mirror = wrap(me + 1), wrap(me - 1), blocks - 1 - me
    partner = at(gx * 2 + 1 - comp, gy)

    strips = [(SIDE + REACH, mirror, False, MIRROR_ROWS[0])]
    for d in (1, -1, 2, -2):
        strips.append((SIDE + REACH + d, wrap(mirror + d), d % 2 == 1, MIRROR_ROWS[abs(d)]))
        strips.append((REACH + d, wrap(me - d), False, OWN_ROWS[abs(d)]))

    def load(src, dst, sem):
        copy = pltpu.make_async_copy(src, dst, sem)
        copy.start()
        return copy

    load_u = load(ocean_u, F.at[LEV : 2 * LEV, 8 : 8 + ROWS, :], in_sem.at[0])
    load_v = load(ocean_v, F.at[2 * LEV : 3 * LEV, 8 : 8 + ROWS, :], in_sem.at[1])
    barrier = pltpu.get_barrier_semaphore()

    def greet(target):
        pl.semaphore_signal(barrier, inc=1, device_id=target, device_id_type=MESH)

    greet(at(east, gy))
    greet(at(west, gy))

    @pl.when(has_north)
    def _():
        for block in (me, east, west):
            greet(at(block, gy + 1))

    @pl.when(has_south)
    def _():
        for block in (me, east, west):
            greet(at(block, gy - 1))

    @pl.when(is_top)
    def _():
        for _, block, own, _ in strips:
            if own:

                @pl.when(block != me)
                def _(block=block):
                    greet(at(block, gy))
            else:
                greet(at(block, gy))

    small = [
        load(ocean_mask, OM, in_sem.at[2]),
        load(remap_in, remap, in_sem.at[4]),
        load(diffusivity_in, diffusivity, in_sem.at[5]),
        load(viscosity_in, viscosity, in_sem.at[6]),
        load(fold_in, fold_partner, in_sem.at[7]),
        load(remap_in, remap_wide, in_sem.at[8]),
    ]
    ice_in = (ice_u, ice_v, ice_mass, ice_strength, ice_mask)

    def ice_place(i, half):
        rows = pl.ds(pl.multiple_of(TOP + HALF * half, 8), HALF)
        if i == 4:
            return IM.at[pl.ds(pl.multiple_of(HALF * half, 8), HALF), :]
        return X.at[i, rows, 0:COLS]

    mine = pl.ds(pl.multiple_of(COLS * comp, COLS), COLS)
    other = pl.ds(pl.multiple_of(COLS * (1 - comp), COLS), COLS)
    for i in range(5):
        load(ice_in[i].at[:, mine], ice_place(i, comp), ice_sem.at[0])

    first8, last8 = slice(TOP, TOP + 8), slice(TOP + ROWS - 8, TOP + ROWS)
    south8, north8 = slice(TOP - 8, TOP), slice(TOP + ROWS, TOP + ROWS + 8)

    @pl.when(jnp.logical_not(has_south))
    def _():
        X[:, south8, 0:COLS] = jnp.zeros((NF, 8, COLS), jnp.float32)
        EBS[...] = jnp.zeros((8, COLS), jnp.float32)
        WBS[...] = jnp.zeros((8, COLS), jnp.float32)
        SR[...] = jnp.zeros((3 * LEV, COLS), jnp.float32)
        SK[...] = jnp.zeros((8, COLS), jnp.float32)

    @pl.when(is_top)
    def _():
        X[:, north8, 0:COLS] = jnp.zeros((NF, 8, COLS), jnp.float32)
        EBN[...] = jnp.zeros((8, COLS), jnp.float32)
        WBN[...] = jnp.zeros((8, COLS), jnp.float32)

    outer = jnp.zeros((NF, 8, 2 * COLS), jnp.float32)
    X[:, 0:8, :] = outer
    X[:, 104:112, :] = outer
    AB[...] = jnp.zeros((2, 112, 2 * COLS), jnp.float32)

    count = 2 + 3 * has_north.astype(jnp.int32) + 3 * has_south.astype(jnp.int32)
    strip_count = 0
    for _, block, own, _ in strips:
        strip_count = strip_count + ((block != me).astype(jnp.int32) if own else 1)
    count = count + is_top.astype(jnp.int32) * strip_count
    pl.semaphore_wait(barrier, count)

    def send(src, dst, send_sem, recv_sem, target):
        copy = pltpu.make_async_remote_copy(
            src_ref=src,
            dst_ref=dst,
            send_sem=send_sem,
            recv_sem=recv_sem,
            device_id=target,
            device_id_type=MESH,
        )
        return copy

    for i in range(5):
        send(ice_in[i].at[:, other], ice_place(i, comp), ice_send.at[0], ice_recv.at[0], partner).start()
    ice_all = X.at[0:5, TOP : TOP + HALF, 0:COLS]
    ice_away = send(ice_all, ice_all, ice_send.at[0], ice_recv.at[0], partner)

    load_t = load(tracer, F.at[0:LEV, 8 : 8 + ROWS, :], in_sem.at[3])
    lane = lax.broadcasted_iota(jnp.int32, (1, COLS), 1)
    even = (lane & 1) == 0
    row8 = lax.broadcasted_iota(jnp.int32, (8, 1), 0)
    tile_rows = slice(TOP, TOP + ROWS)

    for copy in small:
        copy.wait()
    sea = OM[...].astype(jnp.float32)
    F[SEA, 8 : 8 + ROWS, :] = sea
    for i, copy in ((0, load_u), (1, load_v)):
        copy.wait()

        def level(l, sums, i=i):
            weighted = remap[0, l] * F[LEV * (i + 1) + l, 8 : 8 + ROWS, :]
            return sums[0] + weighted, sums[1] + viscosity[l] * weighted

        zero = jnp.zeros((ROWS, COLS), jnp.float32)
        base, spread = lax.fori_loop(0, LEV, level, (zero, zero), unroll=4)
        X[5 + i, tile_rows, 0:COLS] = base
        F[SEA + 1 + i, 8 : 8 + ROWS, :] = spread

    first = [(3 * t + p, SEA + p, slice(8 + 8 * t, 16 + 8 * t)) for t in range(ROWS // 8) for p in range(3)]
    packed = jnp.zeros((8, COLS), jnp.float32)
    for m, f, rows in first:
        packed = jnp.where((lane >> 1) == m, pltpu.roll(F[f, rows, :], 2 * m + 1, 1), packed)
    CK[...] = packed
    for p in range(3):
        TK[p : p + 1, :] = F[SEA + p, 87:88, :]
        BK[p : p + 1, :] = F[SEA + p, 8:9, :]
    first_e = send(CK, RKW, first_send.at[0], first_recv.at[0], at(east, gy))
    first_w = send(CK, RKE, first_send.at[1], first_recv.at[1], at(west, gy))
    first_n = send(TK, SK, first_send.at[2], first_recv.at[2], at(me, gy + 1))
    first_s = send(BK, NK, first_send.at[3], first_recv.at[3], at(me, gy - 1))
    first_f = send(TK, NK, first_send.at[4], first_recv.at[4], at(mirror, gy))
    first_e.start()
    first_w.start()

    @pl.when(has_north)
    def _():
        first_n.start()

    @pl.when(has_south)
    def _():
        first_s.start()

    @pl.when(is_top)
    def _():
        first_f.start()

    load_t.wait()
    for f in range(3 * LEV):
        TR[f : f + 1, :] = F[f, 87:88, :]
        BR[f : f + 1, :] = F[f, 8:9, :]
    row_n = send(TR, SR, edge_send.at[2], edge_recv.at[2], at(me, gy + 1))
    row_s = send(BR, NR, edge_send.at[3], edge_recv.at[3], at(me, gy - 1))
    row_f = send(TR, NR, edge_send.at[4], edge_recv.at[4], at(mirror, gy))

    @pl.when(has_north)
    def _():
        row_n.start()

    @pl.when(has_south)
    def _():
        row_s.start()

    @pl.when(is_top)
    def _():
        row_f.start()

    def pack(f, packed):
        return jnp.where((lane >> 1) == f, pltpu.roll(F[f, 8 : 8 + ROWS, :], 2 * f + 1, 1), packed)

    packed = lax.fori_loop(0, 3 * LEV, pack, jnp.zeros((ROWS, COLS), jnp.float32), unroll=3)
    CE[...] = jnp.where(even, packed[0:HALF], pltpu.roll(packed[HALF:ROWS], 1, 1))
    CW[...] = jnp.where(even, pltpu.roll(packed[HALF:ROWS], COLS - 1, 1), packed[0:HALF])
    col_to_e = send(CE, RW, edge_send.at[0], edge_recv.at[0], at(east, gy))
    col_to_w = send(CW, RE, edge_send.at[1], edge_recv.at[1], at(west, gy))
    col_to_e.start()
    col_to_w.start()

    lane2 = lax.broadcasted_iota(jnp.int32, (LEV, LEV * LEV), 1)
    weights = jnp.zeros((LEV, LEV * LEV), jnp.float32)
    for l in range(LEV):
        weights = jnp.where((lane2 >> 4) == l, remap_wide[:, l : l + 1], weights)
    high = weights.astype(jnp.bfloat16).astype(jnp.float32)
    low = weights - high
    diagonal = (lane2 & 15) == lax.broadcasted_iota(jnp.int32, (LEV, LEV * LEV), 0)
    for k in range(LEV):
        rows = slice(LEV * k, LEV * (k + 1))
        high_k = jnp.where(diagonal, high[k : k + 1], 0.0).astype(jnp.bfloat16)
        KK[rows, 0:256] = high_k
        KK[rows, 256:512] = jnp.where(diagonal, low[k : k + 1], 0.0).astype(jnp.bfloat16)
        KK[rows, 512:768] = high_k

    first_e.wait()
    first_w.wait()

    @pl.when(has_north)
    def _():
        first_n.wait_send()
        first_s.wait_recv()

    @pl.when(has_south)
    def _():
        first_s.wait_send()
        first_n.wait_recv()

    inside_here = fold_partner[...] - COLS * mirror

    @pl.when(is_top)
    def _():
        first_f.wait()
        inside = jnp.broadcast_to(inside_here, (8, COLS))
        taken = jnp.take_along_axis(NK[...], inside, axis=1, mode="promise_in_bounds")
        NK[...] = jnp.where(row8 == 0, taken, -taken)

    GK[...] = jnp.where(even, pltpu.roll(RKE[...], COLS - 1, 1), pltpu.roll(RKW[...], 1, 1))
    for p in range(3):
        F[SEA + p, 88:89, :] = NK[p : p + 1, :]
        F[SEA + p, 7:8, :] = SK[p : p + 1, :]

    def sides_of(f, edges):
        value = F[f, 8 : 8 + ROWS, :]
        to_east = jnp.where(lane == COLS - 1, edges, pltpu.roll(value, COLS - 1, 1))
        to_west = jnp.where(lane == 0, edges, pltpu.roll(value, 1, 1))
        return value, to_east, to_west, F[f, 9 : 9 + ROWS, :], F[f, 7 : 7 + ROWS, :]

    def first_edges(f):
        return jnp.concatenate([pltpu.roll(GK[...], COLS - 1 - 2 * m, 1) for m, g, _ in first if g == f], axis=0)

    def lap(f, edges):
        value, to_east, to_west, to_north, to_south = sides_of(f, edges)
        total = MK[0] * to_east + MK[1] * to_west + MK[2] * to_north + MK[3] * to_south
        return value, total - MK[4] * value

    seas = sides_of(SEA, first_edges(SEA))
    degree = jnp.zeros((ROWS, COLS), jnp.float32)
    for i in range(4):
        weight = seas[0] * seas[i + 1]
        MK[i] = weight
        degree = degree + weight
    MK[4] = degree
    for i in range(2):
        f = SEA + 1 + i
        X[5 + i, tile_rows, 0:COLS] = X[5 + i, tile_rows, 0:COLS] + lap(f, first_edges(f))[1]

    pltpu.make_async_copy(ice_all, ice_all, ice_sem.at[0]).wait()
    ice_away.wait_recv()
    X[4, tile_rows, 0:COLS] = IM[...].astype(jnp.float32)


    def rim_pack(f, packed):
        south_half, north_half = X[f, TOP : TOP + HALF, 0:COLS], X[f, TOP + HALF : TOP + ROWS, 0:COLS]
        group = lane >> 3
        new = []
        for edge, old in ((8, packed[0]), (0, packed[1])):
            kept = jnp.where(group == f, pltpu.roll(south_half, 8 * f + edge, 1), old)
            new.append(jnp.where(group == f + 8, pltpu.roll(north_half, 64 + 8 * f + edge, 1), kept))
        return tuple(new)

    zero = jnp.zeros((HALF, COLS), jnp.float32)
    pack_e, pack_w = lax.fori_loop(0, NF, rim_pack, (zero, zero), unroll=7)
    PE[...] = pack_e
    PW[...] = pack_w
    to_e = send(PE, WB, rim_send.at[0], rim_recv.at[0], at(east, gy))
    to_w = send(PW, EB, rim_send.at[1], rim_recv.at[1], at(west, gy))
    to_n = [
        send(X.at[:, last8, 0:COLS], X.at[:, south8, 0:COLS], rim_send.at[2], rim_recv.at[2], at(me, gy + 1)),
        send(PE.at[HALF - 8 : HALF], WBS, rim_send.at[3], rim_recv.at[3], at(east, gy + 1)),
        send(PW.at[HALF - 8 : HALF], EBS, rim_send.at[4], rim_recv.at[4], at(west, gy + 1)),
    ]
    to_s = [
        send(X.at[:, first8, 0:COLS], X.at[:, north8, 0:COLS], rim_send.at[5], rim_recv.at[5], at(me, gy - 1)),
        send(PE.at[0:8], WBN, rim_send.at[6], rim_recv.at[6], at(east, gy - 1)),
        send(PW.at[0:8], EBN, rim_send.at[7], rim_recv.at[7], at(west, gy - 1)),
    ]

    def strip_ends(src, dst, slot, rows):
        kept = slice(8 - rows, 8)
        return src.at[:, kept, :], dst.at[:, kept, COLS * slot : COLS * (slot + 1)]

    def strip_copy(again, slot, block, own, rows):
        src, dst = strip_ends(SS2, S2, slot, rows) if again else strip_ends(SS, S, slot, rows)
        sent, received = (again_send, again_recv) if again else (strip_send, strip_recv)
        return send(src, dst, sent.at[slot if own else 0], received.at[0], at(block, gy))

    def strips_start(again):
        for slot, block, own, rows in strips:
            if own:

                @pl.when(block != me)
                def _(slot=slot, block=block, rows=rows):
                    strip_copy(again, slot, block, True, rows).start()

                @pl.when(block == me)
                def _(slot=slot, rows=rows):
                    src, dst = strip_ends(SS2, S2, slot, rows) if again else strip_ends(SS, S, slot, rows)
                    pltpu.make_async_copy(src, dst, (again_recv if again else strip_recv).at[0]).start()
            else:
                strip_copy(again, slot, block, False, rows).start()

    def strips_all(again, rows):
        area = (S2 if again else S).at[:, 0:1, 0 : COLS * rows]
        sent, received = (again_send, again_recv) if again else (strip_send, strip_recv)
        return send(area, area, sent.at[0], received.at[0], partner)

    def strips_arrive(again):
        strips_all(again, sum(rows for _, _, _, rows in strips)).wait_recv()

    def strips_sent(again):
        strips_all(again, sum(rows for _, _, own, rows in strips if not own)).wait_send()
        for slot, block, own, rows in strips:
            if own:

                @pl.when(block != me)
                def _(slot=slot, block=block, rows=rows):
                    strip_copy(again, slot, block, True, rows).wait_send()

    middle = slice(COLS * REACH, COLS * (REACH + 1))

    to_e.start()
    to_w.start()

    @pl.when(has_north)
    def _():
        for copy in to_n:
            copy.start()

    @pl.when(has_south)
    def _():
        for copy in to_s:
            copy.start()

    @pl.when(is_top)
    def _():
        SS[0:NF] = X[0:NF, last8, 0:COLS]
        SS[NF] = jnp.broadcast_to(inside_here.astype(jnp.float32), (8, COLS))
        S[:, :, middle] = SS[...]
        strips_start(False)

    col_to_e.wait()
    col_to_w.wait()

    @pl.when(has_north)
    def _():
        row_n.wait_send()
        row_s.wait_recv()

    @pl.when(has_south)
    def _():
        row_s.wait_send()
        row_n.wait_recv()

    @pl.when(is_top)
    def _():
        row_f.wait()
        inside = jnp.broadcast_to(inside_here, (8, COLS))
        for r in range(0, 3 * LEV, 8):
            taken = jnp.take_along_axis(NR[r : r + 8, :], inside, axis=1, mode="promise_in_bounds")
            NR[r : r + 8, :] = taken if r < LEV else -taken

    for f in range(3 * LEV):
        F[f, 88:89, :] = NR[f : f + 1, :]
        F[f, 7:8, :] = SR[f : f + 1, :]
    GE[0:HALF] = jnp.where(even, pltpu.roll(RE[...], COLS - 1, 1), pltpu.roll(RW[...], 1, 1))
    GE[HALF:ROWS] = jnp.where(even, RE[...], RW[...])

    def diffuse(f, carry):
        coefficient = jnp.where(f < LEV, diffusivity[f & (LEV - 1)], viscosity[f & (LEV - 1)])
        value, spread = lap(f, pltpu.roll(GE[...], COLS - 1 - 2 * f, 1))
        new = value + coefficient * spread
        high = new.astype(jnp.bfloat16)
        DH[f] = high
        DL[f] = (new - high.astype(jnp.float32)).astype(jnp.bfloat16)
        return carry

    lax.fori_loop(0, 3 * LEV, diffuse, 0, unroll=4)

    to_e.wait()
    to_w.wait()

    @pl.when(has_north)
    def _():
        for copy in to_n:
            copy.wait_send()
        for copy in to_s:
            copy.wait_recv()

    @pl.when(has_south)
    def _():
        for copy in to_s:
            copy.wait_send()
        for copy in to_n:
            copy.wait_recv()

    def rim_unpack(f, carry):
        def put(rows, e, w, half):
            from_e = pltpu.roll(e, lax.rem(COLS + half - 8 * f, COLS), 1)
            from_w = pltpu.roll(w, lax.rem(2 * COLS - 8 + half - 8 * f, COLS), 1)
            X[f, rows, COLS : 2 * COLS] = jnp.where(
                lane < 8, from_e, jnp.where(lane >= COLS - 8, from_w, 0.0)
            )

        put(slice(TOP, TOP + HALF), EB[...], WB[...], 0)
        put(slice(TOP + HALF, TOP + ROWS), EB[...], WB[...], 64)
        put(slice(TOP - 8, TOP), EBS[...], WBS[...], 64)
        put(slice(TOP + ROWS, TOP + ROWS + 8), EBN[...], WBN[...], 0)
        return carry

    lax.fori_loop(0, NF, rim_unpack, 0, unroll=7)

    def inside_of(i):
        return IDX[:, COLS * i : COLS * (i + 1)]

    def fold_block(ref, f, i, sign):
        j = BLOCKS - 1 - i
        value = ref[f, :, COLS * j : COLS * (j + 1)]
        taken = jnp.take_along_axis(value, inside_of(i), axis=1, mode="promise_in_bounds")
        return taken if sign > 0 else -taken

    def close_top(ref, f, strip_ref, sf, sign):
        own = fold_block(strip_ref, sf, REACH, sign)
        to_the_e = fold_block(strip_ref, sf, REACH + 1, sign)
        to_the_w = fold_block(strip_ref, sf, REACH - 1, sign)
        ref[f, 24:25, 0:COLS] = own[7:8]
        ref[f, 24:25, COLS : 2 * COLS] = jnp.where(lane < COLS // 2, to_the_e, to_the_w)[7:8]

    def window(first, reach):
        middle = first + REACH
        low, high = middle - reach, middle + reach + 1
        wide_low, wide_high = max(low - 1, first), min(high + 1, first + SIDE)
        return low, high, wide_low, wide_high

    def strip_sides(ref, f, win, sign):
        low, high, wide_low, wide_high = win
        wide = ref[f, :, COLS * wide_low : COLS * wide_high]
        length = COLS * (wide_high - wide_low)
        cut = slice(COLS * (low - wide_low), COLS * (high - wide_low))
        value = wide[:, cut]
        to_east = pltpu.roll(wide, length - 1, 1)[:, cut]
        to_west = pltpu.roll(wide, 1, 1)[:, cut]
        folded = jnp.concatenate([fold_block(ref, f, i, sign) for i in range(low, high)], axis=1)
        to_north = jnp.where(row8 == 7, folded, pltpu.roll(value, 7, 0))
        to_south = pltpu.roll(value, 1, 0)
        return value, to_east, to_west, to_north, to_south

    def windows(left):
        found = []
        if left in OWN_REACH:
            found.append(window(0, OWN_REACH[left]))
        if left in MIRROR_REACH:
            found.append(window(SIDE, MIRROR_REACH[left]))
        return found

    SHARE = STEP_SIZE / (1.0 + STEP_SIZE)
    KEEP = 1.0 / (1.0 + STEP_SIZE)

    def ready(ref, rows, cols):
        present = ref[4, rows, cols]
        ref[5, rows, cols] = SHARE * present * ref[5, rows, cols]
        ref[6, rows, cols] = SHARE * present * ref[6, rows, cols]
        mass = ref[2, rows, cols]
        ref[2, rows, cols] = 0.5 * SHARE * present / jnp.where(mass > 0.0, mass, 1.0)
        ref[4, rows, cols] = KEEP * present
        ref[3, rows, cols] = ref[3, rows, cols] * (RELAX / (1.0 + RELAX))

    def main_sides(ref, f, start, size):
        value = ref[f, start : start + size, :]
        return (
            value,
            pltpu.roll(value, 2 * COLS - 1, 1),
            pltpu.roll(value, 1, 1),
            ref[f, start + 1 : start + size + 1, :],
            ref[f, start - 1 : start + size - 1, :],
        )

    CHUNK = 24
    chunks = range(8, 8 + SPAN, CHUNK)

    def stress(u, v, third, old):
        twice_d = (u[1] - u[2]) + (v[3] - v[4])
        twice_h = (u[3] - u[4]) + (v[1] - v[2])
        viscous = third * lax.rsqrt(twice_d * twice_d + 0.25 * (twice_h * twice_h) + 0.04)
        a = viscous * twice_d - third
        b = viscous * twice_h
        if old is not None:
            a = a + old[0] * (1.0 / (1.0 + RELAX))
            b = b + old[1] * (1.0 / (1.0 + RELAX))
        return a, b

    def push(ref, vel, rows, cols, a, b):
        keep, mobility = ref[4, rows, cols], ref[2, rows, cols]
        new_u = keep * vel[0, rows, cols] + mobility * ((a[1] - a[2]) + (b[3] - b[4])) + ref[5, rows, cols]
        new_v = keep * vel[1, rows, cols] + mobility * ((b[1] - b[2]) + (a[3] - a[4])) + ref[6, rows, cols]
        vel[0, rows, cols] = new_u
        vel[1, rows, cols] = new_v

    every = slice(0, 8)

    def chunk_stress(vel, sig, start, first=False):
        rows = slice(start, start + CHUNK)
        u, v = main_sides(vel, 0, start, CHUNK), main_sides(vel, 1, start, CHUNK)
        old = None if first else (sig[0, rows, :], sig[1, rows, :])
        sig[0, rows, :], sig[1, rows, :] = stress(u, v, vel[3, rows, :], old)

    def chunk_push(vel, sig, start):
        a, b = main_sides(sig, 0, start, CHUNK), main_sides(sig, 1, start, CHUNK)
        push(vel, vel, slice(start, start + CHUNK), slice(0, 2 * COLS), a, b)

    def tile_cycle(cycle, carry):
        for start in chunks:
            chunk_stress(X, AB, start)
        for start in chunks:
            chunk_push(X, AB, start)
        return carry

    low_piece, high_piece, low_tile, high_tile = slice(8, 16), slice(16, 24), slice(80, 88), slice(88, 96)

    def top_cycles(cycles):
        vel, sig, i_a, i_b = (S, SAB, 0, 1) if cycles[0] == 0 else (S2, S2, 2, 3)
        for cycle in cycles:
            left = 3 if cycle == cycles[0] else 1
            close_top(XT, 0, vel, 0, -1)
            close_top(XT, 1, vel, 1, -1)
            for win in windows(left):
                cols = slice(COLS * win[0], COLS * win[1])
                u, v = strip_sides(vel, 0, win, -1), strip_sides(vel, 1, win, -1)
                old = (sig[i_a, :, cols], sig[i_b, :, cols]) if cycle else None
                sig[i_a, :, cols], sig[i_b, :, cols] = stress(u, v, S[3, :, cols], old)
            chunk_stress(XT, ABT, 8, cycle == 0)
            close_top(ABT, 0, sig, i_a, 1)
            close_top(ABT, 1, sig, i_b, 1)
            for win in windows(left - 1):
                cols = slice(COLS * win[0], COLS * win[1])
                push(S, vel, every, cols, strip_sides(sig, i_a, win, 1), strip_sides(sig, i_b, win, 1))
            chunk_push(XT, ABT, 8)

    for start in chunks:
        ready(X, slice(start, start + CHUNK), slice(0, 2 * COLS))

    @pl.when(is_top)
    def _():
        XT[...] = X[:, 72:112, :]
        ABT[...] = jnp.zeros((2, 40, 2 * COLS), jnp.float32)

    lax.fori_loop(0, 2, tile_cycle, 0)

    @pl.when(is_top)
    def _():
        strips_arrive(False)
        IDX[...] = jnp.broadcast_to(S[NF, 7:8, 0 : BLOCKS * COLS], IDX.shape).astype(jnp.int32)
        ready(S, every, slice(0, BLOCKS * COLS))
        top_cycles((0, 1))
        SS2[0:2] = XT[0:2, high_piece, 0:COLS]
        SS2[2:4] = ABT[:, high_piece, 0:COLS]
        strips_start(True)
        S2[:, :, middle] = SS2[...]
        X[0:2, high_tile, :] = XT[0:2, high_piece, :]
        AB[:, high_tile, :] = ABT[:, high_piece, :]
        XT[0:2, low_piece, :] = X[0:2, low_tile, :]
        ABT[:, low_piece, :] = AB[:, low_tile, :]

    lax.fori_loop(0, 2, tile_cycle, 0)

    away = pl.ds(pl.multiple_of(TOP + HALF * (1 - comp), 8), HALF)
    here = pl.ds(pl.multiple_of(TOP + HALF * comp, 8), HALF)
    vel_away = send(X.at[0:2, away, 0:COLS], new_ice.at[:, :, mine], vel_send.at[0], vel_recv.at[0], partner)
    vel_here = pltpu.make_async_copy(X.at[0:2, here, 0:COLS], new_ice.at[:, :, mine], out_sem.at[3])

    @pl.when(jnp.logical_not(is_top))
    def _():
        vel_away.start()
        vel_here.start()

    def regrid(g):
        planes = pl.ds(g * LEV, LEV)
        pieces = range(0, ROWS, LEV)
        high = jnp.concatenate([DH[planes, r : r + LEV, :].reshape(LEV * LEV, COLS) for r in pieces], axis=1)
        low = jnp.concatenate([DL[planes, r : r + LEV, :].reshape(LEV * LEV, COLS) for r in pieces], axis=1)
        new = jnp.dot(KK[...], jnp.concatenate([high, high, low], axis=0), preferred_element_type=jnp.float32)
        for i, r in enumerate(pieces):
            O[planes, r : r + LEV, :] = new[:, COLS * i : COLS * (i + 1)].reshape(LEV, LEV, COLS)

    @pl.when(is_top)
    def _():
        def early(g, carry):
            regrid(g)
            return carry

        lax.fori_loop(0, 2, early, 0)
        strips_arrive(True)
        to_the_e = S2[0:2, 7:8, COLS * (REACH + 1) : COLS * (REACH + 2)]
        to_the_w = S2[0:2, 7:8, COLS * (REACH - 1) : COLS * REACH]
        XT[0:2, 23:24, COLS : 2 * COLS] = jnp.where(lane < COLS // 2, to_the_e, to_the_w)
        top_cycles((2, 3))
        X[0:2, high_tile, :] = XT[0:2, high_piece, :]
        vel_away.start()
        vel_here.start()

    outs = (new_tracer, new_ocean_u, new_ocean_v)

    stores = [
        pltpu.make_async_copy(O.at[g * LEV : (g + 1) * LEV], outs[g], out_sem.at[g]) for g in range(3)
    ]

    def finish(g, carry):
        @pl.when(jnp.logical_not(is_top) | (g == 2))
        def _():
            regrid(g)

        for i in range(3):

            @pl.when(g == i)
            def _(i=i):
                if i:
                    tau = X[i - 1, tile_rows, 0:COLS] - X[4 + i, tile_rows, 0:COLS] * (1.0 / SHARE)
                    O[i * LEV] = O[i * LEV] + COUPLE * (F[SEA, 8 : 8 + ROWS, :] * tau)
                stores[i].start()

        return carry

    lax.fori_loop(0, 3, finish, 0)

    @pl.when(is_top)
    def _():
        strips_sent(False)
        strips_sent(True)

    ice_away.wait_send()
    vel_away.wait()
    for copy in [vel_here] + stores:
        copy.wait()


def deliver(tracer, ocean_u, ocean_v, ice, new_tracer, new_ocean_u, new_ocean_v, new_ice_u, new_ice_v, sems):
    pairs = [
        (tracer, new_tracer),
        (ocean_u, new_ocean_u),
        (ocean_v, new_ocean_v),
        (ice.at[0], new_ice_u),
        (ice.at[1], new_ice_v),
    ]
    copies = [pltpu.make_async_copy(src, dst, sems.at[i]) for i, (src, dst) in enumerate(pairs)]
    for copy in copies:
        copy.start()
    for copy in copies:
        copy.wait()


def solution(mesh):
    blocks = mesh.shape["gx"] * 2
    gys = mesh.shape["gy"]
    ocean = P(None, "gy", ("gx", "comp"))
    flat = P("gy", ("gx", "comp"))
    ice = P(("gy", "comp"), "gx")
    in_specs = (ocean, ocean, ocean, flat, P(), P(), P(), P(("gx", "comp")), ice, ice, ice, ice, ice)
    out_specs = (ocean, ocean, ocean, ice, ice)

    def body(tracer, ocean_u, ocean_v, ocean_mask, diffusivity, viscosity, remap, fold_partner, *ice_fields):
        f32 = jnp.float32
        anywhere = pl.BlockSpec(memory_space=pl.ANY)
        main_memory = pl.BlockSpec(memory_space=pltpu.HBM)
        vmem = pltpu.VMEM
        dma = pltpu.SemaphoreType.DMA
        ocean_shape = jax.ShapeDtypeStruct(tracer.shape, f32)
        ice_shape = jax.ShapeDtypeStruct(ice_fields[0].shape, f32)

        def step(*args):
            kernel(blocks, gys, *args)

        shapes = (ocean_shape, ocean_shape, ocean_shape, ice_shape, ice_shape)
        results = pl.pallas_call(
            step,
            out_shape=(*shapes[:3], jax.ShapeDtypeStruct((2, *ice_fields[0].shape), f32)),
            in_specs=[main_memory] * 13,
            out_specs=(anywhere,) * 4,
            scratch_shapes=[
                vmem((PLANES, 96, COLS), f32),
                vmem((3 * LEV, ROWS, COLS), jnp.bfloat16),
                vmem((3 * LEV, ROWS, COLS), jnp.bfloat16),
                vmem((LEV * LEV, 3 * LEV * LEV), jnp.bfloat16),
                vmem((3 * LEV, ROWS, COLS), f32),
                vmem((NF, 112, 2 * COLS), f32),
                vmem((2, 112, 2 * COLS), f32),
                vmem((NF, 40, 2 * COLS), f32),
                vmem((2, 40, 2 * COLS), f32),
                vmem((NS, 8, 2 * BLOCKS * COLS), f32),
                vmem((2, 8, BLOCKS * COLS), f32),
                vmem((NS, 8, COLS), f32),
                vmem((4, 8, 2 * BLOCKS * COLS), f32),
                vmem((4, 8, COLS), f32),
                vmem((HALF, COLS), f32),
                vmem((HALF, COLS), f32),
                vmem((HALF, COLS), f32),
                vmem((HALF, COLS), f32),
                vmem((8, COLS), f32),
                vmem((8, COLS), f32),
                vmem((8, COLS), f32),
                vmem((8, COLS), f32),
                vmem((3 * LEV, COLS), f32),
                vmem((3 * LEV, COLS), f32),
                vmem((3 * LEV, COLS), f32),
                vmem((3 * LEV, COLS), f32),
                *[vmem((8, COLS), f32)] * 8,
                vmem((HALF, COLS), f32),
                vmem((HALF, COLS), f32),
                vmem((HALF, COLS), f32),
                vmem((HALF, COLS), f32),
                vmem((ROWS, COLS), f32),
                vmem((5, ROWS, COLS), f32),
                vmem((ROWS, COLS), jnp.int32),
                vmem((ROWS, COLS), jnp.int32),
                vmem((8, BLOCKS * COLS), jnp.int32),
                pltpu.SMEM((LEV,), f32),
                pltpu.SMEM((LEV,), f32),
                pltpu.SMEM((LEV, LEV), f32),
                vmem((LEV, LEV), f32),
                vmem((1, COLS), jnp.int32),
                dma((9,)),
                dma((5,)),
                dma((5,)),
                dma((5,)),
                dma((5,)),
                dma((5,)),
                dma((5,)),
                dma((5,)),
                dma((8,)),
                dma((8,)),
                dma((BLOCKS,)),
                dma((BLOCKS,)),
                dma((BLOCKS,)),
                dma((BLOCKS,)),
                dma((5,)),
                dma((2,)),
                dma((2,)),
            ],
            compiler_params=pltpu.CompilerParams(
                collective_id=0, has_side_effects=True, vmem_limit_bytes=32 * 1024 * 1024
            ),
        )(
            *[
                pltpu.with_memory_space_constraint(value, pltpu.HBM)
                for value in (
                    tracer,
                    ocean_u,
                    ocean_v,
                    ocean_mask,
                    diffusivity,
                    viscosity,
                    remap,
                    fold_partner.reshape(1, COLS),
                    *ice_fields,
                )
            ]
        )
        return pl.pallas_call(
            deliver,
            out_shape=shapes,
            in_specs=[anywhere] * 4,
            out_specs=(main_memory,) * 5,
            scratch_shapes=[dma((5,))],
            compiler_params=pltpu.CompilerParams(vmem_limit_bytes=1024 * 1024),
        )(*results)

    return jax.shard_map(body, mesh=mesh, in_specs=in_specs, out_specs=out_specs, check_vma=False)
```

```python
import jax
import jax.numpy as jnp
from jax import lax
from jax.experimental import pallas as pl
from jax.experimental.pallas import tpu as pltpu
from jax.sharding import PartitionSpec as P

ITERS = 4
RELAX = 0.5
STEP_SIZE = 0.3
COUPLE = 0.5
MESH = pl.DeviceIdType.MESH

LEV = 16
ROWS = 80
HALF = 40
COLS = 128
NF = 7
NS = NF + 1
REACH = 2
SIDE = 2 * REACH + 1
BLOCKS = 2 * SIDE
TOP = 16
SPAN = 96
OWN_REACH = {2: 0, 3: 1}
MIRROR_REACH = {1: 0, 2: 1, 3: 2}
OWN_ROWS = (8, 2, 1)
MIRROR_ROWS = (4, 3, 2)
SEA = 3 * LEV
PLANES = SEA + 3


def kernel(
    blocks,
    gys,
    tracer,
    ocean_u,
    ocean_v,
    ocean_mask,
    diffusivity_in,
    viscosity_in,
    remap_in,
    fold_in,
    ice_u,
    ice_v,
    ice_mass,
    ice_strength,
    ice_mask,
    new_tracer,
    new_ocean_u,
    new_ocean_v,
    new_ice,
    F,
    DH,
    DL,
    KK,
    O,
    X,
    AB,
    XT,
    ABT,
    S,
    SAB,
    SS,
    S2,
    SS2,
    PE,
    PW,
    EB,
    WB,
    EBS,
    WBS,
    EBN,
    WBN,
    TR,
    BR,
    NR,
    SR,
    CK,
    RKE,
    RKW,
    GK,
    TK,
    BK,
    NK,
    SK,
    CE,
    CW,
    RE,
    RW,
    GE,
    MK,
    OM,
    IM,
    IDX,
    diffusivity,
    viscosity,
    remap,
    remap_wide,
    fold_partner,
    in_sem,
    ice_sem,
    ice_send,
    ice_recv,
    edge_send,
    edge_recv,
    first_send,
    first_recv,
    rim_send,
    rim_recv,
    strip_send,
    strip_recv,
    again_send,
    again_recv,
    out_sem,
    vel_send,
    vel_recv,
):
    gx, gy, comp = lax.axis_index("gx"), lax.axis_index("gy"), lax.axis_index("comp")
    me = gx * 2 + comp
    has_north = gy < gys - 1
    has_south = gy > 0
    is_top = gy == gys - 1

    def at(block, row):
        return {"gx": block // 2, "gy": row, "comp": lax.rem(block, 2)}

    def wrap(block):
        return lax.rem(block + 2 * blocks, blocks)

    east, west, mirror = wrap(me + 1), wrap(me - 1), blocks - 1 - me
    partner = at(gx * 2 + 1 - comp, gy)

    strips = [(SIDE + REACH, mirror, False, MIRROR_ROWS[0])]
    for d in (1, -1, 2, -2):
        strips.append((SIDE + REACH + d, wrap(mirror + d), d % 2 == 1, MIRROR_ROWS[abs(d)]))
        strips.append((REACH + d, wrap(me - d), False, OWN_ROWS[abs(d)]))

    def load(src, dst, sem):
        copy = pltpu.make_async_copy(src, dst, sem)
        copy.start()
        return copy

    load_u = load(ocean_u, F.at[LEV : 2 * LEV, 8 : 8 + ROWS, :], in_sem.at[0])
    load_v = load(ocean_v, F.at[2 * LEV : 3 * LEV, 8 : 8 + ROWS, :], in_sem.at[1])
    barrier = pltpu.get_barrier_semaphore()

    def greet(target):
        pl.semaphore_signal(barrier, inc=1, device_id=target, device_id_type=MESH)

    greet(at(east, gy))
    greet(at(west, gy))

    @pl.when(has_north)
    def _():
        for block in (me, east, west):
            greet(at(block, gy + 1))

    @pl.when(has_south)
    def _():
        for block in (me, east, west):
            greet(at(block, gy - 1))

    @pl.when(is_top)
    def _():
        for _, block, own, _ in strips:
            if own:

                @pl.when(block != me)
                def _(block=block):
                    greet(at(block, gy))
            else:
                greet(at(block, gy))

    small = [
        load(ocean_mask, OM, in_sem.at[2]),
        load(remap_in, remap, in_sem.at[4]),
        load(diffusivity_in, diffusivity, in_sem.at[5]),
        load(viscosity_in, viscosity, in_sem.at[6]),
        load(fold_in, fold_partner, in_sem.at[7]),
        load(remap_in, remap_wide, in_sem.at[8]),
    ]
    ice_in = (ice_u, ice_v, ice_mass, ice_strength, ice_mask)

    def ice_place(i, half):
        rows = pl.ds(pl.multiple_of(TOP + HALF * half, 8), HALF)
        if i == 4:
            return IM.at[pl.ds(pl.multiple_of(HALF * half, 8), HALF), :]
        return X.at[i, rows, 0:COLS]

    mine = pl.ds(pl.multiple_of(COLS * comp, COLS), COLS)
    other = pl.ds(pl.multiple_of(COLS * (1 - comp), COLS), COLS)
    for i in range(5):
        load(ice_in[i].at[:, mine], ice_place(i, comp), ice_sem.at[0])

    first8, last8 = slice(TOP, TOP + 8), slice(TOP + ROWS - 8, TOP + ROWS)
    south8, north8 = slice(TOP - 8, TOP), slice(TOP + ROWS, TOP + ROWS + 8)

    @pl.when(jnp.logical_not(has_south))
    def _():
        X[:, south8, 0:COLS] = jnp.zeros((NF, 8, COLS), jnp.float32)
        EBS[...] = jnp.zeros((8, COLS), jnp.float32)
        WBS[...] = jnp.zeros((8, COLS), jnp.float32)
        SR[...] = jnp.zeros((3 * LEV, COLS), jnp.float32)
        SK[...] = jnp.zeros((8, COLS), jnp.float32)

    @pl.when(is_top)
    def _():
        X[:, north8, 0:COLS] = jnp.zeros((NF, 8, COLS), jnp.float32)
        EBN[...] = jnp.zeros((8, COLS), jnp.float32)
        WBN[...] = jnp.zeros((8, COLS), jnp.float32)

    outer = jnp.zeros((NF, 8, 2 * COLS), jnp.float32)
    X[:, 0:8, :] = outer
    X[:, 104:112, :] = outer
    AB[...] = jnp.zeros((2, 112, 2 * COLS), jnp.float32)

    count = 2 + 3 * has_north.astype(jnp.int32) + 3 * has_south.astype(jnp.int32)
    strip_count = 0
    for _, block, own, _ in strips:
        strip_count = strip_count + ((block != me).astype(jnp.int32) if own else 1)
    count = count + is_top.astype(jnp.int32) * strip_count
    pl.semaphore_wait(barrier, count)

    def send(src, dst, send_sem, recv_sem, target):
        copy = pltpu.make_async_remote_copy(
            src_ref=src,
            dst_ref=dst,
            send_sem=send_sem,
            recv_sem=recv_sem,
            device_id=target,
            device_id_type=MESH,
        )
        return copy

    for i in range(5):
        send(ice_in[i].at[:, other], ice_place(i, comp), ice_send.at[0], ice_recv.at[0], partner).start()
    ice_all = X.at[0:5, TOP : TOP + HALF, 0:COLS]
    ice_away = send(ice_all, ice_all, ice_send.at[0], ice_recv.at[0], partner)

    load_t = load(tracer, F.at[0:LEV, 8 : 8 + ROWS, :], in_sem.at[3])
    lane = lax.broadcasted_iota(jnp.int32, (1, COLS), 1)
    even = (lane & 1) == 0
    row8 = lax.broadcasted_iota(jnp.int32, (8, 1), 0)
    tile_rows = slice(TOP, TOP + ROWS)

    for copy in small:
        copy.wait()
    sea = OM[...].astype(jnp.float32)
    F[SEA, 8 : 8 + ROWS, :] = sea
    for i, copy in ((0, load_u), (1, load_v)):
        copy.wait()

        def level(l, sums, i=i):
            weighted = remap[0, l] * F[LEV * (i + 1) + l, 8 : 8 + ROWS, :]
            return sums[0] + weighted, sums[1] + viscosity[l] * weighted

        zero = jnp.zeros((ROWS, COLS), jnp.float32)
        base, spread = lax.fori_loop(0, LEV, level, (zero, zero), unroll=4)
        X[5 + i, tile_rows, 0:COLS] = base
        F[SEA + 1 + i, 8 : 8 + ROWS, :] = spread

    first = [(3 * t + p, SEA + p, slice(8 + 8 * t, 16 + 8 * t)) for t in range(ROWS // 8) for p in range(3)]
    packed = jnp.zeros((8, COLS), jnp.float32)
    for m, f, rows in first:
        packed = jnp.where((lane >> 1) == m, pltpu.roll(F[f, rows, :], 2 * m + 1, 1), packed)
    CK[...] = packed
    for p in range(3):
        TK[p : p + 1, :] = F[SEA + p, 87:88, :]
        BK[p : p + 1, :] = F[SEA + p, 8:9, :]
    first_e = send(CK, RKW, first_send.at[0], first_recv.at[0], at(east, gy))
    first_w = send(CK, RKE, first_send.at[1], first_recv.at[1], at(west, gy))
    first_n = send(TK, SK, first_send.at[2], first_recv.at[2], at(me, gy + 1))
    first_s = send(BK, NK, first_send.at[3], first_recv.at[3], at(me, gy - 1))
    first_f = send(TK, NK, first_send.at[4], first_recv.at[4], at(mirror, gy))
    first_e.start()
    first_w.start()

    @pl.when(has_north)
    def _():
        first_n.start()

    @pl.when(has_south)
    def _():
        first_s.start()

    @pl.when(is_top)
    def _():
        first_f.start()

    load_t.wait()
    for f in range(3 * LEV):
        TR[f : f + 1, :] = F[f, 87:88, :]
        BR[f : f + 1, :] = F[f, 8:9, :]
    row_n = send(TR, SR, edge_send.at[2], edge_recv.at[2], at(me, gy + 1))
    row_s = send(BR, NR, edge_send.at[3], edge_recv.at[3], at(me, gy - 1))
    row_f = send(TR, NR, edge_send.at[4], edge_recv.at[4], at(mirror, gy))

    @pl.when(has_north)
    def _():
        row_n.start()

    @pl.when(has_south)
    def _():
        row_s.start()

    @pl.when(is_top)
    def _():
        row_f.start()

    def pack(f, packed):
        return jnp.where((lane >> 1) == f, pltpu.roll(F[f, 8 : 8 + ROWS, :], 2 * f + 1, 1), packed)

    packed = lax.fori_loop(0, 3 * LEV, pack, jnp.zeros((ROWS, COLS), jnp.float32), unroll=3)
    CE[...] = jnp.where(even, packed[0:HALF], pltpu.roll(packed[HALF:ROWS], 1, 1))
    CW[...] = jnp.where(even, pltpu.roll(packed[HALF:ROWS], COLS - 1, 1), packed[0:HALF])
    col_to_e = send(CE, RW, edge_send.at[0], edge_recv.at[0], at(east, gy))
    col_to_w = send(CW, RE, edge_send.at[1], edge_recv.at[1], at(west, gy))
    col_to_e.start()
    col_to_w.start()

    lane2 = lax.broadcasted_iota(jnp.int32, (LEV, LEV * LEV), 1)
    weights = jnp.zeros((LEV, LEV * LEV), jnp.float32)
    for l in range(LEV):
        weights = jnp.where((lane2 >> 4) == l, remap_wide[:, l : l + 1], weights)
    high = weights.astype(jnp.bfloat16).astype(jnp.float32)
    low = weights - high
    diagonal = (lane2 & 15) == lax.broadcasted_iota(jnp.int32, (LEV, LEV * LEV), 0)
    for k in range(LEV):
        rows = slice(LEV * k, LEV * (k + 1))
        high_k = jnp.where(diagonal, high[k : k + 1], 0.0).astype(jnp.bfloat16)
        KK[rows, 0:256] = high_k
        KK[rows, 256:512] = jnp.where(diagonal, low[k : k + 1], 0.0).astype(jnp.bfloat16)
        KK[rows, 512:768] = high_k

    first_e.wait()
    first_w.wait()

    @pl.when(has_north)
    def _():
        first_n.wait_send()
        first_s.wait_recv()

    @pl.when(has_south)
    def _():
        first_s.wait_send()
        first_n.wait_recv()

    inside_here = fold_partner[...] - COLS * mirror

    @pl.when(is_top)
    def _():
        first_f.wait()
        inside = jnp.broadcast_to(inside_here, (8, COLS))
        taken = jnp.take_along_axis(NK[...], inside, axis=1, mode="promise_in_bounds")
        NK[...] = jnp.where(row8 == 0, taken, -taken)

    GK[...] = jnp.where(even, pltpu.roll(RKE[...], COLS - 1, 1), pltpu.roll(RKW[...], 1, 1))
    for p in range(3):
        F[SEA + p, 88:89, :] = NK[p : p + 1, :]
        F[SEA + p, 7:8, :] = SK[p : p + 1, :]

    def sides_of(f, edges):
        value = F[f, 8 : 8 + ROWS, :]
        to_east = jnp.where(lane == COLS - 1, edges, pltpu.roll(value, COLS - 1, 1))
        to_west = jnp.where(lane == 0, edges, pltpu.roll(value, 1, 1))
        return value, to_east, to_west, F[f, 9 : 9 + ROWS, :], F[f, 7 : 7 + ROWS, :]

    def first_edges(f):
        return jnp.concatenate([pltpu.roll(GK[...], COLS - 1 - 2 * m, 1) for m, g, _ in first if g == f], axis=0)

    def lap(f, edges):
        value, to_east, to_west, to_north, to_south = sides_of(f, edges)
        total = MK[0] * to_east + MK[1] * to_west + MK[2] * to_north + MK[3] * to_south
        return value, total - MK[4] * value

    seas = sides_of(SEA, first_edges(SEA))
    degree = jnp.zeros((ROWS, COLS), jnp.float32)
    for i in range(4):
        weight = seas[0] * seas[i + 1]
        MK[i] = weight
        degree = degree + weight
    MK[4] = degree
    for i in range(2):
        f = SEA + 1 + i
        X[5 + i, tile_rows, 0:COLS] = X[5 + i, tile_rows, 0:COLS] + lap(f, first_edges(f))[1]

    pltpu.make_async_copy(ice_all, ice_all, ice_sem.at[0]).wait()
    ice_away.wait_recv()
    X[4, tile_rows, 0:COLS] = IM[...].astype(jnp.float32)


    def rim_pack(f, packed):
        south_half, north_half = X[f, TOP : TOP + HALF, 0:COLS], X[f, TOP + HALF : TOP + ROWS, 0:COLS]
        group = lane >> 3
        new = []
        for edge, old in ((8, packed[0]), (0, packed[1])):
            kept = jnp.where(group == f, pltpu.roll(south_half, 8 * f + edge, 1), old)
            new.append(jnp.where(group == f + 8, pltpu.roll(north_half, 64 + 8 * f + edge, 1), kept))
        return tuple(new)

    zero = jnp.zeros((HALF, COLS), jnp.float32)
    pack_e, pack_w = lax.fori_loop(0, NF, rim_pack, (zero, zero), unroll=7)
    PE[...] = pack_e
    PW[...] = pack_w
    to_e = send(PE, WB, rim_send.at[0], rim_recv.at[0], at(east, gy))
    to_w = send(PW, EB, rim_send.at[1], rim_recv.at[1], at(west, gy))
    to_n = [
        send(X.at[:, last8, 0:COLS], X.at[:, south8, 0:COLS], rim_send.at[2], rim_recv.at[2], at(me, gy + 1)),
        send(PE.at[HALF - 8 : HALF], WBS, rim_send.at[3], rim_recv.at[3], at(east, gy + 1)),
        send(PW.at[HALF - 8 : HALF], EBS, rim_send.at[4], rim_recv.at[4], at(west, gy + 1)),
    ]
    to_s = [
        send(X.at[:, first8, 0:COLS], X.at[:, north8, 0:COLS], rim_send.at[5], rim_recv.at[5], at(me, gy - 1)),
        send(PE.at[0:8], WBN, rim_send.at[6], rim_recv.at[6], at(east, gy - 1)),
        send(PW.at[0:8], EBN, rim_send.at[7], rim_recv.at[7], at(west, gy - 1)),
    ]

    def strip_ends(src, dst, slot, rows):
        kept = slice(8 - rows, 8)
        return src.at[:, kept, :], dst.at[:, kept, COLS * slot : COLS * (slot + 1)]

    def strip_copy(again, slot, block, own, rows):
        src, dst = strip_ends(SS2, S2, slot, rows) if again else strip_ends(SS, S, slot, rows)
        sent, received = (again_send, again_recv) if again else (strip_send, strip_recv)
        return send(src, dst, sent.at[slot if own else 0], received.at[0], at(block, gy))

    def strips_start(again):
        for slot, block, own, rows in strips:
            if own:

                @pl.when(block != me)
                def _(slot=slot, block=block, rows=rows):
                    strip_copy(again, slot, block, True, rows).start()

                @pl.when(block == me)
                def _(slot=slot, rows=rows):
                    src, dst = strip_ends(SS2, S2, slot, rows) if again else strip_ends(SS, S, slot, rows)
                    pltpu.make_async_copy(src, dst, (again_recv if again else strip_recv).at[0]).start()
            else:
                strip_copy(again, slot, block, False, rows).start()

    def strips_all(again, rows):
        area = (S2 if again else S).at[:, 0:1, 0 : COLS * rows]
        sent, received = (again_send, again_recv) if again else (strip_send, strip_recv)
        return send(area, area, sent.at[0], received.at[0], partner)

    def strips_arrive(again):
        strips_all(again, sum(rows for _, _, _, rows in strips)).wait_recv()

    def strips_sent(again):
        strips_all(again, sum(rows for _, _, own, rows in strips if not own)).wait_send()
        for slot, block, own, rows in strips:
            if own:

                @pl.when(block != me)
                def _(slot=slot, block=block, rows=rows):
                    strip_copy(again, slot, block, True, rows).wait_send()

    middle = slice(COLS * REACH, COLS * (REACH + 1))

    to_e.start()
    to_w.start()

    @pl.when(has_north)
    def _():
        for copy in to_n:
            copy.start()

    @pl.when(has_south)
    def _():
        for copy in to_s:
            copy.start()

    @pl.when(is_top)
    def _():
        SS[0:NF] = X[0:NF, last8, 0:COLS]
        SS[NF] = jnp.broadcast_to(inside_here.astype(jnp.float32), (8, COLS))
        S[:, :, middle] = SS[...]
        strips_start(False)

    col_to_e.wait()
    col_to_w.wait()

    @pl.when(has_north)
    def _():
        row_n.wait_send()
        row_s.wait_recv()

    @pl.when(has_south)
    def _():
        row_s.wait_send()
        row_n.wait_recv()

    @pl.when(is_top)
    def _():
        row_f.wait()
        inside = jnp.broadcast_to(inside_here, (8, COLS))
        for r in range(0, 3 * LEV, 8):
            taken = jnp.take_along_axis(NR[r : r + 8, :], inside, axis=1, mode="promise_in_bounds")
            NR[r : r + 8, :] = taken if r < LEV else -taken

    for f in range(3 * LEV):
        F[f, 88:89, :] = NR[f : f + 1, :]
        F[f, 7:8, :] = SR[f : f + 1, :]
    GE[0:HALF] = jnp.where(even, pltpu.roll(RE[...], COLS - 1, 1), pltpu.roll(RW[...], 1, 1))
    GE[HALF:ROWS] = jnp.where(even, RE[...], RW[...])

    def diffuse(f, carry):
        coefficient = jnp.where(f < LEV, diffusivity[f & (LEV - 1)], viscosity[f & (LEV - 1)])
        value, spread = lap(f, pltpu.roll(GE[...], COLS - 1 - 2 * f, 1))
        new = value + coefficient * spread
        high = new.astype(jnp.bfloat16)
        DH[f] = high
        DL[f] = (new - high.astype(jnp.float32)).astype(jnp.bfloat16)
        return carry

    lax.fori_loop(0, 2 * LEV, diffuse, 0, unroll=4)

    to_e.wait()
    to_w.wait()

    @pl.when(has_north)
    def _():
        for copy in to_n:
            copy.wait_send()
        for copy in to_s:
            copy.wait_recv()

    @pl.when(has_south)
    def _():
        for copy in to_s:
            copy.wait_send()
        for copy in to_n:
            copy.wait_recv()

    def rim_unpack(f, carry):
        def put(rows, e, w, half):
            from_e = pltpu.roll(e, lax.rem(COLS + half - 8 * f, COLS), 1)
            from_w = pltpu.roll(w, lax.rem(2 * COLS - 8 + half - 8 * f, COLS), 1)
            X[f, rows, COLS : 2 * COLS] = jnp.where(
                lane < 8, from_e, jnp.where(lane >= COLS - 8, from_w, 0.0)
            )

        put(slice(TOP, TOP + HALF), EB[...], WB[...], 0)
        put(slice(TOP + HALF, TOP + ROWS), EB[...], WB[...], 64)
        put(slice(TOP - 8, TOP), EBS[...], WBS[...], 64)
        put(slice(TOP + ROWS, TOP + ROWS + 8), EBN[...], WBN[...], 0)
        return carry

    lax.fori_loop(0, NF, rim_unpack, 0, unroll=7)

    def inside_of(i):
        return IDX[:, COLS * i : COLS * (i + 1)]

    def fold_block(ref, f, i, sign):
        j = BLOCKS - 1 - i
        value = ref[f, :, COLS * j : COLS * (j + 1)]
        taken = jnp.take_along_axis(value, inside_of(i), axis=1, mode="promise_in_bounds")
        return taken if sign > 0 else -taken

    def close_top(ref, f, strip_ref, sf, sign):
        own = fold_block(strip_ref, sf, REACH, sign)
        to_the_e = fold_block(strip_ref, sf, REACH + 1, sign)
        to_the_w = fold_block(strip_ref, sf, REACH - 1, sign)
        ref[f, 24:25, 0:COLS] = own[7:8]
        ref[f, 24:25, COLS : 2 * COLS] = jnp.where(lane < COLS // 2, to_the_e, to_the_w)[7:8]

    def window(first, reach):
        middle = first + REACH
        low, high = middle - reach, middle + reach + 1
        wide_low, wide_high = max(low - 1, first), min(high + 1, first + SIDE)
        return low, high, wide_low, wide_high

    def strip_sides(ref, f, win, sign):
        low, high, wide_low, wide_high = win
        wide = ref[f, :, COLS * wide_low : COLS * wide_high]
        length = COLS * (wide_high - wide_low)
        cut = slice(COLS * (low - wide_low), COLS * (high - wide_low))
        value = wide[:, cut]
        to_east = pltpu.roll(wide, length - 1, 1)[:, cut]
        to_west = pltpu.roll(wide, 1, 1)[:, cut]
        folded = jnp.concatenate([fold_block(ref, f, i, sign) for i in range(low, high)], axis=1)
        to_north = jnp.where(row8 == 7, folded, pltpu.roll(value, 7, 0))
        to_south = pltpu.roll(value, 1, 0)
        return value, to_east, to_west, to_north, to_south

    def windows(left):
        found = []
        if left in OWN_REACH:
            found.append(window(0, OWN_REACH[left]))
        if left in MIRROR_REACH:
            found.append(window(SIDE, MIRROR_REACH[left]))
        return found

    SHARE = STEP_SIZE / (1.0 + STEP_SIZE)
    KEEP = 1.0 / (1.0 + STEP_SIZE)

    def ready(ref, rows, cols):
        present = ref[4, rows, cols]
        ref[5, rows, cols] = SHARE * present * ref[5, rows, cols]
        ref[6, rows, cols] = SHARE * present * ref[6, rows, cols]
        mass = ref[2, rows, cols]
        ref[2, rows, cols] = 0.5 * SHARE * present / jnp.where(mass > 0.0, mass, 1.0)
        ref[4, rows, cols] = KEEP * present
        ref[3, rows, cols] = ref[3, rows, cols] * (RELAX / (1.0 + RELAX))

    def main_sides(ref, f, start, size):
        value = ref[f, start : start + size, :]
        return (
            value,
            pltpu.roll(value, 2 * COLS - 1, 1),
            pltpu.roll(value, 1, 1),
            ref[f, start + 1 : start + size + 1, :],
            ref[f, start - 1 : start + size - 1, :],
        )

    CHUNK = 24
    chunks = range(8, 8 + SPAN, CHUNK)

    def stress(u, v, third, old):
        twice_d = (u[1] - u[2]) + (v[3] - v[4])
        twice_h = (u[3] - u[4]) + (v[1] - v[2])
        viscous = third * lax.rsqrt(twice_d * twice_d + 0.25 * (twice_h * twice_h) + 0.04)
        a = viscous * twice_d - third
        b = viscous * twice_h
        if old is not None:
            a = a + old[0] * (1.0 / (1.0 + RELAX))
            b = b + old[1] * (1.0 / (1.0 + RELAX))
        return a, b

    def push(ref, vel, rows, cols, a, b):
        keep, mobility = ref[4, rows, cols], ref[2, rows, cols]
        new_u = keep * vel[0, rows, cols] + mobility * ((a[1] - a[2]) + (b[3] - b[4])) + ref[5, rows, cols]
        new_v = keep * vel[1, rows, cols] + mobility * ((b[1] - b[2]) + (a[3] - a[4])) + ref[6, rows, cols]
        vel[0, rows, cols] = new_u
        vel[1, rows, cols] = new_v

    every = slice(0, 8)

    def chunk_stress(vel, sig, start, first=False):
        rows = slice(start, start + CHUNK)
        u, v = main_sides(vel, 0, start, CHUNK), main_sides(vel, 1, start, CHUNK)
        old = None if first else (sig[0, rows, :], sig[1, rows, :])
        sig[0, rows, :], sig[1, rows, :] = stress(u, v, vel[3, rows, :], old)

    def chunk_push(vel, sig, start):
        a, b = main_sides(sig, 0, start, CHUNK), main_sides(sig, 1, start, CHUNK)
        push(vel, vel, slice(start, start + CHUNK), slice(0, 2 * COLS), a, b)

    def tile_cycle(cycle, carry):
        for start in chunks:
            chunk_stress(X, AB, start)
        for start in chunks:
            chunk_push(X, AB, start)
        return carry

    low_piece, high_piece, low_tile, high_tile = slice(8, 16), slice(16, 24), slice(80, 88), slice(88, 96)

    def top_cycles(cycles):
        vel, sig, i_a, i_b = (S, SAB, 0, 1) if cycles[0] == 0 else (S2, S2, 2, 3)
        for cycle in cycles:
            left = 3 if cycle == cycles[0] else 1
            close_top(XT, 0, vel, 0, -1)
            close_top(XT, 1, vel, 1, -1)
            for win in windows(left):
                cols = slice(COLS * win[0], COLS * win[1])
                u, v = strip_sides(vel, 0, win, -1), strip_sides(vel, 1, win, -1)
                old = (sig[i_a, :, cols], sig[i_b, :, cols]) if cycle else None
                sig[i_a, :, cols], sig[i_b, :, cols] = stress(u, v, S[3, :, cols], old)
            chunk_stress(XT, ABT, 8, cycle == 0)
            close_top(ABT, 0, sig, i_a, 1)
            close_top(ABT, 1, sig, i_b, 1)
            for win in windows(left - 1):
                cols = slice(COLS * win[0], COLS * win[1])
                push(S, vel, every, cols, strip_sides(sig, i_a, win, 1), strip_sides(sig, i_b, win, 1))
            chunk_push(XT, ABT, 8)

    for start in chunks:
        ready(X, slice(start, start + CHUNK), slice(0, 2 * COLS))

    @pl.when(is_top)
    def _():
        XT[...] = X[:, 72:112, :]
        ABT[...] = jnp.zeros((2, 40, 2 * COLS), jnp.float32)

    lax.fori_loop(0, 2, tile_cycle, 0)

    @pl.when(is_top)
    def _():
        strips_arrive(False)
        IDX[...] = jnp.broadcast_to(S[NF, 7:8, 0 : BLOCKS * COLS], IDX.shape).astype(jnp.int32)
        ready(S, every, slice(0, BLOCKS * COLS))
        top_cycles((0, 1))
        SS2[0:2] = XT[0:2, high_piece, 0:COLS]
        SS2[2:4] = ABT[:, high_piece, 0:COLS]
        strips_start(True)
        S2[:, :, middle] = SS2[...]
        X[0:2, high_tile, :] = XT[0:2, high_piece, :]
        AB[:, high_tile, :] = ABT[:, high_piece, :]
        XT[0:2, low_piece, :] = X[0:2, low_tile, :]
        ABT[:, low_piece, :] = AB[:, low_tile, :]

    lax.fori_loop(0, 2, tile_cycle, 0)

    here = pl.ds(pl.multiple_of(TOP + HALF * comp, 8), HALF)

    def vel_part(i, low, rows):
        away = pl.ds(pl.multiple_of(TOP + HALF * (1 - comp) + low, 8), rows)
        return send(
            X.at[0:2, away, 0:COLS], new_ice.at[:, low : low + rows, mine], vel_send.at[i], vel_recv.at[i], partner
        )

    vel_away = [vel_part(0, 0, HALF - 8), vel_part(1, HALF - 8, 8)]
    vel_here = pltpu.make_async_copy(X.at[0:2, here, 0:COLS], new_ice.at[:, :, mine], out_sem.at[3])

    vel_away[0].start()

    @pl.when(jnp.logical_not(is_top))
    def _():
        vel_away[1].start()
        vel_here.start()

    def regrid(g):
        planes = pl.ds(g * LEV, LEV)
        pieces = range(0, ROWS, LEV)
        high = jnp.concatenate([DH[planes, r : r + LEV, :].reshape(LEV * LEV, COLS) for r in pieces], axis=1)
        low = jnp.concatenate([DL[planes, r : r + LEV, :].reshape(LEV * LEV, COLS) for r in pieces], axis=1)
        new = jnp.dot(KK[...], jnp.concatenate([high, high, low], axis=0), preferred_element_type=jnp.float32)
        for i, r in enumerate(pieces):
            O[planes, r : r + LEV, :] = new[:, COLS * i : COLS * (i + 1)].reshape(LEV, LEV, COLS)

    @pl.when(is_top)
    def _():
        def early(g, carry):
            regrid(g)
            return carry

        lax.fori_loop(0, 2, early, 0)
        strips_arrive(True)
        to_the_e = S2[0:2, 7:8, COLS * (REACH + 1) : COLS * (REACH + 2)]
        to_the_w = S2[0:2, 7:8, COLS * (REACH - 1) : COLS * REACH]
        XT[0:2, 23:24, COLS : 2 * COLS] = jnp.where(lane < COLS // 2, to_the_e, to_the_w)
        top_cycles((2, 3))
        X[0:2, high_tile, :] = XT[0:2, high_piece, :]
        vel_away[1].start()
        vel_here.start()

    lax.fori_loop(2 * LEV, 3 * LEV, diffuse, 0, unroll=4)

    outs = (new_tracer, new_ocean_u, new_ocean_v)

    stores = [
        pltpu.make_async_copy(O.at[g * LEV : (g + 1) * LEV], outs[g], out_sem.at[g]) for g in range(3)
    ]

    def finish(g, carry):
        @pl.when(jnp.logical_not(is_top) | (g == 2))
        def _():
            regrid(g)

        for i in range(3):

            @pl.when(g == i)
            def _(i=i):
                if i:
                    tau = X[i - 1, tile_rows, 0:COLS] - X[4 + i, tile_rows, 0:COLS] * (1.0 / SHARE)
                    O[i * LEV] = O[i * LEV] + COUPLE * (F[SEA, 8 : 8 + ROWS, :] * tau)
                stores[i].start()

        return carry

    lax.fori_loop(0, 3, finish, 0)

    @pl.when(is_top)
    def _():
        strips_sent(False)
        strips_sent(True)

    ice_away.wait_send()
    for copy in vel_away + [vel_here] + stores:
        copy.wait()


def deliver(tracer, ocean_u, ocean_v, ice, new_tracer, new_ocean_u, new_ocean_v, new_ice_u, new_ice_v, sems):
    pairs = [
        (tracer, new_tracer),
        (ocean_u, new_ocean_u),
        (ocean_v, new_ocean_v),
        (ice.at[0], new_ice_u),
        (ice.at[1], new_ice_v),
    ]
    copies = [pltpu.make_async_copy(src, dst, sems.at[i]) for i, (src, dst) in enumerate(pairs)]
    for copy in copies:
        copy.start()
    for copy in copies:
        copy.wait()


def solution(mesh):
    blocks = mesh.shape["gx"] * 2
    gys = mesh.shape["gy"]
    ocean = P(None, "gy", ("gx", "comp"))
    flat = P("gy", ("gx", "comp"))
    ice = P(("gy", "comp"), "gx")
    in_specs = (ocean, ocean, ocean, flat, P(), P(), P(), P(("gx", "comp")), ice, ice, ice, ice, ice)
    out_specs = (ocean, ocean, ocean, ice, ice)

    def body(tracer, ocean_u, ocean_v, ocean_mask, diffusivity, viscosity, remap, fold_partner, *ice_fields):
        f32 = jnp.float32
        anywhere = pl.BlockSpec(memory_space=pl.ANY)
        main_memory = pl.BlockSpec(memory_space=pltpu.HBM)
        vmem = pltpu.VMEM
        dma = pltpu.SemaphoreType.DMA
        ocean_shape = jax.ShapeDtypeStruct(tracer.shape, f32)
        ice_shape = jax.ShapeDtypeStruct(ice_fields[0].shape, f32)

        def step(*args):
            kernel(blocks, gys, *args)

        shapes = (ocean_shape, ocean_shape, ocean_shape, ice_shape, ice_shape)
        results = pl.pallas_call(
            step,
            out_shape=(*shapes[:3], jax.ShapeDtypeStruct((2, *ice_fields[0].shape), f32)),
            in_specs=[main_memory] * 13,
            out_specs=(anywhere,) * 4,
            scratch_shapes=[
                vmem((PLANES, 96, COLS), f32),
                vmem((3 * LEV, ROWS, COLS), jnp.bfloat16),
                vmem((3 * LEV, ROWS, COLS), jnp.bfloat16),
                vmem((LEV * LEV, 3 * LEV * LEV), jnp.bfloat16),
                vmem((3 * LEV, ROWS, COLS), f32),
                vmem((NF, 112, 2 * COLS), f32),
                vmem((2, 112, 2 * COLS), f32),
                vmem((NF, 40, 2 * COLS), f32),
                vmem((2, 40, 2 * COLS), f32),
                vmem((NS, 8, 2 * BLOCKS * COLS), f32),
                vmem((2, 8, BLOCKS * COLS), f32),
                vmem((NS, 8, COLS), f32),
                vmem((4, 8, 2 * BLOCKS * COLS), f32),
                vmem((4, 8, COLS), f32),
                vmem((HALF, COLS), f32),
                vmem((HALF, COLS), f32),
                vmem((HALF, COLS), f32),
                vmem((HALF, COLS), f32),
                vmem((8, COLS), f32),
                vmem((8, COLS), f32),
                vmem((8, COLS), f32),
                vmem((8, COLS), f32),
                vmem((3 * LEV, COLS), f32),
                vmem((3 * LEV, COLS), f32),
                vmem((3 * LEV, COLS), f32),
                vmem((3 * LEV, COLS), f32),
                *[vmem((8, COLS), f32)] * 8,
                vmem((HALF, COLS), f32),
                vmem((HALF, COLS), f32),
                vmem((HALF, COLS), f32),
                vmem((HALF, COLS), f32),
                vmem((ROWS, COLS), f32),
                vmem((5, ROWS, COLS), f32),
                vmem((ROWS, COLS), jnp.int32),
                vmem((ROWS, COLS), jnp.int32),
                vmem((8, BLOCKS * COLS), jnp.int32),
                pltpu.SMEM((LEV,), f32),
                pltpu.SMEM((LEV,), f32),
                pltpu.SMEM((LEV, LEV), f32),
                vmem((LEV, LEV), f32),
                vmem((1, COLS), jnp.int32),
                dma((9,)),
                dma((5,)),
                dma((5,)),
                dma((5,)),
                dma((5,)),
                dma((5,)),
                dma((5,)),
                dma((5,)),
                dma((8,)),
                dma((8,)),
                dma((BLOCKS,)),
                dma((BLOCKS,)),
                dma((BLOCKS,)),
                dma((BLOCKS,)),
                dma((5,)),
                dma((2,)),
                dma((2,)),
            ],
            compiler_params=pltpu.CompilerParams(
                collective_id=0, has_side_effects=True, vmem_limit_bytes=32 * 1024 * 1024
            ),
        )(
            *[
                pltpu.with_memory_space_constraint(value, pltpu.HBM)
                for value in (
                    tracer,
                    ocean_u,
                    ocean_v,
                    ocean_mask,
                    diffusivity,
                    viscosity,
                    remap,
                    fold_partner.reshape(1, COLS),
                    *ice_fields,
                )
            ]
        )
        return pl.pallas_call(
            deliver,
            out_shape=shapes,
            in_specs=[anywhere] * 4,
            out_specs=(main_memory,) * 5,
            scratch_shapes=[dma((5,))],
            compiler_params=pltpu.CompilerParams(vmem_limit_bytes=1024 * 1024),
        )(*results)

    return jax.shard_map(body, mesh=mesh, in_specs=in_specs, out_specs=out_specs, check_vma=False)
```

```python
import jax
import jax.numpy as jnp
from jax import lax
from jax.experimental import pallas as pl
from jax.experimental.pallas import tpu as pltpu
from jax.sharding import PartitionSpec as P

ITERS = 4
RELAX = 0.5
STEP_SIZE = 0.3
COUPLE = 0.5
MESH = pl.DeviceIdType.MESH

LEV = 16
ROWS = 80
HALF = 40
COLS = 128
NF = 7
NS = NF + 1
REACH = 2
SIDE = 2 * REACH + 1
BLOCKS = 2 * SIDE
TOP = 16
SPAN = 96
OWN_REACH = {2: 0, 3: 1}
MIRROR_REACH = {1: 0, 2: 1, 3: 2}
OWN_ROWS = (8, 2, 1)
MIRROR_ROWS = (4, 3, 2)
SEA = 3 * LEV
PLANES = SEA + 3


def kernel(
    blocks,
    gys,
    tracer,
    ocean_u,
    ocean_v,
    ocean_mask,
    diffusivity_in,
    viscosity_in,
    remap_in,
    fold_in,
    ice_u,
    ice_v,
    ice_mass,
    ice_strength,
    ice_mask,
    new_tracer,
    new_ocean_u,
    new_ocean_v,
    new_ice,
    F,
    DH,
    DL,
    KK,
    O,
    X,
    AB,
    XT,
    ABT,
    S,
    SAB,
    SS,
    S2,
    SS2,
    FR,
    FO,
    PE,
    PW,
    EB,
    WB,
    EBS,
    WBS,
    EBN,
    WBN,
    TR,
    BR,
    NR,
    SR,
    CK,
    RKE,
    RKW,
    GK,
    TK,
    BK,
    NK,
    SK,
    CE,
    CW,
    RE,
    RW,
    GE,
    MK,
    OM,
    IM,
    IDX,
    diffusivity,
    viscosity,
    remap,
    remap_wide,
    fold_partner,
    in_sem,
    ice_sem,
    ice_send,
    ice_recv,
    edge_send,
    edge_recv,
    first_send,
    first_recv,
    rim_send,
    rim_recv,
    strip_send,
    strip_recv,
    again_send,
    again_recv,
    out_sem,
    vel_send,
    vel_recv,
):
    gx, gy, comp = lax.axis_index("gx"), lax.axis_index("gy"), lax.axis_index("comp")
    me = gx * 2 + comp
    has_north = gy < gys - 1
    has_south = gy > 0
    is_top = gy == gys - 1

    def at(block, row):
        return {"gx": block // 2, "gy": row, "comp": lax.rem(block, 2)}

    def wrap(block):
        return lax.rem(block + 2 * blocks, blocks)

    east, west, mirror = wrap(me + 1), wrap(me - 1), blocks - 1 - me
    partner = at(gx * 2 + 1 - comp, gy)

    strips = [(SIDE + REACH, mirror, False, MIRROR_ROWS[0])]
    for d in (1, -1, 2, -2):
        strips.append((SIDE + REACH + d, wrap(mirror + d), d % 2 == 1, MIRROR_ROWS[abs(d)]))
        strips.append((REACH + d, wrap(me - d), False, OWN_ROWS[abs(d)]))

    def load(src, dst, sem):
        copy = pltpu.make_async_copy(src, dst, sem)
        copy.start()
        return copy

    load_u = load(ocean_u, F.at[LEV : 2 * LEV, 8 : 8 + ROWS, :], in_sem.at[0])
    load_v = load(ocean_v, F.at[2 * LEV : 3 * LEV, 8 : 8 + ROWS, :], in_sem.at[1])
    barrier = pltpu.get_barrier_semaphore()

    def greet(target):
        pl.semaphore_signal(barrier, inc=1, device_id=target, device_id_type=MESH)

    greet(at(east, gy))
    greet(at(west, gy))

    @pl.when(has_north)
    def _():
        for block in (me, east, west):
            greet(at(block, gy + 1))

    @pl.when(has_south)
    def _():
        for block in (me, east, west):
            greet(at(block, gy - 1))

    @pl.when(is_top)
    def _():
        for _, block, own, _ in strips:
            if own:

                @pl.when(block != me)
                def _(block=block):
                    greet(at(block, gy))
            else:
                greet(at(block, gy))

    small = [
        load(ocean_mask, OM, in_sem.at[2]),
        load(remap_in, remap, in_sem.at[4]),
        load(diffusivity_in, diffusivity, in_sem.at[5]),
        load(viscosity_in, viscosity, in_sem.at[6]),
        load(fold_in, fold_partner, in_sem.at[7]),
        load(remap_in, remap_wide, in_sem.at[8]),
    ]
    ice_in = (ice_u, ice_v, ice_mass, ice_strength, ice_mask)

    def ice_place(i, half):
        rows = pl.ds(pl.multiple_of(TOP + HALF * half, 8), HALF)
        if i == 4:
            return IM.at[pl.ds(pl.multiple_of(HALF * half, 8), HALF), :]
        return X.at[i, rows, 0:COLS]

    mine = pl.ds(pl.multiple_of(COLS * comp, COLS), COLS)
    other = pl.ds(pl.multiple_of(COLS * (1 - comp), COLS), COLS)
    for i in range(5):
        load(ice_in[i].at[:, mine], ice_place(i, comp), ice_sem.at[0])

    first8, last8 = slice(TOP, TOP + 8), slice(TOP + ROWS - 8, TOP + ROWS)
    south8, north8 = slice(TOP - 8, TOP), slice(TOP + ROWS, TOP + ROWS + 8)

    @pl.when(jnp.logical_not(has_south))
    def _():
        X[:, south8, 0:COLS] = jnp.zeros((NF, 8, COLS), jnp.float32)
        EBS[...] = jnp.zeros((8, COLS), jnp.float32)
        WBS[...] = jnp.zeros((8, COLS), jnp.float32)
        SR[...] = jnp.zeros((3 * LEV, COLS), jnp.float32)
        SK[...] = jnp.zeros((8, COLS), jnp.float32)

    @pl.when(is_top)
    def _():
        X[:, north8, 0:COLS] = jnp.zeros((NF, 8, COLS), jnp.float32)
        EBN[...] = jnp.zeros((8, COLS), jnp.float32)
        WBN[...] = jnp.zeros((8, COLS), jnp.float32)

    outer = jnp.zeros((NF, 8, 2 * COLS), jnp.float32)
    X[:, 0:8, :] = outer
    X[:, 104:112, :] = outer
    AB[...] = jnp.zeros((2, 112, 2 * COLS), jnp.float32)

    count = 2 + 3 * has_north.astype(jnp.int32) + 3 * has_south.astype(jnp.int32)
    strip_count = 0
    for _, block, own, _ in strips:
        strip_count = strip_count + ((block != me).astype(jnp.int32) if own else 1)
    count = count + is_top.astype(jnp.int32) * strip_count
    pl.semaphore_wait(barrier, count)

    def send(src, dst, send_sem, recv_sem, target):
        copy = pltpu.make_async_remote_copy(
            src_ref=src,
            dst_ref=dst,
            send_sem=send_sem,
            recv_sem=recv_sem,
            device_id=target,
            device_id_type=MESH,
        )
        return copy

    for i in range(5):
        send(ice_in[i].at[:, other], ice_place(i, comp), ice_send.at[0], ice_recv.at[0], partner).start()
    ice_all = X.at[0:5, TOP : TOP + HALF, 0:COLS]
    ice_away = send(ice_all, ice_all, ice_send.at[0], ice_recv.at[0], partner)

    load_t = load(tracer, F.at[0:LEV, 8 : 8 + ROWS, :], in_sem.at[3])
    lane = lax.broadcasted_iota(jnp.int32, (1, COLS), 1)
    even = (lane & 1) == 0
    row8 = lax.broadcasted_iota(jnp.int32, (8, 1), 0)
    tile_rows = slice(TOP, TOP + ROWS)

    for copy in small:
        copy.wait()
    sea = OM[...].astype(jnp.float32)
    F[SEA, 8 : 8 + ROWS, :] = sea
    for i, copy in ((0, load_u), (1, load_v)):
        copy.wait()

        def level(l, sums, i=i):
            weighted = remap[0, l] * F[LEV * (i + 1) + l, 8 : 8 + ROWS, :]
            return sums[0] + weighted, sums[1] + viscosity[l] * weighted

        zero = jnp.zeros((ROWS, COLS), jnp.float32)
        base, spread = lax.fori_loop(0, LEV, level, (zero, zero), unroll=4)
        X[5 + i, tile_rows, 0:COLS] = base
        F[SEA + 1 + i, 8 : 8 + ROWS, :] = spread

    first = [(3 * t + p, SEA + p, slice(8 + 8 * t, 16 + 8 * t)) for t in range(ROWS // 8) for p in range(3)]
    packed = jnp.zeros((8, COLS), jnp.float32)
    for m, f, rows in first:
        packed = jnp.where((lane >> 1) == m, pltpu.roll(F[f, rows, :], 2 * m + 1, 1), packed)
    CK[...] = packed
    for p in range(3):
        TK[p : p + 1, :] = F[SEA + p, 87:88, :]
        BK[p : p + 1, :] = F[SEA + p, 8:9, :]
    first_e = send(CK, RKW, first_send.at[0], first_recv.at[0], at(east, gy))
    first_w = send(CK, RKE, first_send.at[1], first_recv.at[1], at(west, gy))
    first_n = send(TK, SK, first_send.at[2], first_recv.at[2], at(me, gy + 1))
    first_s = send(BK, NK, first_send.at[3], first_recv.at[3], at(me, gy - 1))
    first_f = send(TK, NK, first_send.at[4], first_recv.at[4], at(mirror, gy))
    first_e.start()
    first_w.start()

    @pl.when(has_north)
    def _():
        first_n.start()

    @pl.when(has_south)
    def _():
        first_s.start()

    @pl.when(is_top)
    def _():
        first_f.start()

    load_t.wait()
    for f in range(3 * LEV):
        TR[f : f + 1, :] = F[f, 87:88, :]
        BR[f : f + 1, :] = F[f, 8:9, :]
    row_n = send(TR, SR, edge_send.at[2], edge_recv.at[2], at(me, gy + 1))
    row_s = send(BR, NR, edge_send.at[3], edge_recv.at[3], at(me, gy - 1))
    row_f = send(TR, NR, edge_send.at[4], edge_recv.at[4], at(mirror, gy))

    @pl.when(has_north)
    def _():
        row_n.start()

    @pl.when(has_south)
    def _():
        row_s.start()

    @pl.when(is_top)
    def _():
        row_f.start()

    def pack(f, packed):
        return jnp.where((lane >> 1) == f, pltpu.roll(F[f, 8 : 8 + ROWS, :], 2 * f + 1, 1), packed)

    packed = lax.fori_loop(0, 3 * LEV, pack, jnp.zeros((ROWS, COLS), jnp.float32), unroll=3)
    CE[...] = jnp.where(even, packed[0:HALF], pltpu.roll(packed[HALF:ROWS], 1, 1))
    CW[...] = jnp.where(even, pltpu.roll(packed[HALF:ROWS], COLS - 1, 1), packed[0:HALF])
    col_to_e = send(CE, RW, edge_send.at[0], edge_recv.at[0], at(east, gy))
    col_to_w = send(CW, RE, edge_send.at[1], edge_recv.at[1], at(west, gy))
    col_to_e.start()
    col_to_w.start()

    lane2 = lax.broadcasted_iota(jnp.int32, (LEV, LEV * LEV), 1)
    weights = jnp.zeros((LEV, LEV * LEV), jnp.float32)
    for l in range(LEV):
        weights = jnp.where((lane2 >> 4) == l, remap_wide[:, l : l + 1], weights)
    high = weights.astype(jnp.bfloat16).astype(jnp.float32)
    low = weights - high
    diagonal = (lane2 & 15) == lax.broadcasted_iota(jnp.int32, (LEV, LEV * LEV), 0)
    for k in range(LEV):
        rows = slice(LEV * k, LEV * (k + 1))
        high_k = jnp.where(diagonal, high[k : k + 1], 0.0).astype(jnp.bfloat16)
        KK[rows, 0:256] = high_k
        KK[rows, 256:512] = jnp.where(diagonal, low[k : k + 1], 0.0).astype(jnp.bfloat16)
        KK[rows, 512:768] = high_k

    first_e.wait()
    first_w.wait()

    @pl.when(has_north)
    def _():
        first_n.wait_send()
        first_s.wait_recv()

    @pl.when(has_south)
    def _():
        first_s.wait_send()
        first_n.wait_recv()

    inside_here = fold_partner[...] - COLS * mirror

    @pl.when(is_top)
    def _():
        first_f.wait()
        inside = jnp.broadcast_to(inside_here, (8, COLS))
        taken = jnp.take_along_axis(NK[...], inside, axis=1, mode="promise_in_bounds")
        NK[...] = jnp.where(row8 == 0, taken, -taken)

    GK[...] = jnp.where(even, pltpu.roll(RKE[...], COLS - 1, 1), pltpu.roll(RKW[...], 1, 1))
    for p in range(3):
        F[SEA + p, 88:89, :] = NK[p : p + 1, :]
        F[SEA + p, 7:8, :] = SK[p : p + 1, :]

    def sides_of(f, edges):
        value = F[f, 8 : 8 + ROWS, :]
        to_east = jnp.where(lane == COLS - 1, edges, pltpu.roll(value, COLS - 1, 1))
        to_west = jnp.where(lane == 0, edges, pltpu.roll(value, 1, 1))
        return value, to_east, to_west, F[f, 9 : 9 + ROWS, :], F[f, 7 : 7 + ROWS, :]

    def first_edges(f):
        return jnp.concatenate([pltpu.roll(GK[...], COLS - 1 - 2 * m, 1) for m, g, _ in first if g == f], axis=0)

    def lap(f, edges):
        value, to_east, to_west, to_north, to_south = sides_of(f, edges)
        total = MK[0] * to_east + MK[1] * to_west + MK[2] * to_north + MK[3] * to_south
        return value, total - MK[4] * value

    seas = sides_of(SEA, first_edges(SEA))
    degree = jnp.zeros((ROWS, COLS), jnp.float32)
    for i in range(4):
        weight = seas[0] * seas[i + 1]
        MK[i] = weight
        degree = degree + weight
    MK[4] = degree
    for i in range(2):
        f = SEA + 1 + i
        X[5 + i, tile_rows, 0:COLS] = X[5 + i, tile_rows, 0:COLS] + lap(f, first_edges(f))[1]

    pltpu.make_async_copy(ice_all, ice_all, ice_sem.at[0]).wait()
    ice_away.wait_recv()
    X[4, tile_rows, 0:COLS] = IM[...].astype(jnp.float32)


    def rim_pack(f, packed):
        south_half, north_half = X[f, TOP : TOP + HALF, 0:COLS], X[f, TOP + HALF : TOP + ROWS, 0:COLS]
        group = lane >> 3
        new = []
        for edge, old in ((8, packed[0]), (0, packed[1])):
            kept = jnp.where(group == f, pltpu.roll(south_half, 8 * f + edge, 1), old)
            new.append(jnp.where(group == f + 8, pltpu.roll(north_half, 64 + 8 * f + edge, 1), kept))
        return tuple(new)

    zero = jnp.zeros((HALF, COLS), jnp.float32)
    pack_e, pack_w = lax.fori_loop(0, NF, rim_pack, (zero, zero), unroll=7)
    PE[...] = pack_e
    PW[...] = pack_w
    to_e = send(PE, WB, rim_send.at[0], rim_recv.at[0], at(east, gy))
    to_w = send(PW, EB, rim_send.at[1], rim_recv.at[1], at(west, gy))
    to_n = [
        send(X.at[:, last8, 0:COLS], X.at[:, south8, 0:COLS], rim_send.at[2], rim_recv.at[2], at(me, gy + 1)),
        send(PE.at[HALF - 8 : HALF], WBS, rim_send.at[3], rim_recv.at[3], at(east, gy + 1)),
        send(PW.at[HALF - 8 : HALF], EBS, rim_send.at[4], rim_recv.at[4], at(west, gy + 1)),
    ]
    to_s = [
        send(X.at[:, first8, 0:COLS], X.at[:, north8, 0:COLS], rim_send.at[5], rim_recv.at[5], at(me, gy - 1)),
        send(PE.at[0:8], WBN, rim_send.at[6], rim_recv.at[6], at(east, gy - 1)),
        send(PW.at[0:8], EBN, rim_send.at[7], rim_recv.at[7], at(west, gy - 1)),
    ]

    def strip_ends(src, dst, slot, rows):
        kept = slice(8 - rows, 8)
        return src.at[:, kept, :], dst.at[:, kept, COLS * slot : COLS * (slot + 1)]

    def strip_copy(again, slot, block, own, rows):
        src, dst = strip_ends(SS2, S2, slot, rows) if again else strip_ends(SS, S, slot, rows)
        sent, received = (again_send, again_recv) if again else (strip_send, strip_recv)
        return send(src, dst, sent.at[slot if own else 0], received.at[0], at(block, gy))

    def strips_start(again):
        for slot, block, own, rows in strips:
            if own:

                @pl.when(block != me)
                def _(slot=slot, block=block, rows=rows):
                    strip_copy(again, slot, block, True, rows).start()

                @pl.when(block == me)
                def _(slot=slot, rows=rows):
                    src, dst = strip_ends(SS2, S2, slot, rows) if again else strip_ends(SS, S, slot, rows)
                    pltpu.make_async_copy(src, dst, (again_recv if again else strip_recv).at[0]).start()
            else:
                strip_copy(again, slot, block, False, rows).start()

    def strips_all(again, rows):
        area = (S2 if again else S).at[:, 0:1, 0 : COLS * rows]
        sent, received = (again_send, again_recv) if again else (strip_send, strip_recv)
        return send(area, area, sent.at[0], received.at[0], partner)

    def strips_arrive(again):
        strips_all(again, sum(rows for _, _, _, rows in strips)).wait_recv()

    def strips_sent(again):
        strips_all(again, sum(rows for _, _, own, rows in strips if not own)).wait_send()
        for slot, block, own, rows in strips:
            if own:

                @pl.when(block != me)
                def _(slot=slot, block=block, rows=rows):
                    strip_copy(again, slot, block, True, rows).wait_send()

    middle = slice(COLS * REACH, COLS * (REACH + 1))

    to_e.start()
    to_w.start()

    @pl.when(has_north)
    def _():
        for copy in to_n:
            copy.start()

    @pl.when(has_south)
    def _():
        for copy in to_s:
            copy.start()

    @pl.when(is_top)
    def _():
        SS[0:NF] = X[0:NF, last8, 0:COLS]
        SS[NF] = jnp.broadcast_to(inside_here.astype(jnp.float32), (8, COLS))
        S[:, :, middle] = SS[...]
        strips_start(False)

    col_to_e.wait()
    col_to_w.wait()

    @pl.when(has_north)
    def _():
        row_n.wait_send()
        row_s.wait_recv()

    @pl.when(has_south)
    def _():
        row_s.wait_send()
        row_n.wait_recv()

    @pl.when(is_top)
    def _():
        row_f.wait()
        inside = jnp.broadcast_to(inside_here, (8, COLS))
        for r in range(0, 3 * LEV, 8):
            taken = jnp.take_along_axis(NR[r : r + 8, :], inside, axis=1, mode="promise_in_bounds")
            NR[r : r + 8, :] = taken if r < LEV else -taken

    for f in range(3 * LEV):
        F[f, 88:89, :] = NR[f : f + 1, :]
        F[f, 7:8, :] = SR[f : f + 1, :]
    GE[0:HALF] = jnp.where(even, pltpu.roll(RE[...], COLS - 1, 1), pltpu.roll(RW[...], 1, 1))
    GE[HALF:ROWS] = jnp.where(even, RE[...], RW[...])

    def diffuse(f, carry):
        coefficient = jnp.where(f < LEV, diffusivity[f & (LEV - 1)], viscosity[f & (LEV - 1)])
        value, spread = lap(f, pltpu.roll(GE[...], COLS - 1 - 2 * f, 1))
        new = value + coefficient * spread
        high = new.astype(jnp.bfloat16)
        DH[f] = high
        DL[f] = (new - high.astype(jnp.float32)).astype(jnp.bfloat16)
        return carry

    lax.fori_loop(0, 2 * LEV, diffuse, 0, unroll=4)

    to_e.wait()
    to_w.wait()

    @pl.when(has_north)
    def _():
        for copy in to_n:
            copy.wait_send()
        for copy in to_s:
            copy.wait_recv()

    @pl.when(has_south)
    def _():
        for copy in to_s:
            copy.wait_send()
        for copy in to_n:
            copy.wait_recv()

    def rim_unpack(f, carry):
        def put(rows, e, w, half):
            from_e = pltpu.roll(e, lax.rem(COLS + half - 8 * f, COLS), 1)
            from_w = pltpu.roll(w, lax.rem(2 * COLS - 8 + half - 8 * f, COLS), 1)
            X[f, rows, COLS : 2 * COLS] = jnp.where(
                lane < 8, from_e, jnp.where(lane >= COLS - 8, from_w, 0.0)
            )

        put(slice(TOP, TOP + HALF), EB[...], WB[...], 0)
        put(slice(TOP + HALF, TOP + ROWS), EB[...], WB[...], 64)
        put(slice(TOP - 8, TOP), EBS[...], WBS[...], 64)
        put(slice(TOP + ROWS, TOP + ROWS + 8), EBN[...], WBN[...], 0)
        return carry

    lax.fori_loop(0, NF, rim_unpack, 0, unroll=7)

    fold_blocks = (REACH - 1, REACH, REACH + 1, *range(SIDE, BLOCKS))

    def block_row(ref, f, i):
        return ref[f, 7:8, COLS * i : COLS * (i + 1)]

    def fold(ref, fields, sign):
        for p, f in enumerate(fields):
            for j, i in enumerate(fold_blocks):
                FR[p, j : j + 1, :] = block_row(ref, f, BLOCKS - 1 - i)
            taken = jnp.take_along_axis(FR[p], IDX[...], axis=1, mode="promise_in_bounds")
            FO[p] = taken if sign > 0 else -taken

    def close_top(ref, p):
        ref[p, 24:25, 0:COLS] = FO[p, 1:2, :]
        ref[p, 24:25, COLS : 2 * COLS] = jnp.where(lane < COLS // 2, FO[p, 2:3, :], FO[p, 0:1, :])

    def window(first, reach):
        middle = first + REACH
        low, high = middle - reach, middle + reach + 1
        wide_low, wide_high = max(low - 1, first), min(high + 1, first + SIDE)
        return low, high, wide_low, wide_high

    def strip_sides(ref, f, win, p):
        low, high, wide_low, wide_high = win
        wide = ref[f, :, COLS * wide_low : COLS * wide_high]
        length = COLS * (wide_high - wide_low)
        cut = slice(COLS * (low - wide_low), COLS * (high - wide_low))
        value = wide[:, cut]
        to_east = pltpu.roll(wide, length - 1, 1)[:, cut]
        to_west = pltpu.roll(wide, 1, 1)[:, cut]
        folded = jnp.concatenate([FO[p, j : j + 1, :] for j in map(fold_blocks.index, range(low, high))], axis=1)
        to_north = jnp.where(row8 == 7, folded, pltpu.roll(value, 7, 0))
        to_south = pltpu.roll(value, 1, 0)
        return value, to_east, to_west, to_north, to_south

    def windows(left):
        found = []
        if left in OWN_REACH:
            found.append(window(0, OWN_REACH[left]))
        if left in MIRROR_REACH:
            found.append(window(SIDE, MIRROR_REACH[left]))
        return found

    SHARE = STEP_SIZE / (1.0 + STEP_SIZE)
    KEEP = 1.0 / (1.0 + STEP_SIZE)

    def ready(ref, rows, cols):
        present = ref[4, rows, cols]
        ref[5, rows, cols] = SHARE * present * ref[5, rows, cols]
        ref[6, rows, cols] = SHARE * present * ref[6, rows, cols]
        mass = ref[2, rows, cols]
        ref[2, rows, cols] = 0.5 * SHARE * present / jnp.where(mass > 0.0, mass, 1.0)
        ref[4, rows, cols] = KEEP * present
        ref[3, rows, cols] = ref[3, rows, cols] * (RELAX / (1.0 + RELAX))

    def main_sides(ref, f, start, size):
        value = ref[f, start : start + size, :]
        return (
            value,
            pltpu.roll(value, 2 * COLS - 1, 1),
            pltpu.roll(value, 1, 1),
            ref[f, start + 1 : start + size + 1, :],
            ref[f, start - 1 : start + size - 1, :],
        )

    CHUNK = 24
    chunks = range(8, 8 + SPAN, CHUNK)

    def stress(u, v, third, old):
        twice_d = (u[1] - u[2]) + (v[3] - v[4])
        twice_h = (u[3] - u[4]) + (v[1] - v[2])
        viscous = third * lax.rsqrt(twice_d * twice_d + 0.25 * (twice_h * twice_h) + 0.04)
        a = viscous * twice_d - third
        b = viscous * twice_h
        if old is not None:
            a = a + old[0] * (1.0 / (1.0 + RELAX))
            b = b + old[1] * (1.0 / (1.0 + RELAX))
        return a, b

    def push(ref, vel, rows, cols, a, b):
        keep, mobility = ref[4, rows, cols], ref[2, rows, cols]
        new_u = keep * vel[0, rows, cols] + mobility * ((a[1] - a[2]) + (b[3] - b[4])) + ref[5, rows, cols]
        new_v = keep * vel[1, rows, cols] + mobility * ((b[1] - b[2]) + (a[3] - a[4])) + ref[6, rows, cols]
        vel[0, rows, cols] = new_u
        vel[1, rows, cols] = new_v

    every = slice(0, 8)

    def chunk_stress(vel, sig, start, first=False):
        rows = slice(start, start + CHUNK)
        u, v = main_sides(vel, 0, start, CHUNK), main_sides(vel, 1, start, CHUNK)
        old = None if first else (sig[0, rows, :], sig[1, rows, :])
        sig[0, rows, :], sig[1, rows, :] = stress(u, v, vel[3, rows, :], old)

    def chunk_push(vel, sig, start):
        a, b = main_sides(sig, 0, start, CHUNK), main_sides(sig, 1, start, CHUNK)
        push(vel, vel, slice(start, start + CHUNK), slice(0, 2 * COLS), a, b)

    def tile_cycle(cycle, carry):
        for start in chunks:
            chunk_stress(X, AB, start)
        for start in chunks:
            chunk_push(X, AB, start)
        return carry

    low_piece, high_piece, low_tile, high_tile = slice(8, 16), slice(16, 24), slice(80, 88), slice(88, 96)

    def top_cycles(cycles):
        vel, sig, i_a, i_b = (S, SAB, 0, 1) if cycles[0] == 0 else (S2, S2, 2, 3)
        for cycle in cycles:
            left = 3 if cycle == cycles[0] else 1
            fold(vel, (0, 1), -1)
            close_top(XT, 0)
            close_top(XT, 1)
            for win in windows(left):
                cols = slice(COLS * win[0], COLS * win[1])
                u, v = strip_sides(vel, 0, win, 0), strip_sides(vel, 1, win, 1)
                old = (sig[i_a, :, cols], sig[i_b, :, cols]) if cycle else None
                sig[i_a, :, cols], sig[i_b, :, cols] = stress(u, v, S[3, :, cols], old)
            chunk_stress(XT, ABT, 8, cycle == 0)
            fold(sig, (i_a, i_b), 1)
            close_top(ABT, 0)
            close_top(ABT, 1)
            for win in windows(left - 1):
                cols = slice(COLS * win[0], COLS * win[1])
                push(S, vel, every, cols, strip_sides(sig, i_a, win, 0), strip_sides(sig, i_b, win, 1))
            chunk_push(XT, ABT, 8)

    for start in chunks:
        ready(X, slice(start, start + CHUNK), slice(0, 2 * COLS))

    @pl.when(is_top)
    def _():
        XT[...] = X[:, 72:112, :]
        ABT[...] = jnp.zeros((2, 40, 2 * COLS), jnp.float32)

    lax.fori_loop(0, 2, tile_cycle, 0)

    @pl.when(is_top)
    def _():
        strips_arrive(False)
        for j, i in enumerate(fold_blocks):
            IDX[j : j + 1, :] = block_row(S, NF, i).astype(jnp.int32)
        ready(S, every, slice(0, BLOCKS * COLS))
        top_cycles((0, 1))
        SS2[0:2] = XT[0:2, high_piece, 0:COLS]
        SS2[2:4] = ABT[:, high_piece, 0:COLS]
        strips_start(True)
        S2[:, :, middle] = SS2[...]
        X[0:2, high_tile, :] = XT[0:2, high_piece, :]
        AB[:, high_tile, :] = ABT[:, high_piece, :]
        XT[0:2, low_piece, :] = X[0:2, low_tile, :]
        ABT[:, low_piece, :] = AB[:, low_tile, :]

    lax.fori_loop(0, 2, tile_cycle, 0)

    here = pl.ds(pl.multiple_of(TOP + HALF * comp, 8), HALF)

    def vel_part(i, low, rows):
        away = pl.ds(pl.multiple_of(TOP + HALF * (1 - comp) + low, 8), rows)
        return send(
            X.at[0:2, away, 0:COLS], new_ice.at[:, low : low + rows, mine], vel_send.at[i], vel_recv.at[i], partner
        )

    vel_away = [vel_part(0, 0, HALF - 8), vel_part(1, HALF - 8, 8)]
    vel_here = pltpu.make_async_copy(X.at[0:2, here, 0:COLS], new_ice.at[:, :, mine], out_sem.at[3])

    vel_away[0].start()

    @pl.when(jnp.logical_not(is_top))
    def _():
        vel_away[1].start()
        vel_here.start()

    def regrid(g):
        planes = pl.ds(g * LEV, LEV)
        pieces = range(0, ROWS, LEV)
        high = jnp.concatenate([DH[planes, r : r + LEV, :].reshape(LEV * LEV, COLS) for r in pieces], axis=1)
        low = jnp.concatenate([DL[planes, r : r + LEV, :].reshape(LEV * LEV, COLS) for r in pieces], axis=1)
        new = jnp.dot(KK[...], jnp.concatenate([high, high, low], axis=0), preferred_element_type=jnp.float32)
        for i, r in enumerate(pieces):
            O[planes, r : r + LEV, :] = new[:, COLS * i : COLS * (i + 1)].reshape(LEV, LEV, COLS)

    @pl.when(is_top)
    def _():
        def early(g, carry):
            regrid(g)
            return carry

        lax.fori_loop(0, 2, early, 0)
        strips_arrive(True)
        to_the_e = S2[0:2, 7:8, COLS * (REACH + 1) : COLS * (REACH + 2)]
        to_the_w = S2[0:2, 7:8, COLS * (REACH - 1) : COLS * REACH]
        XT[0:2, 23:24, COLS : 2 * COLS] = jnp.where(lane < COLS // 2, to_the_e, to_the_w)
        top_cycles((2, 3))
        X[0:2, high_tile, :] = XT[0:2, high_piece, :]
        vel_away[1].start()
        vel_here.start()

    lax.fori_loop(2 * LEV, 3 * LEV, diffuse, 0, unroll=4)

    outs = (new_tracer, new_ocean_u, new_ocean_v)

    stores = [
        pltpu.make_async_copy(O.at[g * LEV : (g + 1) * LEV], outs[g], out_sem.at[g]) for g in range(3)
    ]

    def finish(g, carry):
        @pl.when(jnp.logical_not(is_top) | (g == 2))
        def _():
            regrid(g)

        for i in range(3):

            @pl.when(g == i)
            def _(i=i):
                if i:
                    tau = X[i - 1, tile_rows, 0:COLS] - X[4 + i, tile_rows, 0:COLS] * (1.0 / SHARE)
                    O[i * LEV] = O[i * LEV] + COUPLE * (F[SEA, 8 : 8 + ROWS, :] * tau)
                stores[i].start()

        return carry

    lax.fori_loop(0, 3, finish, 0)

    @pl.when(is_top)
    def _():
        strips_sent(False)
        strips_sent(True)

    ice_away.wait_send()
    for copy in vel_away + [vel_here] + stores:
        copy.wait()


def deliver(tracer, ocean_u, ocean_v, ice, new_tracer, new_ocean_u, new_ocean_v, new_ice_u, new_ice_v, sems):
    pairs = [
        (tracer, new_tracer),
        (ocean_u, new_ocean_u),
        (ocean_v, new_ocean_v),
        (ice.at[0], new_ice_u),
        (ice.at[1], new_ice_v),
    ]
    copies = [pltpu.make_async_copy(src, dst, sems.at[i]) for i, (src, dst) in enumerate(pairs)]
    for copy in copies:
        copy.start()
    for copy in copies:
        copy.wait()


def solution(mesh):
    blocks = mesh.shape["gx"] * 2
    gys = mesh.shape["gy"]
    ocean = P(None, "gy", ("gx", "comp"))
    flat = P("gy", ("gx", "comp"))
    ice = P(("gy", "comp"), "gx")
    in_specs = (ocean, ocean, ocean, flat, P(), P(), P(), P(("gx", "comp")), ice, ice, ice, ice, ice)
    out_specs = (ocean, ocean, ocean, ice, ice)

    def body(tracer, ocean_u, ocean_v, ocean_mask, diffusivity, viscosity, remap, fold_partner, *ice_fields):
        f32 = jnp.float32
        anywhere = pl.BlockSpec(memory_space=pl.ANY)
        main_memory = pl.BlockSpec(memory_space=pltpu.HBM)
        vmem = pltpu.VMEM
        dma = pltpu.SemaphoreType.DMA
        ocean_shape = jax.ShapeDtypeStruct(tracer.shape, f32)
        ice_shape = jax.ShapeDtypeStruct(ice_fields[0].shape, f32)

        def step(*args):
            kernel(blocks, gys, *args)

        shapes = (ocean_shape, ocean_shape, ocean_shape, ice_shape, ice_shape)
        results = pl.pallas_call(
            step,
            out_shape=(*shapes[:3], jax.ShapeDtypeStruct((2, *ice_fields[0].shape), f32)),
            in_specs=[main_memory] * 13,
            out_specs=(anywhere,) * 4,
            scratch_shapes=[
                vmem((PLANES, 96, COLS), f32),
                vmem((3 * LEV, ROWS, COLS), jnp.bfloat16),
                vmem((3 * LEV, ROWS, COLS), jnp.bfloat16),
                vmem((LEV * LEV, 3 * LEV * LEV), jnp.bfloat16),
                vmem((3 * LEV, ROWS, COLS), f32),
                vmem((NF, 112, 2 * COLS), f32),
                vmem((2, 112, 2 * COLS), f32),
                vmem((NF, 40, 2 * COLS), f32),
                vmem((2, 40, 2 * COLS), f32),
                vmem((NS, 8, 2 * BLOCKS * COLS), f32),
                vmem((2, 8, BLOCKS * COLS), f32),
                vmem((NS, 8, COLS), f32),
                vmem((4, 8, 2 * BLOCKS * COLS), f32),
                vmem((4, 8, COLS), f32),
                vmem((2, 8, COLS), f32),
                vmem((2, 8, COLS), f32),
                vmem((HALF, COLS), f32),
                vmem((HALF, COLS), f32),
                vmem((HALF, COLS), f32),
                vmem((HALF, COLS), f32),
                vmem((8, COLS), f32),
                vmem((8, COLS), f32),
                vmem((8, COLS), f32),
                vmem((8, COLS), f32),
                vmem((3 * LEV, COLS), f32),
                vmem((3 * LEV, COLS), f32),
                vmem((3 * LEV, COLS), f32),
                vmem((3 * LEV, COLS), f32),
                *[vmem((8, COLS), f32)] * 8,
                vmem((HALF, COLS), f32),
                vmem((HALF, COLS), f32),
                vmem((HALF, COLS), f32),
                vmem((HALF, COLS), f32),
                vmem((ROWS, COLS), f32),
                vmem((5, ROWS, COLS), f32),
                vmem((ROWS, COLS), jnp.int32),
                vmem((ROWS, COLS), jnp.int32),
                vmem((8, COLS), jnp.int32),
                pltpu.SMEM((LEV,), f32),
                pltpu.SMEM((LEV,), f32),
                pltpu.SMEM((LEV, LEV), f32),
                vmem((LEV, LEV), f32),
                vmem((1, COLS), jnp.int32),
                dma((9,)),
                dma((5,)),
                dma((5,)),
                dma((5,)),
                dma((5,)),
                dma((5,)),
                dma((5,)),
                dma((5,)),
                dma((8,)),
                dma((8,)),
                dma((BLOCKS,)),
                dma((BLOCKS,)),
                dma((BLOCKS,)),
                dma((BLOCKS,)),
                dma((5,)),
                dma((2,)),
                dma((2,)),
            ],
            compiler_params=pltpu.CompilerParams(
                collective_id=0, has_side_effects=True, vmem_limit_bytes=32 * 1024 * 1024
            ),
        )(
            *[
                pltpu.with_memory_space_constraint(value, pltpu.HBM)
                for value in (
                    tracer,
                    ocean_u,
                    ocean_v,
                    ocean_mask,
                    diffusivity,
                    viscosity,
                    remap,
                    fold_partner.reshape(1, COLS),
                    *ice_fields,
                )
            ]
        )
        return pl.pallas_call(
            deliver,
            out_shape=shapes,
            in_specs=[anywhere] * 4,
            out_specs=(main_memory,) * 5,
            scratch_shapes=[dma((5,))],
            compiler_params=pltpu.CompilerParams(vmem_limit_bytes=1024 * 1024),
        )(*results)

    return jax.shard_map(body, mesh=mesh, in_specs=in_specs, out_specs=out_specs, check_vma=False)
```

```python
import jax
import jax.numpy as jnp
from jax import lax
from jax.experimental import pallas as pl
from jax.experimental.pallas import tpu as pltpu
from jax.sharding import PartitionSpec as P

ITERS = 4
RELAX = 0.5
STEP_SIZE = 0.3
COUPLE = 0.5
MESH = pl.DeviceIdType.MESH

LEV = 16
ROWS = 80
HALF = 40
COLS = 128
NF = 7
NS = NF + 1
REACH = 2
SIDE = 2 * REACH + 1
BLOCKS = 2 * SIDE
TOP = 16
SPAN = 96
OWN_REACH = {2: 0, 3: 1}
MIRROR_REACH = {1: 0, 2: 1, 3: 2}
OWN_ROWS = (8, 2, 1)
MIRROR_ROWS = (4, 3, 2)
SEA = 3 * LEV
PLANES = SEA + 3


def kernel(
    blocks,
    gys,
    tracer,
    ocean_u,
    ocean_v,
    ocean_mask,
    diffusivity_in,
    viscosity_in,
    remap_in,
    fold_in,
    ice_u,
    ice_v,
    ice_mass,
    ice_strength,
    ice_mask,
    new_tracer,
    new_ocean_u,
    new_ocean_v,
    new_ice,
    F,
    DH,
    DL,
    KK,
    O,
    X,
    AB,
    XT,
    ABT,
    S,
    SAB,
    SS,
    S2,
    SS2,
    FR,
    FO,
    PE,
    PW,
    EB,
    WB,
    EBS,
    WBS,
    EBN,
    WBN,
    TR,
    BR,
    NR,
    SR,
    CK,
    RKE,
    RKW,
    GK,
    TK,
    BK,
    NK,
    SK,
    CE,
    CW,
    RE,
    RW,
    GE,
    MK,
    OM,
    IM,
    IDX,
    diffusivity,
    viscosity,
    remap,
    remap_wide,
    fold_partner,
    in_sem,
    ice_sem,
    ice_send,
    ice_recv,
    edge_send,
    edge_recv,
    first_send,
    first_recv,
    rim_send,
    rim_recv,
    strip_send,
    strip_recv,
    again_send,
    again_recv,
    out_sem,
    vel_send,
    vel_recv,
):
    gx, gy, comp = lax.axis_index("gx"), lax.axis_index("gy"), lax.axis_index("comp")
    me = gx * 2 + comp
    has_north = gy < gys - 1
    has_south = gy > 0
    is_top = gy == gys - 1

    def at(block, row):
        return {"gx": block // 2, "gy": row, "comp": lax.rem(block, 2)}

    def wrap(block):
        return lax.rem(block + 2 * blocks, blocks)

    east, west, mirror = wrap(me + 1), wrap(me - 1), blocks - 1 - me
    partner = at(gx * 2 + 1 - comp, gy)

    strips = [(SIDE + REACH, mirror, False, MIRROR_ROWS[0])]
    for d in (1, -1, 2, -2):
        strips.append((SIDE + REACH + d, wrap(mirror + d), d % 2 == 1, MIRROR_ROWS[abs(d)]))
        strips.append((REACH + d, wrap(me - d), False, OWN_ROWS[abs(d)]))

    def load(src, dst, sem):
        copy = pltpu.make_async_copy(src, dst, sem)
        copy.start()
        return copy

    load_u = load(ocean_u, F.at[LEV : 2 * LEV, 8 : 8 + ROWS, :], in_sem.at[0])
    load_v = load(ocean_v, F.at[2 * LEV : 3 * LEV, 8 : 8 + ROWS, :], in_sem.at[1])
    barrier = pltpu.get_barrier_semaphore()

    def greet(target):
        pl.semaphore_signal(barrier, inc=1, device_id=target, device_id_type=MESH)

    greet(at(east, gy))
    greet(at(west, gy))

    @pl.when(has_north)
    def _():
        for block in (me, east, west):
            greet(at(block, gy + 1))

    @pl.when(has_south)
    def _():
        for block in (me, east, west):
            greet(at(block, gy - 1))

    @pl.when(is_top)
    def _():
        for _, block, own, _ in strips:
            if own:

                @pl.when(block != me)
                def _(block=block):
                    greet(at(block, gy))
            else:
                greet(at(block, gy))

    small = [
        load(ocean_mask, OM, in_sem.at[2]),
        load(remap_in, remap, in_sem.at[4]),
        load(diffusivity_in, diffusivity, in_sem.at[5]),
        load(viscosity_in, viscosity, in_sem.at[6]),
        load(fold_in, fold_partner, in_sem.at[7]),
        load(remap_in, remap_wide, in_sem.at[8]),
    ]
    ice_in = (ice_u, ice_v, ice_mass, ice_strength, ice_mask)

    def ice_place(i, half):
        rows = pl.ds(pl.multiple_of(TOP + HALF * half, 8), HALF)
        if i == 4:
            return IM.at[pl.ds(pl.multiple_of(HALF * half, 8), HALF), :]
        return X.at[i, rows, 0:COLS]

    mine = pl.ds(pl.multiple_of(COLS * comp, COLS), COLS)
    other = pl.ds(pl.multiple_of(COLS * (1 - comp), COLS), COLS)
    for i in range(5):
        load(ice_in[i].at[:, mine], ice_place(i, comp), ice_sem.at[0])

    first8, last8 = slice(TOP, TOP + 8), slice(TOP + ROWS - 8, TOP + ROWS)
    south8, north8 = slice(TOP - 8, TOP), slice(TOP + ROWS, TOP + ROWS + 8)

    @pl.when(jnp.logical_not(has_south))
    def _():
        X[:, south8, 0:COLS] = jnp.zeros((NF, 8, COLS), jnp.float32)
        EBS[...] = jnp.zeros((8, COLS), jnp.float32)
        WBS[...] = jnp.zeros((8, COLS), jnp.float32)
        SR[...] = jnp.zeros((3 * LEV, COLS), jnp.float32)
        SK[...] = jnp.zeros((8, COLS), jnp.float32)

    @pl.when(is_top)
    def _():
        X[:, north8, 0:COLS] = jnp.zeros((NF, 8, COLS), jnp.float32)
        EBN[...] = jnp.zeros((8, COLS), jnp.float32)
        WBN[...] = jnp.zeros((8, COLS), jnp.float32)

    outer = jnp.zeros((NF, 8, 2 * COLS), jnp.float32)
    X[:, 0:8, :] = outer
    X[:, 104:112, :] = outer
    AB[...] = jnp.zeros((2, 112, 2 * COLS), jnp.float32)

    count = 2 + 3 * has_north.astype(jnp.int32) + 3 * has_south.astype(jnp.int32)
    strip_count = 0
    for _, block, own, _ in strips:
        strip_count = strip_count + ((block != me).astype(jnp.int32) if own else 1)
    count = count + is_top.astype(jnp.int32) * strip_count
    pl.semaphore_wait(barrier, count)

    def send(src, dst, send_sem, recv_sem, target):
        copy = pltpu.make_async_remote_copy(
            src_ref=src,
            dst_ref=dst,
            send_sem=send_sem,
            recv_sem=recv_sem,
            device_id=target,
            device_id_type=MESH,
        )
        return copy

    for i in range(5):
        send(ice_in[i].at[:, other], ice_place(i, comp), ice_send.at[0], ice_recv.at[0], partner).start()
    ice_all = X.at[0:5, TOP : TOP + HALF, 0:COLS]
    ice_away = send(ice_all, ice_all, ice_send.at[0], ice_recv.at[0], partner)

    load_t = load(tracer, F.at[0:LEV, 8 : 8 + ROWS, :], in_sem.at[3])
    lane = lax.broadcasted_iota(jnp.int32, (1, COLS), 1)
    even = (lane & 1) == 0
    row8 = lax.broadcasted_iota(jnp.int32, (8, 1), 0)
    tile_rows = slice(TOP, TOP + ROWS)

    for copy in small:
        copy.wait()
    sea = OM[...].astype(jnp.float32)
    F[SEA, 8 : 8 + ROWS, :] = sea
    for i, copy in ((0, load_u), (1, load_v)):
        copy.wait()

        def level(l, sums, i=i):
            weighted = remap[0, l] * F[LEV * (i + 1) + l, 8 : 8 + ROWS, :]
            return sums[0] + weighted, sums[1] + viscosity[l] * weighted

        zero = jnp.zeros((ROWS, COLS), jnp.float32)
        base, spread = lax.fori_loop(0, LEV, level, (zero, zero), unroll=4)
        X[5 + i, tile_rows, 0:COLS] = base
        F[SEA + 1 + i, 8 : 8 + ROWS, :] = spread

    first = [(3 * t + p, SEA + p, slice(8 + 8 * t, 16 + 8 * t)) for t in range(ROWS // 8) for p in range(3)]
    packed = jnp.zeros((8, COLS), jnp.float32)
    for m, f, rows in first:
        packed = jnp.where((lane >> 1) == m, pltpu.roll(F[f, rows, :], 2 * m + 1, 1), packed)
    CK[...] = packed
    for p in range(3):
        TK[p : p + 1, :] = F[SEA + p, 87:88, :]
        BK[p : p + 1, :] = F[SEA + p, 8:9, :]
    first_e = send(CK, RKW, first_send.at[0], first_recv.at[0], at(east, gy))
    first_w = send(CK, RKE, first_send.at[1], first_recv.at[1], at(west, gy))
    first_n = send(TK, SK, first_send.at[2], first_recv.at[2], at(me, gy + 1))
    first_s = send(BK, NK, first_send.at[3], first_recv.at[3], at(me, gy - 1))
    first_f = send(TK, NK, first_send.at[4], first_recv.at[4], at(mirror, gy))
    first_e.start()
    first_w.start()

    @pl.when(has_north)
    def _():
        first_n.start()

    @pl.when(has_south)
    def _():
        first_s.start()

    @pl.when(is_top)
    def _():
        first_f.start()

    lane2 = lax.broadcasted_iota(jnp.int32, (LEV, LEV * LEV), 1)
    weights = jnp.zeros((LEV, LEV * LEV), jnp.float32)
    for l in range(LEV):
        weights = jnp.where((lane2 >> 4) == l, remap_wide[:, l : l + 1], weights)
    high = weights.astype(jnp.bfloat16).astype(jnp.float32)
    low = weights - high
    diagonal = (lane2 & 15) == lax.broadcasted_iota(jnp.int32, (LEV, LEV * LEV), 0)
    for k in range(LEV):
        rows = slice(LEV * k, LEV * (k + 1))
        high_k = jnp.where(diagonal, high[k : k + 1], 0.0).astype(jnp.bfloat16)
        KK[rows, 0:256] = high_k
        KK[rows, 256:512] = jnp.where(diagonal, low[k : k + 1], 0.0).astype(jnp.bfloat16)
        KK[rows, 512:768] = high_k

    first_e.wait()
    first_w.wait()

    @pl.when(has_north)
    def _():
        first_n.wait_send()
        first_s.wait_recv()

    @pl.when(has_south)
    def _():
        first_s.wait_send()
        first_n.wait_recv()

    inside_here = fold_partner[...] - COLS * mirror

    @pl.when(is_top)
    def _():
        first_f.wait()
        inside = jnp.broadcast_to(inside_here, (8, COLS))
        taken = jnp.take_along_axis(NK[...], inside, axis=1, mode="promise_in_bounds")
        NK[...] = jnp.where(row8 == 0, taken, -taken)

    GK[...] = jnp.where(even, pltpu.roll(RKE[...], COLS - 1, 1), pltpu.roll(RKW[...], 1, 1))
    for p in range(3):
        F[SEA + p, 88:89, :] = NK[p : p + 1, :]
        F[SEA + p, 7:8, :] = SK[p : p + 1, :]

    def sides_of(f, edges):
        value = F[f, 8 : 8 + ROWS, :]
        to_east = jnp.where(lane == COLS - 1, edges, pltpu.roll(value, COLS - 1, 1))
        to_west = jnp.where(lane == 0, edges, pltpu.roll(value, 1, 1))
        return value, to_east, to_west, F[f, 9 : 9 + ROWS, :], F[f, 7 : 7 + ROWS, :]

    def first_edges(f):
        return jnp.concatenate([pltpu.roll(GK[...], COLS - 1 - 2 * m, 1) for m, g, _ in first if g == f], axis=0)

    def lap(f, edges):
        value, to_east, to_west, to_north, to_south = sides_of(f, edges)
        total = MK[0] * to_east + MK[1] * to_west + MK[2] * to_north + MK[3] * to_south
        return value, total - MK[4] * value

    seas = sides_of(SEA, first_edges(SEA))
    degree = jnp.zeros((ROWS, COLS), jnp.float32)
    for i in range(4):
        weight = seas[0] * seas[i + 1]
        MK[i] = weight
        degree = degree + weight
    MK[4] = degree
    for i in range(2):
        f = SEA + 1 + i
        X[5 + i, tile_rows, 0:COLS] = X[5 + i, tile_rows, 0:COLS] + lap(f, first_edges(f))[1]

    pltpu.make_async_copy(ice_all, ice_all, ice_sem.at[0]).wait()
    ice_away.wait_recv()
    X[4, tile_rows, 0:COLS] = IM[...].astype(jnp.float32)


    def rim_pack(f, packed):
        south_half, north_half = X[f, TOP : TOP + HALF, 0:COLS], X[f, TOP + HALF : TOP + ROWS, 0:COLS]
        group = lane >> 3
        new = []
        for edge, old in ((8, packed[0]), (0, packed[1])):
            kept = jnp.where(group == f, pltpu.roll(south_half, 8 * f + edge, 1), old)
            new.append(jnp.where(group == f + 8, pltpu.roll(north_half, 64 + 8 * f + edge, 1), kept))
        return tuple(new)

    zero = jnp.zeros((HALF, COLS), jnp.float32)
    pack_e, pack_w = lax.fori_loop(0, NF, rim_pack, (zero, zero), unroll=7)
    PE[...] = pack_e
    PW[...] = pack_w
    to_e = send(PE, WB, rim_send.at[0], rim_recv.at[0], at(east, gy))
    to_w = send(PW, EB, rim_send.at[1], rim_recv.at[1], at(west, gy))
    to_n = [
        send(X.at[:, last8, 0:COLS], X.at[:, south8, 0:COLS], rim_send.at[2], rim_recv.at[2], at(me, gy + 1)),
        send(PE.at[HALF - 8 : HALF], WBS, rim_send.at[3], rim_recv.at[3], at(east, gy + 1)),
        send(PW.at[HALF - 8 : HALF], EBS, rim_send.at[4], rim_recv.at[4], at(west, gy + 1)),
    ]
    to_s = [
        send(X.at[:, first8, 0:COLS], X.at[:, north8, 0:COLS], rim_send.at[5], rim_recv.at[5], at(me, gy - 1)),
        send(PE.at[0:8], WBN, rim_send.at[6], rim_recv.at[6], at(east, gy - 1)),
        send(PW.at[0:8], EBN, rim_send.at[7], rim_recv.at[7], at(west, gy - 1)),
    ]

    def strip_ends(src, dst, slot, rows):
        kept = slice(8 - rows, 8)
        return src.at[:, kept, :], dst.at[:, kept, COLS * slot : COLS * (slot + 1)]

    def strip_copy(again, slot, block, own, rows):
        src, dst = strip_ends(SS2, S2, slot, rows) if again else strip_ends(SS, S, slot, rows)
        sent, received = (again_send, again_recv) if again else (strip_send, strip_recv)
        return send(src, dst, sent.at[slot if own else 0], received.at[0], at(block, gy))

    def strips_start(again):
        for slot, block, own, rows in strips:
            if own:

                @pl.when(block != me)
                def _(slot=slot, block=block, rows=rows):
                    strip_copy(again, slot, block, True, rows).start()

                @pl.when(block == me)
                def _(slot=slot, rows=rows):
                    src, dst = strip_ends(SS2, S2, slot, rows) if again else strip_ends(SS, S, slot, rows)
                    pltpu.make_async_copy(src, dst, (again_recv if again else strip_recv).at[0]).start()
            else:
                strip_copy(again, slot, block, False, rows).start()

    def strips_all(again, rows):
        area = (S2 if again else S).at[:, 0:1, 0 : COLS * rows]
        sent, received = (again_send, again_recv) if again else (strip_send, strip_recv)
        return send(area, area, sent.at[0], received.at[0], partner)

    def strips_arrive(again):
        strips_all(again, sum(rows for _, _, _, rows in strips)).wait_recv()

    def strips_sent(again):
        strips_all(again, sum(rows for _, _, own, rows in strips if not own)).wait_send()
        for slot, block, own, rows in strips:
            if own:

                @pl.when(block != me)
                def _(slot=slot, block=block, rows=rows):
                    strip_copy(again, slot, block, True, rows).wait_send()

    middle = slice(COLS * REACH, COLS * (REACH + 1))

    to_e.start()
    to_w.start()

    @pl.when(has_north)
    def _():
        for copy in to_n:
            copy.start()

    @pl.when(has_south)
    def _():
        for copy in to_s:
            copy.start()

    @pl.when(is_top)
    def _():
        SS[0:NF] = X[0:NF, last8, 0:COLS]
        SS[NF] = jnp.broadcast_to(inside_here.astype(jnp.float32), (8, COLS))
        S[:, :, middle] = SS[...]
        strips_start(False)

    load_t.wait()
    for f in range(3 * LEV):
        TR[f : f + 1, :] = F[f, 87:88, :]
        BR[f : f + 1, :] = F[f, 8:9, :]
    row_n = send(TR, SR, edge_send.at[2], edge_recv.at[2], at(me, gy + 1))
    row_s = send(BR, NR, edge_send.at[3], edge_recv.at[3], at(me, gy - 1))
    row_f = send(TR, NR, edge_send.at[4], edge_recv.at[4], at(mirror, gy))

    @pl.when(has_north)
    def _():
        row_n.start()

    @pl.when(has_south)
    def _():
        row_s.start()

    @pl.when(is_top)
    def _():
        row_f.start()

    def pack(f, packed):
        return jnp.where((lane >> 1) == f, pltpu.roll(F[f, 8 : 8 + ROWS, :], 2 * f + 1, 1), packed)

    packed = lax.fori_loop(0, 3 * LEV, pack, jnp.zeros((ROWS, COLS), jnp.float32), unroll=3)
    CE[...] = jnp.where(even, packed[0:HALF], pltpu.roll(packed[HALF:ROWS], 1, 1))
    CW[...] = jnp.where(even, pltpu.roll(packed[HALF:ROWS], COLS - 1, 1), packed[0:HALF])
    col_to_e = send(CE, RW, edge_send.at[0], edge_recv.at[0], at(east, gy))
    col_to_w = send(CW, RE, edge_send.at[1], edge_recv.at[1], at(west, gy))
    col_to_e.start()
    col_to_w.start()

    to_e.wait()
    to_w.wait()

    @pl.when(has_north)
    def _():
        for copy in to_n:
            copy.wait_send()
        for copy in to_s:
            copy.wait_recv()

    @pl.when(has_south)
    def _():
        for copy in to_s:
            copy.wait_send()
        for copy in to_n:
            copy.wait_recv()

    def rim_unpack(f, carry):
        def put(rows, e, w, half):
            from_e = pltpu.roll(e, lax.rem(COLS + half - 8 * f, COLS), 1)
            from_w = pltpu.roll(w, lax.rem(2 * COLS - 8 + half - 8 * f, COLS), 1)
            X[f, rows, COLS : 2 * COLS] = jnp.where(
                lane < 8, from_e, jnp.where(lane >= COLS - 8, from_w, 0.0)
            )

        put(slice(TOP, TOP + HALF), EB[...], WB[...], 0)
        put(slice(TOP + HALF, TOP + ROWS), EB[...], WB[...], 64)
        put(slice(TOP - 8, TOP), EBS[...], WBS[...], 64)
        put(slice(TOP + ROWS, TOP + ROWS + 8), EBN[...], WBN[...], 0)
        return carry

    lax.fori_loop(0, NF, rim_unpack, 0, unroll=7)

    fold_blocks = (REACH - 1, REACH, REACH + 1, *range(SIDE, BLOCKS))

    def block_row(ref, f, i):
        return ref[f, 7:8, COLS * i : COLS * (i + 1)]

    def fold(ref, fields, sign):
        for p, f in enumerate(fields):
            for j, i in enumerate(fold_blocks):
                FR[p, j : j + 1, :] = block_row(ref, f, BLOCKS - 1 - i)
            taken = jnp.take_along_axis(FR[p], IDX[...], axis=1, mode="promise_in_bounds")
            FO[p] = taken if sign > 0 else -taken

    def close_top(ref, p):
        ref[p, 24:25, 0:COLS] = FO[p, 1:2, :]
        ref[p, 24:25, COLS : 2 * COLS] = jnp.where(lane < COLS // 2, FO[p, 2:3, :], FO[p, 0:1, :])

    def window(first, reach):
        middle = first + REACH
        low, high = middle - reach, middle + reach + 1
        wide_low, wide_high = max(low - 1, first), min(high + 1, first + SIDE)
        return low, high, wide_low, wide_high

    def strip_sides(ref, f, win, p):
        low, high, wide_low, wide_high = win
        wide = ref[f, :, COLS * wide_low : COLS * wide_high]
        length = COLS * (wide_high - wide_low)
        cut = slice(COLS * (low - wide_low), COLS * (high - wide_low))
        value = wide[:, cut]
        to_east = pltpu.roll(wide, length - 1, 1)[:, cut]
        to_west = pltpu.roll(wide, 1, 1)[:, cut]
        folded = jnp.concatenate([FO[p, j : j + 1, :] for j in map(fold_blocks.index, range(low, high))], axis=1)
        to_north = jnp.where(row8 == 7, folded, pltpu.roll(value, 7, 0))
        to_south = pltpu.roll(value, 1, 0)
        return value, to_east, to_west, to_north, to_south

    def windows(left):
        found = []
        if left in OWN_REACH:
            found.append(window(0, OWN_REACH[left]))
        if left in MIRROR_REACH:
            found.append(window(SIDE, MIRROR_REACH[left]))
        return found

    SHARE = STEP_SIZE / (1.0 + STEP_SIZE)
    KEEP = 1.0 / (1.0 + STEP_SIZE)

    def ready(ref, rows, cols):
        present = ref[4, rows, cols]
        ref[5, rows, cols] = SHARE * present * ref[5, rows, cols]
        ref[6, rows, cols] = SHARE * present * ref[6, rows, cols]
        mass = ref[2, rows, cols]
        ref[2, rows, cols] = 0.5 * SHARE * present / jnp.where(mass > 0.0, mass, 1.0)
        ref[4, rows, cols] = KEEP * present
        ref[3, rows, cols] = ref[3, rows, cols] * (RELAX / (1.0 + RELAX))

    def main_sides(ref, f, start, size):
        value = ref[f, start : start + size, :]
        return (
            value,
            pltpu.roll(value, 2 * COLS - 1, 1),
            pltpu.roll(value, 1, 1),
            ref[f, start + 1 : start + size + 1, :],
            ref[f, start - 1 : start + size - 1, :],
        )

    CHUNK = 24
    chunks = range(8, 8 + SPAN, CHUNK)

    def stress(u, v, third, old):
        twice_d = (u[1] - u[2]) + (v[3] - v[4])
        twice_h = (u[3] - u[4]) + (v[1] - v[2])
        viscous = third * lax.rsqrt(twice_d * twice_d + 0.25 * (twice_h * twice_h) + 0.04)
        a = viscous * twice_d - third
        b = viscous * twice_h
        if old is not None:
            a = a + old[0] * (1.0 / (1.0 + RELAX))
            b = b + old[1] * (1.0 / (1.0 + RELAX))
        return a, b

    def push(ref, vel, rows, cols, a, b):
        keep, mobility = ref[4, rows, cols], ref[2, rows, cols]
        new_u = keep * vel[0, rows, cols] + mobility * ((a[1] - a[2]) + (b[3] - b[4])) + ref[5, rows, cols]
        new_v = keep * vel[1, rows, cols] + mobility * ((b[1] - b[2]) + (a[3] - a[4])) + ref[6, rows, cols]
        vel[0, rows, cols] = new_u
        vel[1, rows, cols] = new_v

    every = slice(0, 8)

    def chunk_stress(vel, sig, start, first=False):
        rows = slice(start, start + CHUNK)
        u, v = main_sides(vel, 0, start, CHUNK), main_sides(vel, 1, start, CHUNK)
        old = None if first else (sig[0, rows, :], sig[1, rows, :])
        sig[0, rows, :], sig[1, rows, :] = stress(u, v, vel[3, rows, :], old)

    def chunk_push(vel, sig, start):
        a, b = main_sides(sig, 0, start, CHUNK), main_sides(sig, 1, start, CHUNK)
        push(vel, vel, slice(start, start + CHUNK), slice(0, 2 * COLS), a, b)

    def tile_cycle(cycle, carry):
        for start in chunks:
            chunk_stress(X, AB, start)
        for start in chunks:
            chunk_push(X, AB, start)
        return carry

    low_piece, high_piece, low_tile, high_tile = slice(8, 16), slice(16, 24), slice(80, 88), slice(88, 96)

    def top_cycles(cycles):
        vel, sig, i_a, i_b = (S, SAB, 0, 1) if cycles[0] == 0 else (S2, S2, 2, 3)
        for cycle in cycles:
            left = 3 if cycle == cycles[0] else 1
            fold(vel, (0, 1), -1)
            close_top(XT, 0)
            close_top(XT, 1)
            for win in windows(left):
                cols = slice(COLS * win[0], COLS * win[1])
                u, v = strip_sides(vel, 0, win, 0), strip_sides(vel, 1, win, 1)
                old = (sig[i_a, :, cols], sig[i_b, :, cols]) if cycle else None
                sig[i_a, :, cols], sig[i_b, :, cols] = stress(u, v, S[3, :, cols], old)
            chunk_stress(XT, ABT, 8, cycle == 0)
            fold(sig, (i_a, i_b), 1)
            close_top(ABT, 0)
            close_top(ABT, 1)
            for win in windows(left - 1):
                cols = slice(COLS * win[0], COLS * win[1])
                push(S, vel, every, cols, strip_sides(sig, i_a, win, 0), strip_sides(sig, i_b, win, 1))
            chunk_push(XT, ABT, 8)

    for start in chunks:
        ready(X, slice(start, start + CHUNK), slice(0, 2 * COLS))

    @pl.when(is_top)
    def _():
        XT[...] = X[:, 72:112, :]
        ABT[...] = jnp.zeros((2, 40, 2 * COLS), jnp.float32)

    lax.fori_loop(0, 2, tile_cycle, 0)

    @pl.when(is_top)
    def _():
        strips_arrive(False)
        for j, i in enumerate(fold_blocks):
            IDX[j : j + 1, :] = block_row(S, NF, i).astype(jnp.int32)
        ready(S, every, slice(0, BLOCKS * COLS))
        top_cycles((0, 1))
        SS2[0:2] = XT[0:2, high_piece, 0:COLS]
        SS2[2:4] = ABT[:, high_piece, 0:COLS]
        strips_start(True)
        S2[:, :, middle] = SS2[...]
        X[0:2, high_tile, :] = XT[0:2, high_piece, :]
        AB[:, high_tile, :] = ABT[:, high_piece, :]
        XT[0:2, low_piece, :] = X[0:2, low_tile, :]
        ABT[:, low_piece, :] = AB[:, low_tile, :]

    lax.fori_loop(0, 2, tile_cycle, 0)

    here = pl.ds(pl.multiple_of(TOP + HALF * comp, 8), HALF)

    def vel_part(i, low, rows):
        away = pl.ds(pl.multiple_of(TOP + HALF * (1 - comp) + low, 8), rows)
        return send(
            X.at[0:2, away, 0:COLS], new_ice.at[:, low : low + rows, mine], vel_send.at[i], vel_recv.at[i], partner
        )

    vel_away = [vel_part(0, 0, HALF - 8), vel_part(1, HALF - 8, 8)]
    vel_here = pltpu.make_async_copy(X.at[0:2, here, 0:COLS], new_ice.at[:, :, mine], out_sem.at[3])

    vel_away[0].start()

    @pl.when(jnp.logical_not(is_top))
    def _():
        vel_away[1].start()
        vel_here.start()

    col_to_e.wait()
    col_to_w.wait()

    @pl.when(has_north)
    def _():
        row_n.wait_send()
        row_s.wait_recv()

    @pl.when(has_south)
    def _():
        row_s.wait_send()
        row_n.wait_recv()

    @pl.when(is_top)
    def _():
        row_f.wait()
        inside = jnp.broadcast_to(inside_here, (8, COLS))
        for r in range(0, 3 * LEV, 8):
            taken = jnp.take_along_axis(NR[r : r + 8, :], inside, axis=1, mode="promise_in_bounds")
            NR[r : r + 8, :] = taken if r < LEV else -taken

    for f in range(3 * LEV):
        F[f, 88:89, :] = NR[f : f + 1, :]
        F[f, 7:8, :] = SR[f : f + 1, :]
    GE[0:HALF] = jnp.where(even, pltpu.roll(RE[...], COLS - 1, 1), pltpu.roll(RW[...], 1, 1))
    GE[HALF:ROWS] = jnp.where(even, RE[...], RW[...])

    def diffuse(f, carry):
        coefficient = jnp.where(f < LEV, diffusivity[f & (LEV - 1)], viscosity[f & (LEV - 1)])
        value, spread = lap(f, pltpu.roll(GE[...], COLS - 1 - 2 * f, 1))
        new = value + coefficient * spread
        high = new.astype(jnp.bfloat16)
        DH[f] = high
        DL[f] = (new - high.astype(jnp.float32)).astype(jnp.bfloat16)
        return carry

    lax.fori_loop(0, 2 * LEV, diffuse, 0, unroll=4)

    def regrid(g):
        planes = pl.ds(g * LEV, LEV)
        pieces = range(0, ROWS, LEV)
        high = jnp.concatenate([DH[planes, r : r + LEV, :].reshape(LEV * LEV, COLS) for r in pieces], axis=1)
        low = jnp.concatenate([DL[planes, r : r + LEV, :].reshape(LEV * LEV, COLS) for r in pieces], axis=1)
        new = jnp.dot(KK[...], jnp.concatenate([high, high, low], axis=0), preferred_element_type=jnp.float32)
        for i, r in enumerate(pieces):
            O[planes, r : r + LEV, :] = new[:, COLS * i : COLS * (i + 1)].reshape(LEV, LEV, COLS)

    @pl.when(is_top)
    def _():
        def early(g, carry):
            regrid(g)
            return carry

        lax.fori_loop(0, 2, early, 0)
        strips_arrive(True)
        to_the_e = S2[0:2, 7:8, COLS * (REACH + 1) : COLS * (REACH + 2)]
        to_the_w = S2[0:2, 7:8, COLS * (REACH - 1) : COLS * REACH]
        XT[0:2, 23:24, COLS : 2 * COLS] = jnp.where(lane < COLS // 2, to_the_e, to_the_w)
        top_cycles((2, 3))
        X[0:2, high_tile, :] = XT[0:2, high_piece, :]
        vel_away[1].start()
        vel_here.start()

    lax.fori_loop(2 * LEV, 3 * LEV, diffuse, 0, unroll=4)

    outs = (new_tracer, new_ocean_u, new_ocean_v)

    stores = [
        pltpu.make_async_copy(O.at[g * LEV : (g + 1) * LEV], outs[g], out_sem.at[g]) for g in range(3)
    ]

    def finish(g, carry):
        @pl.when(jnp.logical_not(is_top) | (g == 2))
        def _():
            regrid(g)

        for i in range(3):

            @pl.when(g == i)
            def _(i=i):
                if i:
                    tau = X[i - 1, tile_rows, 0:COLS] - X[4 + i, tile_rows, 0:COLS] * (1.0 / SHARE)
                    O[i * LEV] = O[i * LEV] + COUPLE * (F[SEA, 8 : 8 + ROWS, :] * tau)
                stores[i].start()

        return carry

    lax.fori_loop(0, 3, finish, 0)

    @pl.when(is_top)
    def _():
        strips_sent(False)
        strips_sent(True)

    ice_away.wait_send()
    for copy in vel_away + [vel_here] + stores:
        copy.wait()


def deliver(tracer, ocean_u, ocean_v, ice, new_tracer, new_ocean_u, new_ocean_v, new_ice_u, new_ice_v, sems):
    pairs = [
        (tracer, new_tracer),
        (ocean_u, new_ocean_u),
        (ocean_v, new_ocean_v),
        (ice.at[0], new_ice_u),
        (ice.at[1], new_ice_v),
    ]
    copies = [pltpu.make_async_copy(src, dst, sems.at[i]) for i, (src, dst) in enumerate(pairs)]
    for copy in copies:
        copy.start()
    for copy in copies:
        copy.wait()


def solution(mesh):
    blocks = mesh.shape["gx"] * 2
    gys = mesh.shape["gy"]
    ocean = P(None, "gy", ("gx", "comp"))
    flat = P("gy", ("gx", "comp"))
    ice = P(("gy", "comp"), "gx")
    in_specs = (ocean, ocean, ocean, flat, P(), P(), P(), P(("gx", "comp")), ice, ice, ice, ice, ice)
    out_specs = (ocean, ocean, ocean, ice, ice)

    def body(tracer, ocean_u, ocean_v, ocean_mask, diffusivity, viscosity, remap, fold_partner, *ice_fields):
        f32 = jnp.float32
        anywhere = pl.BlockSpec(memory_space=pl.ANY)
        main_memory = pl.BlockSpec(memory_space=pltpu.HBM)
        vmem = pltpu.VMEM
        dma = pltpu.SemaphoreType.DMA
        ocean_shape = jax.ShapeDtypeStruct(tracer.shape, f32)
        ice_shape = jax.ShapeDtypeStruct(ice_fields[0].shape, f32)

        def step(*args):
            kernel(blocks, gys, *args)

        shapes = (ocean_shape, ocean_shape, ocean_shape, ice_shape, ice_shape)
        results = pl.pallas_call(
            step,
            out_shape=(*shapes[:3], jax.ShapeDtypeStruct((2, *ice_fields[0].shape), f32)),
            in_specs=[main_memory] * 13,
            out_specs=(anywhere,) * 4,
            scratch_shapes=[
                vmem((PLANES, 96, COLS), f32),
                vmem((3 * LEV, ROWS, COLS), jnp.bfloat16),
                vmem((3 * LEV, ROWS, COLS), jnp.bfloat16),
                vmem((LEV * LEV, 3 * LEV * LEV), jnp.bfloat16),
                vmem((3 * LEV, ROWS, COLS), f32),
                vmem((NF, 112, 2 * COLS), f32),
                vmem((2, 112, 2 * COLS), f32),
                vmem((NF, 40, 2 * COLS), f32),
                vmem((2, 40, 2 * COLS), f32),
                vmem((NS, 8, 2 * BLOCKS * COLS), f32),
                vmem((2, 8, BLOCKS * COLS), f32),
                vmem((NS, 8, COLS), f32),
                vmem((4, 8, 2 * BLOCKS * COLS), f32),
                vmem((4, 8, COLS), f32),
                vmem((2, 8, COLS), f32),
                vmem((2, 8, COLS), f32),
                vmem((HALF, COLS), f32),
                vmem((HALF, COLS), f32),
                vmem((HALF, COLS), f32),
                vmem((HALF, COLS), f32),
                vmem((8, COLS), f32),
                vmem((8, COLS), f32),
                vmem((8, COLS), f32),
                vmem((8, COLS), f32),
                vmem((3 * LEV, COLS), f32),
                vmem((3 * LEV, COLS), f32),
                vmem((3 * LEV, COLS), f32),
                vmem((3 * LEV, COLS), f32),
                *[vmem((8, COLS), f32)] * 8,
                vmem((HALF, COLS), f32),
                vmem((HALF, COLS), f32),
                vmem((HALF, COLS), f32),
                vmem((HALF, COLS), f32),
                vmem((ROWS, COLS), f32),
                vmem((5, ROWS, COLS), f32),
                vmem((ROWS, COLS), jnp.int32),
                vmem((ROWS, COLS), jnp.int32),
                vmem((8, COLS), jnp.int32),
                pltpu.SMEM((LEV,), f32),
                pltpu.SMEM((LEV,), f32),
                pltpu.SMEM((LEV, LEV), f32),
                vmem((LEV, LEV), f32),
                vmem((1, COLS), jnp.int32),
                dma((9,)),
                dma((5,)),
                dma((5,)),
                dma((5,)),
                dma((5,)),
                dma((5,)),
                dma((5,)),
                dma((5,)),
                dma((8,)),
                dma((8,)),
                dma((BLOCKS,)),
                dma((BLOCKS,)),
                dma((BLOCKS,)),
                dma((BLOCKS,)),
                dma((5,)),
                dma((2,)),
                dma((2,)),
            ],
            compiler_params=pltpu.CompilerParams(
                collective_id=0, has_side_effects=True, vmem_limit_bytes=32 * 1024 * 1024
            ),
        )(
            *[
                pltpu.with_memory_space_constraint(value, pltpu.HBM)
                for value in (
                    tracer,
                    ocean_u,
                    ocean_v,
                    ocean_mask,
                    diffusivity,
                    viscosity,
                    remap,
                    fold_partner.reshape(1, COLS),
                    *ice_fields,
                )
            ]
        )
        return pl.pallas_call(
            deliver,
            out_shape=shapes,
            in_specs=[anywhere] * 4,
            out_specs=(main_memory,) * 5,
            scratch_shapes=[dma((5,))],
            compiler_params=pltpu.CompilerParams(vmem_limit_bytes=1024 * 1024),
        )(*results)

    return jax.shard_map(body, mesh=mesh, in_specs=in_specs, out_specs=out_specs, check_vma=False)
```
